128 devices in a mesh: req: 16 (over x, z), tp: 8 (over y, core).
Axes of the slice: x: 4, y: 4, z: 4, core: 2. Of those that a mesh axis runs over, the one named last changes fastest.
Arguments:
- tokens: int32 [4, 384], replicated, may hold values from 0 to 32767
- finish: int32 [4, 384], replicated, may hold values from 0 to 1, as said below
- holder: int32 [4, 384], replicated, may hold values from 0 to 15, as said below
- slot_index: int32 [4, 384], replicated, may hold values from 0 to 63, as said below
- embedding: bfloat16 [32768, 8192], P('tp', 'req'), may hold values from -12 to 12, as said below
- norm_gain: float32 [8192], P('req'), may hold values from 0.5 to 1.5
- proj_inner: bfloat16 [8192, 16384], P('req', 'tp'), may hold values from -0.0625 to 0.0625
- proj_gate: bfloat16 [8192, 16384], P('req', 'tp'), may hold values from -0.0625 to 0.0625
- conv_weight: float32 [4, 16384], P(None, 'tp'), may hold values from -2.5 to 2.5
- conv_bias: float32 [16384], P('tp'), may hold values from -2.5 to 2.5
- proj_low: bfloat16 [16384, 512], P('tp'), may hold values from -0.046875 to 0.046875
- proj_select: bfloat16 [32, 16384], P(None, 'tp'), may hold values from -0.046875 to 0.046875
- proj_dt: bfloat16 [512, 16384], P(None, 'tp'), may hold values from -0.25 to 0.25
- dt_bias: float32 [16384], P('tp'), may hold values from -5 to -1.5
- decay_log: float32 [16, 16384], P(None, 'tp'), may hold values from 0 to 2.77
- skip_gain: float32 [16384], P('tp'), may hold values from 0.5 to 1.5
- proj_out: bfloat16 [16384, 8192], P('tp', 'req'), may hold values from -0.046875 to 0.046875
- state_codes: bfloat16 [384, 16, 16384], P('req', None, 'tp'), may hold values from -1 to 1
- state_scales: bfloat16 [384, 128], P('req', 'tp'), may hold values from 0.099609375 to 1
- conv_state: bfloat16 [384, 3, 16384], P('req', None, 'tp'), may hold values from -6 to 6
Outputs:
- mixed: bfloat16 [4, 384, 8192], P(None, None, 'req')
- next_codes: bfloat16 [384, 16, 16384], P('req', None, 'tp')
- next_scales: bfloat16 [384, 128], P('req', 'tp')
- next_window: bfloat16 [384, 3, 16384], P('req', None, 'tp')
- cache_codes: bfloat16 [1024, 16, 16384], P('req', None, 'tp')
- cache_scales: bfloat16 [1024, 128], P('req', 'tp')
- cache_window: bfloat16 [1024, 3, 16384], P('req', None, 'tp')
The draws below stay inside these ranges and needn't reach their ends.
Inputs may be any that keep to these rules, and one draw needn't show every extreme that they name: `finish`: 1 where the turn ends; in every step, among the rows of one device (aligned blocks of 24 requests), at most 2 finishing requests name the same holder, and this bound is reached. Where finish is 1, the holder of the saved state. Each holder receives at most 64 saves over all steps, and some holder receives exactly 64; other holders may receive far fewer. Where finish is 0 the entry is arbitrary. Where finish is 1, each pair of holder and slot_index occurs at most once over all steps and requests; where finish is 0 the entry is arbitrary. `embedding`: token vectors.
All inputs are finite; a program needn't handle non-finite values.
Results may differ from the reference program's by a relative error of at most 0.035.
Values may be sent and summed in bfloat16 or wider, within the bound.
A program may use at most 128 MiB of HBM per device.

```python
import math
import jax
import jax.numpy as jnp
import numpy as np
from jax import lax

D = 8192
INNER = 16384
STATE = 16
CONV = 4
DT_RANK = 512
VOCAB = 32768
PAGE = 128
STEPS = 4
CAP = 2
R_DEV = 24
REQS = 384
SLOTS = 64
CACHE = 1024
N_REQ = 16


def page_plan(key):
    keys = jax.random.split(key, 7)
    holders = REQS // R_DEV
    hot = jax.random.randint(keys[0], (), 0, holders)
    relabel = jax.random.permutation(keys[1], holders)
    picks = jax.random.randint(keys[2], (3, STEPS, REQS), 0, holders)
    holder_raw = relabel[jnp.min(picks, axis=0)]
    finish_raw = jax.random.randint(keys[3], (STEPS, REQS), 0, 4) != 0
    within = jnp.arange(REQS, dtype=jnp.int32) % R_DEV
    scores = jax.random.randint(keys[4], (STEPS, REQS), 0, 1 << 20) * R_DEV + within[None, :]
    score_blocks = scores.reshape(STEPS, holders, R_DEV)
    below = jnp.sum((score_blocks[:, :, None, :] < score_blocks[:, :, :, None]).astype(jnp.int32), axis=3)
    forced = below.reshape(STEPS, REQS) < CAP
    holder_all = jnp.where(forced, hot, holder_raw)
    finish_all = finish_raw | forced
    priority = (1 - forced.astype(jnp.int32)) * R_DEV + within[None, :]
    prio_blocks = priority.reshape(STEPS, holders, R_DEV)
    hold_blocks = holder_all.reshape(STEPS, holders, R_DEV)
    fin_blocks = finish_all.reshape(STEPS, holders, R_DEV)
    ahead = (prio_blocks[:, :, None, :] < prio_blocks[:, :, :, None]) & (hold_blocks[:, :, None, :] == hold_blocks[:, :, :, None]) & fin_blocks[:, :, None, :]
    ranks = jnp.sum(ahead.astype(jnp.int32), axis=3).reshape(STEPS, REQS)
    finish_cap = finish_all & (ranks < CAP)
    onehot = ((holder_all.reshape(-1)[:, None] == jnp.arange(holders)[None, :]) & finish_cap.reshape(-1)[:, None]).astype(jnp.int32)
    earlier_count = jnp.cumsum(onehot, axis=0) - onehot
    order = jnp.sum(earlier_count * onehot, axis=1).reshape(STEPS, REQS)
    finish_final = finish_cap & (order < SLOTS)
    filler_holder = jax.random.randint(keys[5], (STEPS, REQS), 0, holders)
    filler_slot = jax.random.randint(keys[6], (STEPS, REQS), 0, SLOTS)
    holder_out = jnp.where(finish_final, holder_all, filler_holder).astype(jnp.int32)
    slot_out = jnp.where(finish_final, order, filler_slot).astype(jnp.int32)
    return (finish_final.astype(jnp.int32), holder_out, slot_out)


def draw_finish(key, part):
    return page_plan(key)[0]


def draw_holder(key, part):
    return page_plan(key)[1]


def draw_slot_index(key, part):
    return page_plan(key)[2]


def draw_embedding(key, part):
    key = jax.random.fold_in(key, 7)
    keys = jax.random.split(key, 3)
    position = jnp.arange(D, dtype=jnp.float32) / D
    column = jnp.exp(jax.random.uniform(keys[1], (D,), jnp.float32, 0.0, math.log(10.0)))
    row = jnp.exp(jax.random.uniform(keys[2], (VOCAB, 1), jnp.float32, math.log(0.3), math.log(3.0)))
    base = jnp.clip(jax.random.normal(keys[0], (VOCAB, D), jnp.float32), -4.0, 4.0)
    trend = jnp.exp(0.5 * math.log(3.0) * position)
    return (base * row * (column * trend)[None, :] / 30.0).astype(jnp.bfloat16)


def plant(values, stream_key, least, top_value):
    dims = values.shape
    spot = [jax.random.randint(jax.random.fold_in(stream_key, axis), (), 0, dims[axis]) for axis in range(len(dims))]
    values = values.at[tuple(spot)].set(least)
    longest = dims.index(max(dims))
    spot[longest] = (spot[longest] + 1) % dims[longest]
    return values.at[tuple(spot)].set(top_value)


def shard_levels(rng, dims, cuts, least, top_value):
    loudness = 1.0
    for axis_at, blocks in cuts:
        draws = jax.random.uniform(jax.random.fold_in(jax.random.fold_in(rng, 6), axis_at), (blocks,), jnp.float32, least / len(cuts), top_value / len(cuts))
        loudness = loudness * jnp.repeat(jnp.exp(draws), dims[axis_at] // blocks).reshape((-1,) + (1,) * (len(dims) - 1 - axis_at))
    return loudness


def rank_bounds(count, slope):
    loads = [(1 << 20) // math.isqrt(standing ** slope) + 1 for standing in range(1, count + 1)]
    scale = 1 + sum(loads) // (1 << 30)
    return np.cumsum(np.array([max(1, weight // scale) for weight in loads]))


def ranked(rng, shape, amount, skew):
    table = rank_bounds(amount, skew)
    lot = jax.random.randint(jax.random.fold_in(rng, 1), shape, 0, int(table[amount - 1]))
    standing = jnp.searchsorted(jnp.asarray(table, jnp.int32), lot, side="right")
    return jax.random.permutation(jax.random.fold_in(rng, 2), amount)[standing].astype(jnp.int32)


def gaussian(key, dims, spread, reach, cuts=(), kind=jnp.bfloat16):
    entries = jax.random.normal(key, dims, jnp.float32) * spread
    if len(cuts) > 0:
        entries = shard_levels(key, dims, cuts, -0.22, 0.18) * entries
    return jnp.clip(entries, min=-reach, max=reach).astype(kind)


def setup_inputs(seed: int = 0) -> dict:
    key_of = jax.random.split(jax.random.key(seed), 21)
    return {
        "tokens": plant(ranked(key_of[0], (STEPS, REQS), VOCAB, 2), jax.random.fold_in(key_of[0], 3), 0, VOCAB - 1).astype(jnp.int32),
        "finish": draw_finish(jax.random.fold_in(key_of[20], 71), 0),
        "holder": draw_holder(jax.random.fold_in(key_of[20], 71), 0),
        "slot_index": draw_slot_index(jax.random.fold_in(key_of[20], 71), 0),
        "embedding": draw_embedding(jax.random.fold_in(key_of[20], 71), 0),
        "norm_gain": jnp.clip(0.5 + 1.0 * jax.random.uniform(key_of[5], (D,), jnp.float32) ** shard_levels(key_of[5], (D,), ((0, 16),), -0.2, 0.2), 0.5, 1.5),
        "proj_inner": gaussian(key_of[6], (D, INNER), D ** -0.5, 0.0625, ((0, 16), (1, 8))),
        "proj_gate": gaussian(key_of[7], (D, INNER), D ** -0.5, 0.0625, ((0, 16), (1, 8))),
        "conv_weight": gaussian(key_of[8], (CONV, INNER), 0.5, 2.5, ((1, 8),), jnp.float32),
        "conv_bias": gaussian(key_of[9], (INNER,), 0.5, 2.5, ((0, 8),), jnp.float32),
        "proj_low": gaussian(key_of[10], (INNER, DT_RANK), INNER ** -0.5, 0.046875, ((0, 8),)),
        "proj_select": gaussian(key_of[11], (2 * STATE, INNER), INNER ** -0.5, 0.046875, ((1, 8),)),
        "proj_dt": gaussian(key_of[12], (DT_RANK, INNER), DT_RANK ** -0.5, 0.25, ((1, 8),)),
        "dt_bias": jnp.clip(-5.0 + 3.5 * jax.random.uniform(key_of[13], (INNER,), jnp.float32) ** shard_levels(key_of[13], (INNER,), ((0, 8),), -0.2, 0.2), -5.0, -1.5),
        "decay_log": jnp.clip(2.77 * jax.random.uniform(key_of[14], (STATE, INNER), jnp.float32) ** shard_levels(key_of[14], (STATE, INNER), ((1, 8),), -0.2, 0.2), 0.0, 2.77),
        "skip_gain": jnp.clip(0.5 + 1.0 * jax.random.uniform(key_of[15], (INNER,), jnp.float32) ** shard_levels(key_of[15], (INNER,), ((0, 8),), -0.2, 0.2), 0.5, 1.5),
        "proj_out": gaussian(key_of[16], (INNER, D), INNER ** -0.5, 0.046875, ((0, 8), (1, 16))),
        "state_codes": jnp.clip(jax.random.uniform(key_of[17], (REQS, STATE, INNER), jnp.float32, -1.0, 1.0) * shard_levels(key_of[17], (REQS, STATE, INNER), ((0, 16), (2, 8)), -0.4, 0.0), -1.0, 1.0).astype(jnp.bfloat16),
        "state_scales": jnp.clip(jnp.exp(math.log(1.0) - 2.306499 * jax.random.uniform(key_of[18], (REQS, INNER // PAGE), jnp.float32) ** shard_levels(key_of[18], (REQS, INNER // PAGE), ((0, 16), (1, 8)), -0.2, 0.2)), 0.099609375, 1.0).astype(jnp.bfloat16),
        "conv_state": gaussian(key_of[19], (REQS, CONV - 1, INNER), 1.0, 6.0, ((0, 16), (2, 8))),
    }


def page_expand(page_values):
    return jnp.repeat(page_values.astype(jnp.float32), PAGE, axis=-1)

def state_update(codes, scales, step_size, activ, b_in, c_out, gate_sum, decay_rate, skip_gain):
    activ_f = activ.astype(jnp.float32)
    previous = codes.astype(jnp.float32) * page_expand(scales)[:, None, :]
    decay = jnp.exp(step_size[:, None, :] * decay_rate[None, :, :])
    current = decay * previous + (step_size * activ_f)[:, None, :] * b_in[:, :, None]
    output = lax.optimization_barrier(jnp.sum(current * c_out[:, :, None], axis=1)) + skip_gain[None, :] * activ_f
    gated = (output * jax.nn.silu(gate_sum)).astype(jnp.bfloat16)
    paged = current.reshape(current.shape[0], current.shape[1], -1, PAGE)
    peak = lax.optimization_barrier(jnp.max(jnp.abs(paged), axis=(1, 3)))
    new_scales = (peak + 1e-06).astype(jnp.bfloat16)
    new_codes = (current / page_expand(new_scales)[:, None, :]).astype(jnp.bfloat16)
    return (gated, new_codes, new_scales)

def blocked_product(normed, weight):
    slab_width = normed.shape[1] // N_REQ
    running_sum = jnp.zeros((normed.shape[0], weight.shape[1]), jnp.float32)
    for block_index in range(N_REQ):
        lower = block_index * slab_width
        partial_term = jnp.dot(normed[:, lower:lower + slab_width], weight[lower:lower + slab_width], preferred_element_type=jnp.float32)
        rounded = lax.optimization_barrier(partial_term.astype(jnp.bfloat16))
        running_sum = running_sum + rounded.astype(jnp.float32)
    return running_sum

def reference(tokens, finish, holder, slot_index, embedding, norm_gain, proj_inner, proj_gate, conv_weight, conv_bias, proj_low, proj_select, proj_dt, dt_bias, decay_log, skip_gain, proj_out, state_codes, state_scales, conv_state):
    embedded = embedding[tokens].astype(jnp.float32)
    inv_rms = lax.rsqrt(lax.optimization_barrier(jnp.mean(embedded * embedded, axis=2)) + 1e-05)
    decay_rate = -jnp.exp(decay_log)
    codes, scales, window = (state_codes, state_scales, conv_state)
    cache_codes = jnp.zeros((CACHE, STATE, INNER), jnp.bfloat16)
    cache_scales = jnp.zeros((CACHE, INNER // PAGE), jnp.bfloat16)
    cache_window = jnp.zeros((CACHE, CONV - 1, INNER), jnp.bfloat16)

    def per_block(pieces):
        return state_update(*pieces, decay_rate, skip_gain)
    mixed_steps = []
    for step_index in range(STEPS):
        normed = (embedded[step_index] * inv_rms[step_index][:, None] * norm_gain[None, :]).astype(jnp.bfloat16)
        inner_sum = blocked_product(normed, proj_inner)
        gate_sum = blocked_product(normed, proj_gate)
        full_window = jnp.concatenate([window, inner_sum.astype(jnp.bfloat16)[:, None, :]], axis=1)
        conv_out = lax.optimization_barrier(jnp.sum(full_window.astype(jnp.float32) * conv_weight[None], axis=1)) + conv_bias[None, :]
        activ = jax.nn.silu(conv_out).astype(jnp.bfloat16)
        low_rank = jnp.dot(activ, proj_low, preferred_element_type=jnp.float32)
        selectors = lax.dot_general(activ, proj_select, (((1,), (1,)), ((), ())), preferred_element_type=jnp.float32)
        step_size = jax.nn.softplus(jnp.dot(low_rank.astype(jnp.bfloat16), proj_dt, preferred_element_type=jnp.float32) + dt_bias[None, :])
        members = (codes, scales, step_size, activ, selectors[:, :STATE], selectors[:, STATE:], gate_sum)
        shaped = tuple((member.reshape((N_REQ, R_DEV) + member.shape[1:]) for member in members))
        gated, codes, scales = lax.map(per_block, shaped)
        gated = gated.reshape(REQS, INNER)
        codes = codes.reshape(REQS, STATE, INNER)
        scales = scales.reshape(REQS, INNER // PAGE)
        window = full_window[:, 1:]
        mixed_steps.append(jnp.dot(gated, proj_out, preferred_element_type=jnp.float32).astype(jnp.bfloat16))
        target = jnp.where(finish[step_index] == 1, holder[step_index] * SLOTS + slot_index[step_index], CACHE).astype(jnp.int32)
        cache_codes = cache_codes.at[target].set(codes, mode='drop')
        cache_scales = cache_scales.at[target].set(scales, mode='drop')
        cache_window = cache_window.at[target].set(window, mode='drop')
    return (jnp.stack(mixed_steps), codes, scales, window, cache_codes, cache_scales, cache_window)
```

```python
import functools

import jax
import jax.numpy as jnp
from jax import lax
from jax.experimental import pallas as pl
from jax.experimental.pallas import tpu as pltpu
from jax.sharding import PartitionSpec as P

D = 8192
STATE = 16
PAGE = 128
STEPS = 4
CAP = 2
ROWS = 24
BLOCKS = 16
BROWS = STEPS * ROWS
SLOTS = 64
INNER = 2048
FEATS = 512
WIDE = 512
RANK = 512
PAIRS = STEPS * CAP
F32 = jnp.float32
BF16 = jnp.bfloat16
MESH = pl.DeviceIdType.MESH
VMEM_LIMIT = 60 * 1024 * 1024


def rcopy(src, dst, send, recv, dev):
    return pltpu.make_async_remote_copy(
        src_ref=src, dst_ref=dst, send_sem=send, recv_sem=recv, device_id=dev, device_id_type=MESH
    )


def mod4(v):
    return lax.rem(v + 8, 4)


def dot(a, b):
    return jnp.dot(a, b, preferred_element_type=F32)


def greet(devices):
    barrier = pltpu.get_barrier_semaphore()
    for dev in devices:
        pl.semaphore_signal(barrier, inc=1, device_id=dev, device_id_type=MESH)
    pl.semaphore_wait(barrier, len(devices))


TP_SCRATCH = [
    pltpu.VMEM((4, 2, BROWS, FEATS), BF16),
    pltpu.VMEM((4, 2, BROWS, FEATS), BF16),
    pltpu.VMEM((4, 2, BROWS, FEATS), F32),
    pltpu.VMEM((2, BROWS, FEATS), BF16),
    pltpu.VMEM((2, BROWS, FEATS), BF16),
    pltpu.VMEM((2, BROWS, FEATS), BF16),
    pltpu.VMEM((2, BROWS, FEATS), BF16),
    pltpu.VMEM((2, BROWS, FEATS), BF16),
    pltpu.VMEM((2, BROWS, FEATS), BF16),
    pltpu.SemaphoreType.DMA((20,)),
    pltpu.SemaphoreType.DMA((20,)),
]


def tp_partners():
    r, t = lax.axis_index("req"), lax.axis_index("tp")
    y, c = lax.div(t, 2), lax.rem(t, 2)
    return [(r, y * 2 + 1 - c), (r, mod4(y + 1) * 2 + c), (r, mod4(y - 1) * 2 + c)]


def tp_sum(get, total, bufs):
    half_s, half_r, part, far_s, far_r, dir_s, dir_r, com_s, com_r, ss, rs = bufs
    t = lax.axis_index("tp")
    y, c = lax.div(t, 2), lax.rem(t, 2)
    core, up, down = tp_partners()
    order = [mod4(y + 2), mod4(y + 1), mod4(y - 1), y]
    sent = []

    def send(src, dst, n, dev):
        copy = rcopy(src, dst, ss.at[n], rs.at[n], dev)
        copy.start()
        sent.append(copy)

    def arrived(ref, n):
        rcopy(ref, ref, ss.at[n], rs.at[n], core).wait_recv()

    def pair(group, yy):
        return pl.ds(2 * (group * 4 + yy), 2)

    for k in range(4):
        half_s[k] = get((1 - c) * 4 + order[k]).astype(BF16)
        send(half_s.at[k], half_r.at[k], k, core)
    for k in range(4):
        mine = get(c * 4 + order[k])
        arrived(half_r.at[k], k)
        part[k] = mine + half_r[k].astype(F32)
        if k == 0:
            far_s[...] = part[0].astype(BF16)
            send(far_s.at[0], far_r.at[0], 4, up)
            send(far_s.at[1], far_r.at[1], 5, down)
        if k == 1:
            dir_s[1] = part[1, 1].astype(BF16)
            send(dir_s.at[1], dir_r.at[1], 7, up)
        if k == 2:
            dir_s[0] = part[2, 0].astype(BF16)
            send(dir_s.at[0], dir_r.at[0], 6, down)
    arrived(far_r.at[0], 4)
    com_s[0] = (part[1, 0] + far_r[0].astype(F32)).astype(BF16)
    send(com_s.at[0], com_r.at[0], 8, up)
    arrived(far_r.at[1], 5)
    com_s[1] = (part[2, 1] + far_r[1].astype(F32)).astype(BF16)
    send(com_s.at[1], com_r.at[1], 9, down)
    own = 2 * (c * 4 + y)
    for h in range(2):
        arrived(dir_r.at[h], 6 + h)
        arrived(com_r.at[h], 8 + h)
        total[own + h] = (part[3, h] + dir_r[h].astype(F32) + com_r[h].astype(F32)).astype(BF16)
    mine = total.at[pair(c, y)]
    send(mine, mine, 10, up)
    send(mine, mine, 11, down)
    send(mine, mine, 12, core)
    below = total.at[pair(c, mod4(y - 1))]
    above = total.at[pair(c, mod4(y + 1))]
    arrived(below, 10)
    first = total.at[2 * (c * 4 + mod4(y - 1))]
    send(first, first, 13, up)
    send(below, below, 15, core)
    arrived(above, 11)
    second = total.at[2 * (c * 4 + mod4(y + 1)) + 1]
    send(second, second, 14, down)
    send(above, above, 16, core)
    far = 2 * (c * 4 + mod4(y + 2))
    arrived(total.at[far], 13)
    send(total.at[far], total.at[far], 17, core)
    arrived(total.at[far + 1], 14)
    send(total.at[far + 1], total.at[far + 1], 18, core)
    arrived(total.at[pair(1 - c, y)], 12)
    arrived(total.at[pair(1 - c, mod4(y - 1))], 15)
    arrived(total.at[pair(1 - c, mod4(y + 1))], 16)
    other = 2 * ((1 - c) * 4 + mod4(y + 2))
    arrived(total.at[other], 17)
    arrived(total.at[other + 1], 18)
    for copy in sent:
        copy.wait_send()


def shift_req(axis, d):
    r, t = lax.axis_index("req"), lax.axis_index("tp")
    x, z = lax.div(r, 4), lax.rem(r, 4)
    if axis == 0:
        return (mod4(x + d) * 4 + z, t)
    return (x * 4 + mod4(z + d), t)


def req_place(axis):
    r = lax.axis_index("req")
    return lax.div(r, 4) if axis == 0 else lax.rem(r, 4)


def req_partners():
    return [shift_req(axis, d) for axis in (0, 1) for d in (1, -1)]


FRONT_SCRATCH = (
    [
        pltpu.VMEM((BLOCKS, BROWS, FEATS), BF16),
        pltpu.VMEM((4, 4 * BROWS, FEATS), BF16),
        pltpu.VMEM((4, 4 * BROWS, FEATS), BF16),
        pltpu.VMEM((4, 4 * BROWS, PAGE), F32),
    ]
    + [pltpu.VMEM((2, 4, 4 * BROWS, WIDE), BF16)] * 6
    + [pltpu.VMEM((2, 4, BROWS, WIDE), BF16)] * 6
    + [pltpu.VMEM((2, 4, 4, BROWS, WIDE), F32)]
    + [pltpu.SemaphoreType.DMA((6, 2, 4)), pltpu.SemaphoreType.DMA((6, 2, 4))]
    + [pltpu.VMEM((4 * BROWS, PAGE), BF16)] * 6
    + [pltpu.VMEM((BROWS, PAGE), BF16)] * 6
    + [pltpu.VMEM((4, BROWS, PAGE), F32)]
    + [pltpu.SemaphoreType.DMA((6,)), pltpu.SemaphoreType.DMA((6,))]
)


class ScatterSum:
    def __init__(self, axis, d, partial, bufs, total, ss, rs):
        self.axes = (axis, 1 - axis)
        self.d = d
        self.partial = partial
        self.far_s, self.far_r, self.dir_s, self.dir_r, self.com_s, self.com_r = bufs[:6]
        self.far2_s, self.far2_r, self.dir2_s, self.dir2_r, self.com2_s, self.com2_r = bufs[6:]
        self.total = total
        self.ss, self.rs = ss, rs

    def copy(self, n):
        src = (self.far_s, self.dir_s, self.com_s, self.far2_s, self.dir2_s, self.com2_s)[n]
        dst = (self.far_r, self.dir_r, self.com_r, self.far2_r, self.dir2_r, self.com2_r)[n]
        d = -self.d if n % 3 == 1 else self.d
        return rcopy(src, dst, self.ss(n), self.rs(n), shift_req(self.axes[n // 3], d))

    def far(self):
        p = req_place(self.axes[0])
        self.far_s[...] = self.partial(mod4(p + 2)).astype(BF16)
        self.copy(0).start()

    def direct(self):
        p = req_place(self.axes[0])
        self.dir_s[...] = self.partial(mod4(p - self.d)).astype(BF16)
        self.copy(1).start()

    def combined(self):
        p = req_place(self.axes[0])
        mine = self.partial(mod4(p + self.d))
        self.copy(0).wait_recv()
        self.com_s[...] = (mine + self.far_r[...].astype(F32)).astype(BF16)
        self.copy(2).start()

    def own(self):
        p, q = req_place(self.axes[0]), req_place(self.axes[1])
        mine = self.partial(p)
        self.copy(1).wait_recv()
        self.copy(2).wait_recv()
        mine = mine + self.dir_r[...].astype(F32) + self.com_r[...].astype(F32)
        self.total[...] = mine.reshape(4, BROWS, mine.shape[1])
        self.far2_s[...] = self.total[mod4(q + 2)].astype(BF16)
        self.copy(3).start()
        self.dir2_s[...] = self.total[mod4(q - self.d)].astype(BF16)
        self.copy(4).start()

    def combined2(self):
        q = req_place(self.axes[1])
        self.copy(3).wait_recv()
        self.com2_s[...] = (self.total[mod4(q + self.d)] + self.far2_r[...].astype(F32)).astype(
            BF16
        )
        self.copy(5).start()

    def result(self):
        q = req_place(self.axes[1])
        self.copy(4).wait_recv()
        self.copy(5).wait_recv()
        return self.total[q] + self.dir2_r[...].astype(F32) + self.com2_r[...].astype(F32)

    def drain(self):
        for n in range(6):
            self.copy(n).wait_send()


def front_kernel(ids, emb, gain, w_inner, w_gate, out, *scratch):
    tp_bufs, rest = scratch[: len(TP_SCRATCH)], scratch[len(TP_SCRATCH) :]
    embedded, lhs_x, lhs_z, squares = rest[:4]
    big = rest[4:17]
    big_ss, big_rs = rest[17:19]
    small = rest[19:32]
    small_ss, small_rs = rest[32:34]
    greet(tp_partners() + req_partners())

    def looked(ch):
        want = ids[pl.ds(2 * ch, 2)].reshape(2 * BROWS, 1)
        span = 1024
        acc = jnp.zeros((2 * BROWS, FEATS), F32)
        for k in range(emb.shape[0] // span):
            lane = lax.broadcasted_iota(jnp.int32, (2 * BROWS, span), 1) + k * span
            hot = jnp.where(lane == want, 1.0, 0.0).astype(BF16)
            acc = acc + dot(hot, emb[k * span : (k + 1) * span, :])
        return acc.reshape(2, BROWS, FEATS)

    tp_sum(looked, embedded, tp_bufs)

    def spread(b, carry):
        x, z = lax.div(b, 4), lax.rem(b, 4)
        rows = embedded[b].astype(F32)
        scaled = (rows * gain[...]).astype(BF16)
        lhs_x[x, pl.ds(pl.multiple_of(z * BROWS, BROWS), BROWS), :] = scaled
        lhs_z[z, pl.ds(pl.multiple_of(x * BROWS, BROWS), BROWS), :] = scaled
        squares[x, pl.ds(pl.multiple_of(z * BROWS, BROWS), BROWS), :] = jnp.broadcast_to(
            jnp.sum(rows * rows, axis=1, keepdims=True), (BROWS, PAGE)
        )
        return carry

    lax.fori_loop(0, BLOCKS, spread, 0)

    def unit(ab, u):
        lhs, weight = ((lhs_x, w_inner), (lhs_z, w_gate))[ab]

        def partial(chunk):
            cols = pl.ds(pl.multiple_of(u * WIDE, WIDE), WIDE)
            return dot(lhs[chunk], weight[:, cols])

        views = [ref.at[ab, u] for ref in big[:12]]
        return ScatterSum(
            ab,
            1 - 2 * lax.rem(u, 2),
            partial,
            views,
            big[12].at[ab, u],
            lambda n: big_ss.at[n, ab, u],
            lambda n: big_rs.at[n, ab, u],
        )

    norm = ScatterSum(
        0, 1, lambda chunk: squares[chunk], small[:12], small[12],
        lambda n: small_ss.at[n], lambda n: small_rs.at[n],
    )

    def each(step):
        def body(u, carry):
            for ab in range(2):
                step(ab, u, unit(ab, u))
            return carry

        lax.fori_loop(0, 4, body, 0)

    norm.far()
    each(lambda ab, u, s: s.far())
    norm.direct()
    each(lambda ab, u, s: s.direct())
    norm.combined()
    each(lambda ab, u, s: s.combined())
    norm.own()
    each(lambda ab, u, s: s.own())
    norm.combined2()
    each(lambda ab, u, s: s.combined2())
    inv_rms = lax.rsqrt(norm.result()[:, :1] / D + 1e-05)

    def finish(ab, u, s):
        cols = pl.ds(pl.multiple_of((ab * 4 + u) * WIDE, WIDE), WIDE)
        out[:, cols] = s.result() * inv_rms

    each(finish)
    norm.drain()
    each(lambda ab, u, s: s.drain())


def vmem_call(kernel, out_shape, n_in, scratch, **params):
    spec = pl.BlockSpec(memory_space=pltpu.VMEM)
    return pl.pallas_call(
        kernel,
        out_shape=out_shape,
        in_specs=[spec] * n_in,
        out_specs=jax.tree.map(lambda _: spec, out_shape),
        scratch_shapes=scratch,
        compiler_params=pltpu.CompilerParams(vmem_limit_bytes=VMEM_LIMIT, **params),
    )


def silu(v):
    return v / (1.0 + jnp.exp(-v))


RCOLS = RANK + 128


def rank_kernel(
    sums, conv, taps, bias, w_low, w_select, w_dt, dt_bias, step, activ, select,
    pair_s, pair_r, quad_s, quad_r, full, ss, rs,
):
    r, t = lax.axis_index("req"), lax.axis_index("tp")
    y, c = lax.div(t, 2), lax.rem(t, 2)
    core = (r, y * 2 + 1 - c)
    others = [(r, mod4(y + d) * 2 + c) for d in (1, 2, 3)]
    greet([core] + others)
    for n in range(STEPS):
        total = bias[...] + jnp.zeros((ROWS, INNER), F32)
        for k in range(4):
            at = n + k
            if at < 3:
                row = conv[at * ROWS : (at + 1) * ROWS, :]
            else:
                row = sums[(at - 3) * ROWS : (at - 2) * ROWS, :INNER].astype(BF16).astype(F32)
            total = total + row * taps[k : k + 1, :]
        activ[n * ROWS : (n + 1) * ROWS, :] = silu(total).astype(BF16).astype(F32)
    act = activ[...].astype(BF16)
    low = dot(act, w_low[...]).reshape(2, BROWS // 2, RANK)
    sel = lax.dot_general(
        act, w_select[...], (((1,), (1,)), ((), ())), preferred_element_type=F32
    ).reshape(2, BROWS // 2, 128)
    pair_s[:, :, :RANK] = low
    pair_s[:, :, RANK:] = sel
    swap = rcopy(pair_s, pair_r, ss.at[0], rs.at[0], core)
    swap.start()
    swap.wait_recv()
    chip = pair_s[c] + pair_r[c]
    quad_s[...] = chip.astype(BF16)
    copies = [rcopy(quad_s, quad_r.at[n], ss.at[1 + n], rs.at[1 + n], others[n]) for n in range(3)]
    for copy in copies:
        copy.start()
    acc = quad_s[...].astype(F32)
    for n in range(3):
        copies[n].wait_recv()
        acc = acc + quad_r[n].astype(F32)
    full[c] = acc
    back = rcopy(full.at[c], full.at[c], ss.at[4], rs.at[4], core)
    back.start()
    rcopy(full.at[1 - c], full.at[1 - c], ss.at[4], rs.at[4], core).wait_recv()
    low_rank = full[:, :, :RANK].reshape(BROWS, RANK).astype(BF16)
    select[...] = full[:, :, RANK:].reshape(BROWS, 128)
    v = dot(low_rank, w_dt[...]) + dt_bias[...]
    step[...] = jnp.maximum(v, 0.0) + jnp.log1p(jnp.exp(-jnp.abs(v)))
    swap.wait_send()
    for copy in copies:
        copy.wait_send()
    back.wait_send()


def state_kernel(
    index, codes, scales, step, activ, select, sums, conv, decay_log, skip,
    gated, final, packed, source, new_codes, output, scale_rows, rates,
):
    lane = lax.broadcasted_iota(jnp.int32, (STATE, 128), 1)
    row_of = lax.broadcasted_iota(jnp.int32, (STATE, 128), 0)
    page_lane = lax.broadcasted_iota(jnp.int32, (1, 128), 1)
    width = 4 * PAGE

    def request(i, carry):
        b_in, c_out = [], []
        for n in range(STEPS):
            row = select[pl.ds(n * ROWS + i, 1), :]
            b_in.append(jnp.sum(jnp.where(lane == row_of, row, 0.0), axis=1, keepdims=True))
            c_out.append(
                jnp.sum(jnp.where(lane == row_of + STATE, row, 0.0), axis=1, keepdims=True)
            )
        kept = [jnp.zeros((1, 128), F32) for _ in range(STEPS)]
        for part in range(INNER // width):
            cols = slice(part * width, (part + 1) * width)
            rate = rates[:, cols]
            current = codes[i, :, cols].astype(F32) * scales[pl.ds(i, 1), cols]
            for n in range(STEPS):
                at = n * ROWS + i
                dt = step[pl.ds(at, 1), cols]
                act = activ[pl.ds(at, 1), cols]
                current = jnp.exp2(dt * rate) * current + (dt * act) * b_in[n]
                output[pl.ds(at, 1), cols] = jnp.sum(current * c_out[n], axis=0, keepdims=True)
                peak = jnp.max(jnp.abs(current), axis=0, keepdims=True)
                for page in range(4):
                    here = slice(page * PAGE, (page + 1) * PAGE)
                    top = jnp.max(peak[:, here], axis=1, keepdims=True)
                    scale = (top + 1e-06).astype(BF16).astype(F32)
                    kept[n] = jnp.where(page_lane == part * 4 + page, scale, kept[n])
                    new_codes[at, :, part * width + page * PAGE : part * width + (page + 1) * PAGE] = (
                        current[:, here] * (1.0 / scale)
                    ).astype(BF16)
        for n in range(STEPS):
            scale_rows[pl.ds(n * ROWS + i, 1), :] = kept[n]
        final[i] = new_codes[(STEPS - 1) * ROWS + i]
        return carry

    rates[...] = -jnp.exp(decay_log[...]) * 1.4426950408889634
    lax.fori_loop(0, ROWS, request, 0)
    gated[...] = (
        (output[...] + skip[...] * activ[...]) * silu(sums[:, INNER:])
    ).astype(BF16)
    for k in range(3):
        if k < 2:
            source[k * BROWS : (k + 1) * BROWS, :] = jnp.concatenate(
                [conv[(k + 1) * ROWS :, :], sums[: (k + 2) * ROWS, :INNER]], axis=0
            ).astype(BF16)
        else:
            source[k * BROWS : (k + 1) * BROWS, :] = sums[:, :INNER].astype(BF16)
    source[3 * BROWS :, :] = jnp.zeros((BROWS, INNER), BF16)
    source[3 * BROWS :, :128] = scale_rows[...].astype(BF16)

    def pack(n, carry):
        packed[n] = new_codes[index[n]]
        return carry

    lax.fori_loop(0, BLOCKS * PAIRS, pack, 0)


SIDE = 4 * PAIRS

BACK_SCRATCH = [
    pltpu.VMEM((BLOCKS, BROWS, INNER // 2), BF16),
    pltpu.VMEM((BLOCKS, BROWS, INNER // 2), BF16),
    pltpu.VMEM((BLOCKS, BROWS, FEATS), F32),
    pltpu.VMEM((BLOCKS, BROWS, FEATS), F32),
    pltpu.VMEM((BLOCKS, SIDE, INNER), BF16),
    pltpu.SemaphoreType.DMA((2, 16)),
    pltpu.SemaphoreType.DMA((2, 16)),
    pltpu.SemaphoreType.DMA((2, 16)),
    pltpu.SemaphoreType.DMA((2, 16)),
]


class Gather:
    def __init__(self, axis, buf, ss, rs):
        self.axes = (axis, 1 - axis)
        self.buf, self.ss, self.rs = buf, ss, rs
        self.q, self.p = req_place(axis), req_place(1 - axis)
        self.order = [self.q, mod4(self.q - 1), mod4(self.q + 1), mod4(self.q + 2)]
        self.sent = []

    def send(self, ref, n, axis, d):
        copy = rcopy(ref, ref, self.ss.at[n], self.rs.at[n], shift_req(axis, d))
        copy.start()
        self.sent.append(copy)

    def arrived(self, ref, n):
        rcopy(ref, ref, self.ss.at[n], self.rs.at[n], shift_req(self.axes[0], 1)).wait_recv()

    def block(self, p, q):
        return self.buf.at[p * 4 + q]

    def rows(self, p, q, h):
        return self.buf.at[p * 4 + q, pl.ds(h * (BROWS // 2), BROWS // 2)]

    def start(self):
        mine = self.block(self.p, self.q)
        self.send(mine, 0, self.axes[0], 1)
        self.send(mine, 1, self.axes[0], -1)
        self.spread(0)

    def spread(self, k):
        block = self.block(self.p, self.order[k])
        self.send(block, 4 + k, self.axes[1], 1)
        self.send(block, 8 + k, self.axes[1], -1)

    def near(self):
        self.arrived(self.block(self.p, self.order[1]), 0)
        self.send(self.rows(self.p, self.order[1], 0), 2, self.axes[0], 1)
        self.spread(1)
        self.arrived(self.block(self.p, self.order[2]), 1)
        self.send(self.rows(self.p, self.order[2], 1), 3, self.axes[0], -1)
        self.spread(2)

    def last(self):
        self.arrived(self.rows(self.p, self.order[3], 0), 2)
        self.arrived(self.rows(self.p, self.order[3], 1), 3)
        self.spread(3)

    def relay(self, k):
        below, above = mod4(self.p - 1), mod4(self.p + 1)
        self.arrived(self.block(below, self.order[k]), 4 + k)
        if k < 2:
            self.send(self.block(below, self.order[k]), 12 + k, self.axes[1], 1)
        self.arrived(self.block(above, self.order[k]), 8 + k)
        if k >= 2:
            self.send(self.block(above, self.order[k]), 12 + k, self.axes[1], -1)

    def end(self, k):
        self.arrived(self.block(mod4(self.p + 2), self.order[k]), 12 + k)

    def drain(self):
        for copy in self.sent:
            copy.wait_send()


def back_kernel(gated, w_out, want, source, packed, mixed, got_codes, got_side, *scratch):
    tp_bufs, rest = scratch[: len(TP_SCRATCH)], scratch[len(TP_SCRATCH) :]
    buf_a, buf_b, acc_a, acc_b, side, gss, grs, css, crs = rest
    r, t = lax.axis_index("req"), lax.axis_index("tp")
    x, z = lax.div(r, 4), lax.rem(r, 4)
    offsets = [(dx, dz) for dx in range(4) for dz in range(4) if (dx, dz) != (0, 0)]
    peers = [mod4(x + dx) * 4 + mod4(z + dz) for dx, dz in offsets]
    froms = [mod4(x - dx) * 4 + mod4(z - dz) for dx, dz in offsets]
    greet(tp_partners() + [(peer, t) for peer in peers])
    half = INNER // 2
    buf_a[r] = gated[:, :half]
    buf_b[z * 4 + x] = gated[:, half:]
    parts = [
        Gather(1, buf_a, gss.at[0], grs.at[0]),
        Gather(0, buf_b, gss.at[1], grs.at[1]),
    ]
    for part in parts:
        part.start()

    def project(part, p, k):
        buf, acc, rows = ((buf_a, acc_a, slice(0, half)), (buf_b, acc_b, slice(half, INNER)))[part]
        at = p * 4 + parts[part].order[k]
        acc[at] = dot(buf[at], w_out[rows, :])

    for n in range(4):
        rows = slice(n * 128, (n + 1) * 128)
        lane = lax.broadcasted_iota(jnp.int32, (128, 4 * BROWS), 1)
        hot = jnp.where(lane == want[rows, :], 1.0, 0.0).astype(BF16)
        side[4 * n : 4 * (n + 1)] = dot(hot, source[...]).astype(BF16).reshape(4, SIDE, INNER)
    for n in range(2):
        project(n, parts[n].p, 0)
    for part in parts:
        part.near()
    for n in range(2):
        project(n, parts[n].p, 1)
        project(n, parts[n].p, 2)
    for part in parts:
        part.last()
    for n in range(2):
        project(n, parts[n].p, 3)
    for k in range(4):
        for part in parts:
            part.relay(k)
        for n in range(2):
            project(n, mod4(parts[n].p - 1), k)
            project(n, mod4(parts[n].p + 1), k)
    saves = []
    for n, peer in enumerate(peers):
        saves.append(rcopy(packed.at[peer], got_codes.at[r], css.at[0, n], crs.at[0, n], (peer, t)))
        saves.append(rcopy(side.at[peer], got_side.at[r], css.at[1, n], crs.at[1, n], (peer, t)))
    for copy in saves:
        copy.start()
    local = [
        pltpu.make_async_copy(packed.at[r], got_codes.at[r], css.at[0, 15]),
        pltpu.make_async_copy(side.at[r], got_side.at[r], css.at[1, 15]),
    ]
    for copy in local:
        copy.start()
    for k in range(4):
        for n in range(2):
            parts[n].end(k)
            project(n, mod4(parts[n].p + 2), k)

    def summed(ch):
        both = []
        for h in range(2):
            b = 2 * ch + h
            both.append(acc_a[b] + acc_b[lax.rem(b, 4) * 4 + lax.div(b, 4)])
        return jnp.stack(both)

    tp_sum(summed, mixed, tp_bufs)
    for part in parts:
        part.drain()
    for n, src in enumerate(froms):
        rcopy(got_codes.at[src], got_codes.at[src], css.at[0, n], crs.at[0, n], (src, t)).wait_recv()
        rcopy(got_side.at[src], got_side.at[src], css.at[1, n], crs.at[1, n], (src, t)).wait_recv()
    for copy in saves:
        copy.wait_send()
    for copy in local:
        copy.wait()


def place_kernel(where_s, where_v, side, codes, out, win0, win1, win2, scale, zero, sems):
    zero[...] = jnp.zeros_like(zero)

    def begin(s, carry):
        at = where_s[s]

        @pl.when(at >= 0)
        def _():
            pltpu.make_async_copy(codes.at[at], out.at[s], sems.at[s]).start()

        @pl.when(at < 0)
        def _():
            pltpu.make_async_copy(zero, out.at[s], sems.at[s]).start()

        return carry

    lax.fori_loop(0, SLOTS, begin, 0)
    at = where_v[...]
    lane = lax.broadcasted_iota(jnp.int32, (SLOTS, BLOCKS * SIDE), 1)
    first = lax.div(at, PAIRS) * SIDE + lax.rem(at, PAIRS)
    for k, ref in enumerate((win0, win1, win2)):
        hot = jnp.where((lane == first + k * PAIRS) & (at >= 0), 1.0, 0.0).astype(BF16)
        ref[...] = dot(hot, side[...]).astype(BF16)
    hot = jnp.where((lane == first + 3 * PAIRS) & (at >= 0), 1.0, 0.0).astype(BF16)
    scale[...] = dot(hot, side[:, :128]).astype(BF16)

    def end(s, carry):
        pltpu.make_async_copy(zero, out.at[s], sems.at[s]).wait()
        return carry

    lax.fori_loop(0, SLOTS, end, 0)


def save_plan(finish, holder, slot_index, me):
    fin = finish.reshape(STEPS, BLOCKS, ROWS) == 1
    own = holder.reshape(STEPS, BLOCKS, ROWS)
    slot = slot_index.reshape(STEPS, BLOCKS, ROWS)
    earlier = jnp.arange(ROWS)[None, :] < jnp.arange(ROWS)[:, None]
    ahead = earlier & (own[..., None, :] == own[..., :, None]) & fin[..., None, :]
    ranks = jnp.sum(ahead.astype(jnp.int32), axis=3)
    block = lax.broadcasted_iota(jnp.int32, (STEPS, BLOCKS, ROWS), 1)
    step = lax.broadcasted_iota(jnp.int32, (STEPS, BLOCKS, ROWS), 0)
    value = block * PAIRS + step * CAP + ranks + 1
    taken = (fin & (own == me)).reshape(1, -1) & (
        slot.reshape(1, -1) == jnp.arange(SLOTS)[:, None]
    )
    where = jnp.sum(jnp.where(taken, value.reshape(1, -1), 0), axis=1) - 1
    fin_own = lax.dynamic_index_in_dim(fin, me, 1, False)
    own_own = lax.dynamic_index_in_dim(own, me, 1, False)
    rank_own = lax.dynamic_index_in_dim(ranks, me, 1, False)
    row = lax.broadcasted_iota(jnp.int32, (STEPS, ROWS), 0) * ROWS + lax.broadcasted_iota(
        jnp.int32, (STEPS, ROWS), 1
    )
    match = (
        fin_own[None, :, None, :]
        & (own_own[None, :, None, :] == jnp.arange(BLOCKS)[:, None, None, None])
        & (rank_own[None, :, None, :] == jnp.arange(CAP)[None, None, :, None])
    )
    index = jnp.sum(jnp.where(match, row[None, :, None, :] + 1, 0), axis=3).reshape(-1) - 1
    return index, where


def per_device(
    tokens, finish, holder, slot_index, embedding, norm_gain, proj_inner, proj_gate, conv_weight,
    conv_bias, proj_low, proj_select, proj_dt, dt_bias, decay_log, skip_gain, proj_out, state_codes,
    state_scales, conv_state,
):
    me = lax.axis_index("req")
    ids = tokens.reshape(STEPS, BLOCKS, ROWS).transpose(1, 0, 2).reshape(BLOCKS, BROWS, 1)
    ids = ids - lax.axis_index("tp") * embedding.shape[0]
    index, where = save_plan(finish, holder, slot_index, me)
    conv = conv_state.transpose(1, 0, 2).reshape(3 * ROWS, INNER).astype(F32)
    scales = jnp.repeat(state_scales.astype(F32), PAGE, axis=1)
    shape = jax.ShapeDtypeStruct
    sums = vmem_call(
        front_kernel, shape((BROWS, 2 * INNER), F32), 5, TP_SCRATCH + list(FRONT_SCRATCH),
        collective_id=0, has_side_effects=True,
    )(ids, embedding, norm_gain.reshape(1, -1), proj_inner, proj_gate)
    half = BROWS // 2
    select_pad = jnp.pad(proj_select, ((0, 128 - 2 * STATE), (0, 0)))
    step, activ, select = vmem_call(
        rank_kernel,
        [shape((BROWS, INNER), F32), shape((BROWS, INNER), F32), shape((BROWS, 128), F32)],
        8,
        [
            pltpu.VMEM((2, half, RCOLS), F32),
            pltpu.VMEM((2, half, RCOLS), F32),
            pltpu.VMEM((half, RCOLS), BF16),
            pltpu.VMEM((3, half, RCOLS), BF16),
            pltpu.VMEM((2, half, RCOLS), F32),
            pltpu.SemaphoreType.DMA((5,)),
            pltpu.SemaphoreType.DMA((5,)),
        ],
        collective_id=1, has_side_effects=True,
    )(
        sums, conv, conv_weight, conv_bias.reshape(1, -1), proj_low, select_pad, proj_dt,
        dt_bias.reshape(1, -1),
    )
    vmem = pl.BlockSpec(memory_space=pltpu.VMEM)
    smem = pl.BlockSpec(memory_space=pltpu.SMEM)
    anywhere = pl.BlockSpec(memory_space=pl.ANY)
    params = pltpu.CompilerParams(vmem_limit_bytes=VMEM_LIMIT)
    gated, final, packed, source = pl.pallas_call(
        state_kernel,
        out_shape=[
            shape((BROWS, INNER), BF16),
            shape((ROWS, STATE, INNER), BF16),
            shape((BLOCKS * PAIRS, STATE, INNER), BF16),
            shape((4 * BROWS, INNER), BF16),
        ],
        in_specs=[smem] + [vmem] * 9,
        out_specs=[vmem] * 4,
        scratch_shapes=[
            pltpu.VMEM((BROWS, STATE, INNER), BF16),
            pltpu.VMEM((BROWS, INNER), F32),
            pltpu.VMEM((BROWS, 128), F32),
            pltpu.VMEM((STATE, INNER), F32),
        ],
        compiler_params=params,
    )(
        jnp.maximum(index, 0), state_codes, scales, step, activ, select, sums, conv, decay_log,
        skip_gain.reshape(1, -1),
    )
    kind = jnp.arange(4, dtype=jnp.int32)[None, :, None] * BROWS
    want = index.reshape(BLOCKS, 1, PAIRS)
    want = jnp.where(want >= 0, want + kind, -1).reshape(BLOCKS * SIDE, 1)
    mixed, got_codes, got_side = pl.pallas_call(
        back_kernel,
        out_shape=[
            shape((BLOCKS, BROWS, FEATS), BF16),
            shape((BLOCKS, PAIRS, STATE, INNER), BF16),
            shape((BLOCKS, SIDE, INNER), BF16),
        ],
        in_specs=[vmem] * 4 + [anywhere],
        out_specs=[vmem, anywhere, anywhere],
        scratch_shapes=TP_SCRATCH + BACK_SCRATCH,
        compiler_params=pltpu.CompilerParams(
            vmem_limit_bytes=VMEM_LIMIT, collective_id=2, has_side_effects=True
        ),
    )(gated, proj_out, want, source, packed.reshape(BLOCKS, PAIRS, STATE, INNER))
    cache_codes, win0, win1, win2, cache_scales = pl.pallas_call(
        place_kernel,
        out_shape=[shape((SLOTS, STATE, INNER), BF16)]
        + [shape((SLOTS, INNER), BF16)] * 3
        + [shape((SLOTS, 128), BF16)],
        in_specs=[smem, vmem, vmem, anywhere],
        out_specs=[anywhere] + [vmem] * 4,
        scratch_shapes=[pltpu.VMEM((STATE, INNER), BF16), pltpu.SemaphoreType.DMA((SLOTS,))],
        compiler_params=params,
    )(
        where, where.reshape(-1, 1), got_side.reshape(BLOCKS * SIDE, INNER),
        got_codes.reshape(BLOCKS * PAIRS, STATE, INNER),
    )
    mixed = mixed.reshape(BLOCKS, STEPS, ROWS, FEATS).transpose(1, 0, 2, 3)
    mixed = mixed.reshape(STEPS, BLOCKS * ROWS, FEATS)
    last = slice((STEPS - 1) * ROWS, BROWS)
    pages = INNER // PAGE
    next_scales = source[3 * BROWS :][last, :pages]
    next_window = jnp.stack([source[k * BROWS : (k + 1) * BROWS][last] for k in range(3)], axis=1)
    cache_window = jnp.stack([win0, win1, win2], axis=1)
    return (
        mixed, final, next_scales, next_window, cache_codes, cache_scales[:, :pages], cache_window,
    )


def solution(mesh):
    in_specs = (
        P(), P(), P(), P(), P("tp", "req"), P("req"), P("req", "tp"), P("req", "tp"),
        P(None, "tp"), P("tp"), P("tp", None), P(None, "tp"), P(None, "tp"), P("tp"),
        P(None, "tp"), P("tp"), P("tp", "req"), P("req", None, "tp"), P("req", "tp"),
        P("req", None, "tp"),
    )
    out_specs = (
        P(None, None, "req"), P("req", None, "tp"), P("req", "tp"), P("req", None, "tp"),
        P("req", None, "tp"), P("req", "tp"), P("req", None, "tp"),
    )
    return jax.shard_map(
        per_device, mesh=mesh, in_specs=in_specs, out_specs=out_specs, check_vma=False
    )
```

```python
import functools

import jax
import jax.numpy as jnp
from jax import lax
from jax.experimental import pallas as pl
from jax.experimental.pallas import tpu as pltpu
from jax.sharding import PartitionSpec as P

D = 8192
STATE = 16
PAGE = 128
STEPS = 4
CAP = 2
ROWS = 24
BLOCKS = 16
BROWS = STEPS * ROWS
SLOTS = 64
INNER = 2048
FEATS = 512
WIDE = 512
RANK = 512
PAIRS = STEPS * CAP
F32 = jnp.float32
BF16 = jnp.bfloat16
MESH = pl.DeviceIdType.MESH
VMEM_LIMIT = 60 * 1024 * 1024


def rcopy(src, dst, send, recv, dev):
    return pltpu.make_async_remote_copy(
        src_ref=src, dst_ref=dst, send_sem=send, recv_sem=recv, device_id=dev, device_id_type=MESH
    )


def mod4(v):
    return lax.rem(v + 8, 4)


def dot(a, b):
    return jnp.dot(a, b, preferred_element_type=F32)


def greet(devices):
    barrier = pltpu.get_barrier_semaphore()
    for dev in devices:
        pl.semaphore_signal(barrier, inc=1, device_id=dev, device_id_type=MESH)
    pl.semaphore_wait(barrier, len(devices))


TP_SCRATCH = [
    pltpu.VMEM((4, 2, BROWS, FEATS), BF16),
    pltpu.VMEM((4, 2, BROWS, FEATS), BF16),
    pltpu.VMEM((4, 2, BROWS, FEATS), F32),
    pltpu.VMEM((2, BROWS, FEATS), BF16),
    pltpu.VMEM((2, BROWS, FEATS), BF16),
    pltpu.VMEM((2, BROWS, FEATS), BF16),
    pltpu.VMEM((2, BROWS, FEATS), BF16),
    pltpu.VMEM((2, BROWS, FEATS), BF16),
    pltpu.VMEM((2, BROWS, FEATS), BF16),
    pltpu.SemaphoreType.DMA((20,)),
    pltpu.SemaphoreType.DMA((20,)),
]


def tp_partners():
    r, t = lax.axis_index("req"), lax.axis_index("tp")
    y, c = lax.div(t, 2), lax.rem(t, 2)
    return [(r, y * 2 + 1 - c), (r, mod4(y + 1) * 2 + c), (r, mod4(y - 1) * 2 + c)]


def tp_sum(get, total, bufs):
    half_s, half_r, part, far_s, far_r, dir_s, dir_r, com_s, com_r, ss, rs = bufs
    t = lax.axis_index("tp")
    y, c = lax.div(t, 2), lax.rem(t, 2)
    core, up, down = tp_partners()
    order = [mod4(y + 2), mod4(y + 1), mod4(y - 1), y]
    sent = []

    def send(src, dst, n, dev):
        copy = rcopy(src, dst, ss.at[n], rs.at[n], dev)
        copy.start()
        sent.append(copy)

    def arrived(ref, n):
        rcopy(ref, ref, ss.at[n], rs.at[n], core).wait_recv()

    def pair(group, yy):
        return pl.ds(2 * (group * 4 + yy), 2)

    for k in range(4):
        half_s[k] = get((1 - c) * 4 + order[k]).astype(BF16)
        send(half_s.at[k], half_r.at[k], k, core)
    for k in range(4):
        mine = get(c * 4 + order[k])
        arrived(half_r.at[k], k)
        part[k] = mine + half_r[k].astype(F32)
        if k == 0:
            far_s[...] = part[0].astype(BF16)
            send(far_s.at[0], far_r.at[0], 4, up)
            send(far_s.at[1], far_r.at[1], 5, down)
        if k == 1:
            dir_s[1] = part[1, 1].astype(BF16)
            send(dir_s.at[1], dir_r.at[1], 7, up)
        if k == 2:
            dir_s[0] = part[2, 0].astype(BF16)
            send(dir_s.at[0], dir_r.at[0], 6, down)
    arrived(far_r.at[0], 4)
    com_s[0] = (part[1, 0] + far_r[0].astype(F32)).astype(BF16)
    send(com_s.at[0], com_r.at[0], 8, up)
    arrived(far_r.at[1], 5)
    com_s[1] = (part[2, 1] + far_r[1].astype(F32)).astype(BF16)
    send(com_s.at[1], com_r.at[1], 9, down)
    own = 2 * (c * 4 + y)
    for h in range(2):
        arrived(dir_r.at[h], 6 + h)
        arrived(com_r.at[h], 8 + h)
        total[own + h] = (part[3, h] + dir_r[h].astype(F32) + com_r[h].astype(F32)).astype(BF16)
    mine = total.at[pair(c, y)]
    send(mine, mine, 10, up)
    send(mine, mine, 11, down)
    send(mine, mine, 12, core)
    below = total.at[pair(c, mod4(y - 1))]
    above = total.at[pair(c, mod4(y + 1))]
    arrived(below, 10)
    first = total.at[2 * (c * 4 + mod4(y - 1))]
    send(first, first, 13, up)
    send(below, below, 15, core)
    arrived(above, 11)
    second = total.at[2 * (c * 4 + mod4(y + 1)) + 1]
    send(second, second, 14, down)
    send(above, above, 16, core)
    far = 2 * (c * 4 + mod4(y + 2))
    arrived(total.at[far], 13)
    send(total.at[far], total.at[far], 17, core)
    arrived(total.at[far + 1], 14)
    send(total.at[far + 1], total.at[far + 1], 18, core)
    arrived(total.at[pair(1 - c, y)], 12)
    arrived(total.at[pair(1 - c, mod4(y - 1))], 15)
    arrived(total.at[pair(1 - c, mod4(y + 1))], 16)
    other = 2 * ((1 - c) * 4 + mod4(y + 2))
    arrived(total.at[other], 17)
    arrived(total.at[other + 1], 18)
    for copy in sent:
        copy.wait_send()


def shift_req(axis, d):
    r, t = lax.axis_index("req"), lax.axis_index("tp")
    x, z = lax.div(r, 4), lax.rem(r, 4)
    if axis == 0:
        return (mod4(x + d) * 4 + z, t)
    return (x * 4 + mod4(z + d), t)


def req_place(axis):
    r = lax.axis_index("req")
    return lax.div(r, 4) if axis == 0 else lax.rem(r, 4)


def req_partners():
    return [shift_req(axis, d) for axis in (0, 1) for d in (1, -1)]


FRONT_SCRATCH = (
    [
        pltpu.VMEM((BLOCKS, BROWS, FEATS), BF16),
        pltpu.VMEM((4, 4 * BROWS, FEATS), BF16),
        pltpu.VMEM((4, 4 * BROWS, FEATS), BF16),
        pltpu.VMEM((4, 4 * BROWS, PAGE), F32),
    ]
    + [pltpu.VMEM((2, 4, 4 * BROWS, WIDE), BF16)] * 6
    + [pltpu.VMEM((2, 4, BROWS, WIDE), BF16)] * 6
    + [pltpu.VMEM((2, 4, 4, BROWS, WIDE), F32)]
    + [pltpu.SemaphoreType.DMA((6, 2, 4)), pltpu.SemaphoreType.DMA((6, 2, 4))]
    + [pltpu.VMEM((4 * BROWS, PAGE), BF16)] * 6
    + [pltpu.VMEM((BROWS, PAGE), BF16)] * 6
    + [pltpu.VMEM((4, BROWS, PAGE), F32)]
    + [pltpu.SemaphoreType.DMA((6,)), pltpu.SemaphoreType.DMA((6,))]
)


class ScatterSum:
    def __init__(self, axis, d, partial, bufs, total, ss, rs):
        self.axes = (axis, 1 - axis)
        self.d = d
        self.partial = partial
        self.far_s, self.far_r, self.dir_s, self.dir_r, self.com_s, self.com_r = bufs[:6]
        self.far2_s, self.far2_r, self.dir2_s, self.dir2_r, self.com2_s, self.com2_r = bufs[6:]
        self.total = total
        self.ss, self.rs = ss, rs

    def copy(self, n):
        src = (self.far_s, self.dir_s, self.com_s, self.far2_s, self.dir2_s, self.com2_s)[n]
        dst = (self.far_r, self.dir_r, self.com_r, self.far2_r, self.dir2_r, self.com2_r)[n]
        d = -self.d if n % 3 == 1 else self.d
        return rcopy(src, dst, self.ss(n), self.rs(n), shift_req(self.axes[n // 3], d))

    def far(self):
        p = req_place(self.axes[0])
        self.far_s[...] = self.partial(mod4(p + 2)).astype(BF16)
        self.copy(0).start()

    def direct(self):
        p = req_place(self.axes[0])
        self.dir_s[...] = self.partial(mod4(p - self.d)).astype(BF16)
        self.copy(1).start()

    def combined(self):
        p = req_place(self.axes[0])
        mine = self.partial(mod4(p + self.d))
        self.copy(0).wait_recv()
        self.com_s[...] = (mine + self.far_r[...].astype(F32)).astype(BF16)
        self.copy(2).start()

    def own(self):
        p, q = req_place(self.axes[0]), req_place(self.axes[1])
        mine = self.partial(p)
        self.copy(1).wait_recv()
        self.copy(2).wait_recv()
        mine = mine + self.dir_r[...].astype(F32) + self.com_r[...].astype(F32)
        self.total[...] = mine.reshape(4, BROWS, mine.shape[1])
        self.far2_s[...] = self.total[mod4(q + 2)].astype(BF16)
        self.copy(3).start()
        self.dir2_s[...] = self.total[mod4(q - self.d)].astype(BF16)
        self.copy(4).start()

    def combined2(self):
        q = req_place(self.axes[1])
        self.copy(3).wait_recv()
        self.com2_s[...] = (self.total[mod4(q + self.d)] + self.far2_r[...].astype(F32)).astype(
            BF16
        )
        self.copy(5).start()

    def result(self):
        q = req_place(self.axes[1])
        self.copy(4).wait_recv()
        self.copy(5).wait_recv()
        return self.total[q] + self.dir2_r[...].astype(F32) + self.com2_r[...].astype(F32)

    def drain(self):
        for n in range(6):
            self.copy(n).wait_send()


def front_kernel(ids, emb, gain, w_inner, w_gate, out, *scratch):
    tp_bufs, rest = scratch[: len(TP_SCRATCH)], scratch[len(TP_SCRATCH) :]
    embedded, lhs_x, lhs_z, squares = rest[:4]
    big = rest[4:17]
    big_ss, big_rs = rest[17:19]
    small = rest[19:32]
    small_ss, small_rs = rest[32:34]
    greet(tp_partners() + req_partners())

    def looked(ch):
        want = ids[pl.ds(2 * ch, 2)].reshape(2 * BROWS, 1)
        span = 1024
        acc = jnp.zeros((2 * BROWS, FEATS), F32)
        for k in range(emb.shape[0] // span):
            lane = lax.broadcasted_iota(jnp.int32, (2 * BROWS, span), 1) + k * span
            hot = jnp.where(lane == want, 1.0, 0.0).astype(BF16)
            acc = acc + dot(hot, emb[k * span : (k + 1) * span, :])
        return acc.reshape(2, BROWS, FEATS)

    tp_sum(looked, embedded, tp_bufs)

    def spread(b, carry):
        x, z = lax.div(b, 4), lax.rem(b, 4)
        rows = embedded[b].astype(F32)
        scaled = (rows * gain[...]).astype(BF16)
        lhs_x[x, pl.ds(pl.multiple_of(z * BROWS, BROWS), BROWS), :] = scaled
        lhs_z[z, pl.ds(pl.multiple_of(x * BROWS, BROWS), BROWS), :] = scaled
        squares[x, pl.ds(pl.multiple_of(z * BROWS, BROWS), BROWS), :] = jnp.broadcast_to(
            jnp.sum(rows * rows, axis=1, keepdims=True), (BROWS, PAGE)
        )
        return carry

    lax.fori_loop(0, BLOCKS, spread, 0)

    def unit(ab, u):
        lhs, weight = ((lhs_x, w_inner), (lhs_z, w_gate))[ab]

        def partial(chunk):
            cols = pl.ds(pl.multiple_of(u * WIDE, WIDE), WIDE)
            return dot(lhs[chunk], weight[:, cols])

        views = [ref.at[ab, u] for ref in big[:12]]
        return ScatterSum(
            ab,
            1 - 2 * lax.rem(u, 2),
            partial,
            views,
            big[12].at[ab, u],
            lambda n: big_ss.at[n, ab, u],
            lambda n: big_rs.at[n, ab, u],
        )

    norm = ScatterSum(
        0, 1, lambda chunk: squares[chunk], small[:12], small[12],
        lambda n: small_ss.at[n], lambda n: small_rs.at[n],
    )

    def each(step):
        def body(u, carry):
            for ab in range(2):
                step(ab, u, unit(ab, u))
            return carry

        lax.fori_loop(0, 4, body, 0)

    norm.far()
    each(lambda ab, u, s: s.far())
    norm.direct()
    each(lambda ab, u, s: s.direct())
    norm.combined()
    each(lambda ab, u, s: s.combined())
    norm.own()
    each(lambda ab, u, s: s.own())
    norm.combined2()
    each(lambda ab, u, s: s.combined2())
    inv_rms = lax.rsqrt(norm.result()[:, :1] / D + 1e-05)

    def finish(ab, u, s):
        cols = pl.ds(pl.multiple_of((ab * 4 + u) * WIDE, WIDE), WIDE)
        out[:, cols] = s.result() * inv_rms

    each(finish)
    norm.drain()
    each(lambda ab, u, s: s.drain())


def vmem_call(kernel, out_shape, n_in, scratch, **params):
    spec = pl.BlockSpec(memory_space=pltpu.VMEM)
    return pl.pallas_call(
        kernel,
        out_shape=out_shape,
        in_specs=[spec] * n_in,
        out_specs=jax.tree.map(lambda _: spec, out_shape),
        scratch_shapes=scratch,
        compiler_params=pltpu.CompilerParams(vmem_limit_bytes=VMEM_LIMIT, **params),
    )


def silu(v):
    return v / (1.0 + jnp.exp(-v))


RCOLS = RANK + 128


def rank_kernel(
    sums, conv, taps, bias, w_low, w_select, w_dt, dt_bias, step, activ, select,
    pair_s, pair_r, quad_s, quad_r, full, ss, rs,
):
    r, t = lax.axis_index("req"), lax.axis_index("tp")
    y, c = lax.div(t, 2), lax.rem(t, 2)
    core = (r, y * 2 + 1 - c)
    others = [(r, mod4(y + d) * 2 + c) for d in (1, 2, 3)]
    greet([core] + others)
    for n in range(STEPS):
        total = bias[...] + jnp.zeros((ROWS, INNER), F32)
        for k in range(4):
            at = n + k
            if at < 3:
                row = conv[at * ROWS : (at + 1) * ROWS, :]
            else:
                row = sums[(at - 3) * ROWS : (at - 2) * ROWS, :INNER].astype(BF16).astype(F32)
            total = total + row * taps[k : k + 1, :]
        activ[n * ROWS : (n + 1) * ROWS, :] = silu(total).astype(BF16).astype(F32)
    act = activ[...].astype(BF16)
    low = dot(act, w_low[...]).reshape(2, BROWS // 2, RANK)
    sel = lax.dot_general(
        act, w_select[...], (((1,), (1,)), ((), ())), preferred_element_type=F32
    ).reshape(2, BROWS // 2, 128)
    pair_s[:, :, :RANK] = low
    pair_s[:, :, RANK:] = sel
    swap = rcopy(pair_s, pair_r, ss.at[0], rs.at[0], core)
    swap.start()
    swap.wait_recv()
    chip = pair_s[c] + pair_r[c]
    quad_s[...] = chip.astype(BF16)
    copies = [rcopy(quad_s, quad_r.at[n], ss.at[1 + n], rs.at[1 + n], others[n]) for n in range(3)]
    for copy in copies:
        copy.start()
    acc = quad_s[...].astype(F32)
    for n in range(3):
        copies[n].wait_recv()
        acc = acc + quad_r[n].astype(F32)
    full[c] = acc
    back = rcopy(full.at[c], full.at[c], ss.at[4], rs.at[4], core)
    back.start()
    rcopy(full.at[1 - c], full.at[1 - c], ss.at[4], rs.at[4], core).wait_recv()
    low_rank = full[:, :, :RANK].reshape(BROWS, RANK).astype(BF16)
    select[...] = full[:, :, RANK:].reshape(BROWS, 128)
    v = dot(low_rank, w_dt[...]) + dt_bias[...]
    step[...] = jnp.maximum(v, 0.0) + jnp.log1p(jnp.exp(-jnp.abs(v)))
    swap.wait_send()
    for copy in copies:
        copy.wait_send()
    back.wait_send()


def state_kernel(
    codes, scales, step, activ, select, sums, conv, decay_log, skip,
    gated, final, new_codes, source, output, scale_rows, rates,
):
    lane = lax.broadcasted_iota(jnp.int32, (STATE, 128), 1)
    row_of = lax.broadcasted_iota(jnp.int32, (STATE, 128), 0)
    page_lane = lax.broadcasted_iota(jnp.int32, (1, 128), 1)
    width = 4 * PAGE

    def request(i, carry):
        b_in, c_out = [], []
        for n in range(STEPS):
            row = select[pl.ds(n * ROWS + i, 1), :]
            b_in.append(jnp.sum(jnp.where(lane == row_of, row, 0.0), axis=1, keepdims=True))
            c_out.append(
                jnp.sum(jnp.where(lane == row_of + STATE, row, 0.0), axis=1, keepdims=True)
            )
        kept = [jnp.zeros((1, 128), F32) for _ in range(STEPS)]
        for part in range(INNER // width):
            cols = slice(part * width, (part + 1) * width)
            rate = rates[:, cols]
            current = codes[i, :, cols].astype(F32) * scales[pl.ds(i, 1), cols]
            for n in range(STEPS):
                at = n * ROWS + i
                dt = step[pl.ds(at, 1), cols]
                act = activ[pl.ds(at, 1), cols]
                current = jnp.exp2(dt * rate) * current + (dt * act) * b_in[n]
                output[pl.ds(at, 1), cols] = jnp.sum(current * c_out[n], axis=0, keepdims=True)
                peak = jnp.max(jnp.abs(current), axis=0, keepdims=True)
                for page in range(4):
                    here = slice(page * PAGE, (page + 1) * PAGE)
                    top = jnp.max(peak[:, here], axis=1, keepdims=True)
                    scale = (top + 1e-06).astype(BF16).astype(F32)
                    kept[n] = jnp.where(page_lane == part * 4 + page, scale, kept[n])
                    new_codes[at, :, part * width + page * PAGE : part * width + (page + 1) * PAGE] = (
                        current[:, here] * (1.0 / scale)
                    ).astype(BF16)
        for n in range(STEPS):
            scale_rows[pl.ds(n * ROWS + i, 1), :] = kept[n]
        final[i] = new_codes[(STEPS - 1) * ROWS + i]
        return carry

    rates[...] = -jnp.exp(decay_log[...]) * 1.4426950408889634
    lax.fori_loop(0, ROWS, request, 0)
    gated[...] = (
        (output[...] + skip[...] * activ[...]) * silu(sums[:, INNER:])
    ).astype(BF16)
    for k in range(3):
        if k < 2:
            source[k * BROWS : (k + 1) * BROWS, :] = jnp.concatenate(
                [conv[(k + 1) * ROWS :, :], sums[: (k + 2) * ROWS, :INNER]], axis=0
            ).astype(BF16)
        else:
            source[k * BROWS : (k + 1) * BROWS, :] = sums[:, :INNER].astype(BF16)
    source[3 * BROWS :, :] = jnp.zeros((BROWS, INNER), BF16)
    source[3 * BROWS :, :128] = scale_rows[...].astype(BF16)


BACK_SCRATCH = [
    pltpu.VMEM((BLOCKS, BROWS, INNER // 2), BF16),
    pltpu.VMEM((BLOCKS, BROWS, INNER // 2), BF16),
    pltpu.VMEM((BLOCKS, BROWS, FEATS), F32),
    pltpu.VMEM((BLOCKS, BROWS, FEATS), F32),
    pltpu.SemaphoreType.DMA((2, 16)),
    pltpu.SemaphoreType.DMA((2, 16)),
]


class Gather:
    def __init__(self, axis, buf, ss, rs):
        self.axes = (axis, 1 - axis)
        self.buf, self.ss, self.rs = buf, ss, rs
        self.q, self.p = req_place(axis), req_place(1 - axis)
        self.order = [self.q, mod4(self.q - 1), mod4(self.q + 1), mod4(self.q + 2)]
        self.sent = []

    def send(self, ref, n, axis, d):
        copy = rcopy(ref, ref, self.ss.at[n], self.rs.at[n], shift_req(axis, d))
        copy.start()
        self.sent.append(copy)

    def arrived(self, ref, n):
        rcopy(ref, ref, self.ss.at[n], self.rs.at[n], shift_req(self.axes[0], 1)).wait_recv()

    def block(self, p, q):
        return self.buf.at[p * 4 + q]

    def rows(self, p, q, h):
        return self.buf.at[p * 4 + q, pl.ds(h * (BROWS // 2), BROWS // 2)]

    def start(self):
        mine = self.block(self.p, self.q)
        self.send(mine, 0, self.axes[0], 1)
        self.send(mine, 1, self.axes[0], -1)
        self.spread(0)

    def spread(self, k):
        block = self.block(self.p, self.order[k])
        self.send(block, 4 + k, self.axes[1], 1)
        self.send(block, 8 + k, self.axes[1], -1)

    def near(self):
        self.arrived(self.block(self.p, self.order[1]), 0)
        self.send(self.rows(self.p, self.order[1], 0), 2, self.axes[0], 1)
        self.spread(1)
        self.arrived(self.block(self.p, self.order[2]), 1)
        self.send(self.rows(self.p, self.order[2], 1), 3, self.axes[0], -1)
        self.spread(2)

    def last(self):
        self.arrived(self.rows(self.p, self.order[3], 0), 2)
        self.arrived(self.rows(self.p, self.order[3], 1), 3)
        self.spread(3)

    def relay(self, k):
        below, above = mod4(self.p - 1), mod4(self.p + 1)
        self.arrived(self.block(below, self.order[k]), 4 + k)
        if k < 2:
            self.send(self.block(below, self.order[k]), 12 + k, self.axes[1], 1)
        self.arrived(self.block(above, self.order[k]), 8 + k)
        if k >= 2:
            self.send(self.block(above, self.order[k]), 12 + k, self.axes[1], -1)

    def end(self, k):
        self.arrived(self.block(mod4(self.p + 2), self.order[k]), 12 + k)

    def drain(self):
        for copy in self.sent:
            copy.wait_send()


def back_kernel(gated, w_out, mixed, *scratch):
    tp_bufs, rest = scratch[: len(TP_SCRATCH)], scratch[len(TP_SCRATCH) :]
    buf_a, buf_b, acc_a, acc_b, gss, grs = rest
    r = lax.axis_index("req")
    x, z = lax.div(r, 4), lax.rem(r, 4)
    greet(tp_partners() + req_partners())
    half = INNER // 2
    buf_a[r] = gated[:, :half]
    buf_b[z * 4 + x] = gated[:, half:]
    parts = [
        Gather(1, buf_a, gss.at[0], grs.at[0]),
        Gather(0, buf_b, gss.at[1], grs.at[1]),
    ]
    for part in parts:
        part.start()

    def project(part, p, k):
        buf, acc, rows = ((buf_a, acc_a, slice(0, half)), (buf_b, acc_b, slice(half, INNER)))[part]
        at = p * 4 + parts[part].order[k]
        acc[at] = dot(buf[at], w_out[rows, :])

    for n in range(2):
        project(n, parts[n].p, 0)
    for part in parts:
        part.near()
    for n in range(2):
        project(n, parts[n].p, 1)
        project(n, parts[n].p, 2)
    for part in parts:
        part.last()
    for n in range(2):
        project(n, parts[n].p, 3)
    for k in range(4):
        for part in parts:
            part.relay(k)
        for n in range(2):
            project(n, mod4(parts[n].p - 1), k)
            project(n, mod4(parts[n].p + 1), k)
    for k in range(4):
        for n in range(2):
            parts[n].end(k)
            project(n, mod4(parts[n].p + 2), k)

    def summed(ch):
        both = []
        for h in range(2):
            b = 2 * ch + h
            both.append(acc_a[b] + acc_b[lax.rem(b, 4) * 4 + lax.div(b, 4)])
        return jnp.stack(both)

    tp_sum(summed, mixed, tp_bufs)
    for part in parts:
        part.drain()


MOST = 32
HALF = INNER // 2
SAVE_SCRATCH = [
    pltpu.VMEM((2, 4 * MOST, STATE, HALF), BF16),
    pltpu.VMEM((2, 4 * MOST, STATE, HALF), BF16),
    pltpu.VMEM((2, 4 * MOST, STATE, HALF), BF16),
    pltpu.VMEM((2, 16 * MOST, HALF), BF16),
    pltpu.VMEM((2, 16 * MOST, HALF), BF16),
    pltpu.VMEM((2, 16 * MOST, HALF), BF16),
    pltpu.SemaphoreType.DMA((2, 2, 3, 2)),
    pltpu.SemaphoreType.DMA((2, 2, 3, 2)),
]


def save_kernel(
    counts, index, want1, want2, want3, codes, source, out, win0, win1, win2, scale,
    sent, got1, got2, side, side1, side2, ss, rs,
):
    side1[...] = jnp.zeros_like(side1)
    side2[...] = jnp.zeros_like(side2)
    offsets = (2, 1, 3)
    greet([shift_req(axis, d) for axis in (0, 1) for d in offsets])

    def hot(want, span):
        lane = lax.broadcasted_iota(jnp.int32, (want.shape[0], span), 1)
        return jnp.where(lane == want, 1.0, 0.0).astype(BF16)

    def rows(ref, h, at, count):
        return ref.at[h, pl.ds(pl.multiple_of(at, 16), count)]

    def phase(n, want, load, side_from, into, side_into):
        count = counts[n]
        copies = []
        for d in offsets + (0,):
            for h in range(2):
                axis = h if n == 0 else 1 - h
                here = req_place(axis)
                dest = mod4(here + d)
                keep = (into, side_into) if d == 0 else (sent, side)

                def pack(m, carry):
                    at = index[(n * 2 + h) * 4 * MOST + dest * MOST + m]
                    keep[0][h, dest * MOST + m] = load(h, jnp.maximum(at, 0))
                    return carry

                lax.fori_loop(0, count, pack, 0)
                block = pl.ds(pl.multiple_of(dest * 4 * MOST, 4 * MOST), 4 * MOST)
                keep[1][h, block, :] = dot(
                    hot(want[h, block, :], side_from(h).shape[0]), side_from(h)
                ).astype(BF16)
                if d == 0:
                    continue
                k = offsets.index(d)
                dev = shift_req(axis, d)
                pairs = (
                    (rows(sent, h, dest * MOST, count), rows(into, h, here * MOST, count)),
                    (
                        rows(side, h, dest * 4 * MOST, 4 * count),
                        rows(side_into, h, here * 4 * MOST, 4 * count),
                    ),
                )
                for i, (src, dst) in enumerate(pairs):
                    copy = rcopy(src, dst, ss.at[n, h, k, i], rs.at[n, h, k, i], dev)
                    copy.start()
                    copies.append(copy)
        for k, d in enumerate(offsets):
            for h in range(2):
                axis = h if n == 0 else 1 - h
                origin = mod4(req_place(axis) - d)
                dev = shift_req(axis, d)
                for i, ref in enumerate(
                    (
                        rows(into, h, origin * MOST, count),
                        rows(side_into, h, origin * 4 * MOST, 4 * count),
                    )
                ):
                    rcopy(ref, ref, ss.at[n, h, k, i], rs.at[n, h, k, i], dev).wait_recv()
        for copy in copies:
            copy.wait_send()

    phase(
        0, want1, lambda h, at: codes[at, :, h * HALF : (h + 1) * HALF],
        lambda h: source[:, h * HALF : (h + 1) * HALF], got1, side1,
    )
    phase(1, want2, lambda h, at: got1[h, at], lambda h: side1[h], got2, side2)
    base = 4 * 4 * MOST

    def place(s, carry):
        for h in range(2):
            at = index[base + h * SLOTS + s]
            row = got2[h, jnp.maximum(at, 0)]
            out[s, :, h * HALF : (h + 1) * HALF] = jnp.where(at >= 0, row, jnp.zeros_like(row))
        return carry

    lax.fori_loop(0, SLOTS, place, 0)
    for h in range(2):
        cols = slice(h * HALF, (h + 1) * HALF)
        for k, ref in enumerate((win0, win1, win2)):
            ref[:, cols] = dot(hot(want3[h, k], 16 * MOST), side2[h]).astype(BF16)
    scale[...] = dot(hot(want3[0, 3], 16 * MOST), side2[0, :, :128]).astype(BF16)


SAVE_COUNTS = ((20, 24), (24, 28), (MOST, MOST))


def before(flags, keys):
    n = flags.shape[1]
    earlier = jnp.arange(n)[None, :] < jnp.arange(n)[:, None]
    same = earlier[None] & flags[:, None, :] & (keys[:, None, :] == keys[:, :, None])
    return jnp.sum(same.astype(jnp.int32), axis=2)


def chosen(mask, value):
    return jnp.sum(jnp.where(mask, value + 1, 0), axis=-1) - 1


def save_plan(finish, holder, slot_index, me):
    def events(a):
        return a.reshape(STEPS, 4, 4, ROWS).transpose(1, 2, 0, 3).reshape(4, 4, BROWS)

    fin, own, slot = events(finish) == 1, events(holder), events(slot_index)
    first, second, last, needs = [], [], [], []
    for h in range(2):
        if h == 1:
            fin, own, slot = (a.transpose(1, 0, 2) for a in (fin, own, slot))
        p_of = (lax.div(own, 4), lax.rem(own, 4))[h]
        q_of = (lax.rem(own, 4), lax.div(own, 4))[h]
        p_me = (lax.div(me, 4), lax.rem(me, 4))[h]
        q_me = (lax.rem(me, 4), lax.div(me, 4))[h]
        rank1 = before(fin.reshape(16, BROWS), p_of.reshape(16, BROWS)).reshape(4, 4, BROWS)
        by_q = [a.transpose(1, 0, 2).reshape(4, 4 * BROWS) for a in (fin, own)]
        rank2 = before(*by_q).reshape(4, 4, BROWS).transpose(1, 0, 2)
        needs.append((jnp.max(jnp.where(fin, rank1, 0)), jnp.max(jnp.where(fin, rank2, 0))))
        number = jnp.arange(4)[:, None, None]
        count = jnp.arange(MOST)[None, :, None]

        def mine(a):
            return lax.dynamic_slice(a, (p_me, q_me, 0), (1, 1, BROWS)).reshape(1, 1, BROWS)

        mask = mine(fin) & (mine(p_of) == number) & (mine(rank1) == count)
        first.append(chosen(mask, jnp.arange(BROWS)[None, None, :]))

        def column(a):
            return lax.dynamic_slice(a, (0, q_me, 0), (4, 1, BROWS)).reshape(1, 1, 4 * BROWS)

        at = jnp.arange(4)[:, None, None] * MOST + rank1
        mask = column(fin) & (column(p_of) == p_me) & (column(q_of) == number)
        second.append(chosen(mask & (column(rank2) == count), column(at)))
        at = jnp.arange(4)[None, :, None] * MOST + rank2
        mask = (fin & (own == me)).reshape(1, -1) & (
            slot.reshape(1, -1) == jnp.arange(SLOTS)[:, None]
        )
        last.append(chosen(mask, at.reshape(1, -1)))
    first, second, last = (jnp.stack(a) for a in (first, second, last))
    index = jnp.concatenate([first.reshape(-1), second.reshape(-1), last.reshape(-1)])
    kind = jnp.arange(4, dtype=jnp.int32)

    def column_of(base, value, axis):
        return jnp.where(jnp.expand_dims(base, axis) >= 0, value, -1)

    want1 = column_of(first, first[..., None] + kind * BROWS, -1).reshape(2, 16 * MOST, 1)
    want2 = column_of(second, second[..., None] * 4 + kind, -1).reshape(2, 16 * MOST, 1)
    want3 = column_of(last, last[:, None, :] * 4 + kind[:, None], 1).reshape(2, 4, SLOTS, 1)
    need1 = jnp.maximum(needs[0][0], needs[1][0]) + 1
    need2 = jnp.maximum(needs[0][1], needs[1][1]) + 1
    return index, want1, want2, want3, need1, need2


def per_device(
    tokens, finish, holder, slot_index, embedding, norm_gain, proj_inner, proj_gate, conv_weight,
    conv_bias, proj_low, proj_select, proj_dt, dt_bias, decay_log, skip_gain, proj_out, state_codes,
    state_scales, conv_state,
):
    me = lax.axis_index("req")
    ids = tokens.reshape(STEPS, BLOCKS, ROWS).transpose(1, 0, 2).reshape(BLOCKS, BROWS, 1)
    ids = ids - lax.axis_index("tp") * embedding.shape[0]
    index, want1, want2, want3, need1, need2 = save_plan(finish, holder, slot_index, me)
    conv = conv_state.transpose(1, 0, 2).reshape(3 * ROWS, INNER).astype(F32)
    scales = jnp.repeat(state_scales.astype(F32), PAGE, axis=1)
    shape = jax.ShapeDtypeStruct
    sums = vmem_call(
        front_kernel, shape((BROWS, 2 * INNER), F32), 5, TP_SCRATCH + list(FRONT_SCRATCH),
        collective_id=0, has_side_effects=True,
    )(ids, embedding, norm_gain.reshape(1, -1), proj_inner, proj_gate)
    half = BROWS // 2
    select_pad = jnp.pad(proj_select, ((0, 128 - 2 * STATE), (0, 0)))
    step, activ, select = vmem_call(
        rank_kernel,
        [shape((BROWS, INNER), F32), shape((BROWS, INNER), F32), shape((BROWS, 128), F32)],
        8,
        [
            pltpu.VMEM((2, half, RCOLS), F32),
            pltpu.VMEM((2, half, RCOLS), F32),
            pltpu.VMEM((half, RCOLS), BF16),
            pltpu.VMEM((3, half, RCOLS), BF16),
            pltpu.VMEM((2, half, RCOLS), F32),
            pltpu.SemaphoreType.DMA((5,)),
            pltpu.SemaphoreType.DMA((5,)),
        ],
        collective_id=1, has_side_effects=True,
    )(
        sums, conv, conv_weight, conv_bias.reshape(1, -1), proj_low, select_pad, proj_dt,
        dt_bias.reshape(1, -1),
    )
    vmem = pl.BlockSpec(memory_space=pltpu.VMEM)
    smem = pl.BlockSpec(memory_space=pltpu.SMEM)
    gated, final, new_codes, source = vmem_call(
        state_kernel,
        [
            shape((BROWS, INNER), BF16),
            shape((ROWS, STATE, INNER), BF16),
            shape((BROWS, STATE, INNER), BF16),
            shape((4 * BROWS, INNER), BF16),
        ],
        9,
        [
            pltpu.VMEM((BROWS, INNER), F32),
            pltpu.VMEM((BROWS, 128), F32),
            pltpu.VMEM((STATE, INNER), F32),
        ],
    )(
        state_codes, scales, step, activ, select, sums, conv, decay_log, skip_gain.reshape(1, -1),
    )
    mixed = vmem_call(
        back_kernel, shape((BLOCKS, BROWS, FEATS), BF16), 2, TP_SCRATCH + BACK_SCRATCH,
        collective_id=2, has_side_effects=True,
    )(gated, proj_out)

    def save(n):
        counts = SAVE_COUNTS[n]

        def call(*operands):
            return pl.pallas_call(
                functools.partial(save_kernel, counts),
                out_shape=[shape((SLOTS, STATE, INNER), BF16)]
                + [shape((SLOTS, INNER), BF16)] * 3
                + [shape((SLOTS, 128), BF16)],
                in_specs=[smem] + [vmem] * 5,
                out_specs=[vmem] * 5,
                scratch_shapes=SAVE_SCRATCH,
                compiler_params=pltpu.CompilerParams(
                    vmem_limit_bytes=VMEM_LIMIT, collective_id=3 + n, has_side_effects=True
                ),
            )(*operands)

        return call

    tight = [(need1 <= a) & (need2 <= b) for a, b in SAVE_COUNTS[:-1]]
    which = jnp.where(tight[0], 0, jnp.where(tight[1], 1, 2))
    cache_codes, win0, win1, win2, cache_scales = lax.switch(
        which, [save(n) for n in range(len(SAVE_COUNTS))], index, want1, want2, want3, new_codes,
        source,
    )
    mixed = mixed.reshape(BLOCKS, STEPS, ROWS, FEATS).transpose(1, 0, 2, 3)
    mixed = mixed.reshape(STEPS, BLOCKS * ROWS, FEATS)
    last = slice((STEPS - 1) * ROWS, BROWS)
    pages = INNER // PAGE
    next_scales = source[3 * BROWS :][last, :pages]
    next_window = jnp.stack([source[k * BROWS : (k + 1) * BROWS][last] for k in range(3)], axis=1)
    cache_window = jnp.stack([win0, win1, win2], axis=1)
    return (
        mixed, final, next_scales, next_window, cache_codes, cache_scales[:, :pages], cache_window,
    )


def solution(mesh):
    in_specs = (
        P(), P(), P(), P(), P("tp", "req"), P("req"), P("req", "tp"), P("req", "tp"),
        P(None, "tp"), P("tp"), P("tp", None), P(None, "tp"), P(None, "tp"), P("tp"),
        P(None, "tp"), P("tp"), P("tp", "req"), P("req", None, "tp"), P("req", "tp"),
        P("req", None, "tp"),
    )
    out_specs = (
        P(None, None, "req"), P("req", None, "tp"), P("req", "tp"), P("req", None, "tp"),
        P("req", None, "tp"), P("req", "tp"), P("req", None, "tp"),
    )
    return jax.shard_map(
        per_device, mesh=mesh, in_specs=in_specs, out_specs=out_specs, check_vma=False
    )
```

```python
import functools

import jax
import jax.numpy as jnp
from jax import lax
from jax.experimental import pallas as pl
from jax.experimental.pallas import tpu as pltpu
from jax.sharding import PartitionSpec as P

D = 8192
STATE = 16
PAGE = 128
STEPS = 4
CAP = 2
ROWS = 24
BLOCKS = 16
BROWS = STEPS * ROWS
SLOTS = 64
INNER = 2048
FEATS = 512
WIDE = 512
RANK = 512
PAIRS = STEPS * CAP
F32 = jnp.float32
BF16 = jnp.bfloat16
MESH = pl.DeviceIdType.MESH
VMEM_LIMIT = 62 * 1024 * 1024


def rcopy(src, dst, send, recv, dev):
    return pltpu.make_async_remote_copy(
        src_ref=src, dst_ref=dst, send_sem=send, recv_sem=recv, device_id=dev, device_id_type=MESH
    )


def mod4(v):
    return lax.rem(v + 8, 4)


def dot(a, b):
    return jnp.dot(a, b, preferred_element_type=F32)


def greet(devices):
    barrier = pltpu.get_barrier_semaphore()
    for dev in devices:
        pl.semaphore_signal(barrier, inc=1, device_id=dev, device_id_type=MESH)
    pl.semaphore_wait(barrier, len(devices))


TP_SCRATCH = [
    pltpu.VMEM((4, 2, BROWS, FEATS), BF16),
    pltpu.VMEM((4, 2, BROWS, FEATS), BF16),
    pltpu.VMEM((4, 2, BROWS, FEATS), F32),
    pltpu.VMEM((2, BROWS, FEATS), BF16),
    pltpu.VMEM((2, BROWS, FEATS), BF16),
    pltpu.VMEM((2, BROWS, FEATS), BF16),
    pltpu.VMEM((2, BROWS, FEATS), BF16),
    pltpu.VMEM((2, BROWS, FEATS), BF16),
    pltpu.VMEM((2, BROWS, FEATS), BF16),
    pltpu.SemaphoreType.DMA((20,)),
    pltpu.SemaphoreType.DMA((20,)),
]


def tp_partners():
    r, t = lax.axis_index("req"), lax.axis_index("tp")
    y, c = lax.div(t, 2), lax.rem(t, 2)
    return [(r, y * 2 + 1 - c), (r, mod4(y + 1) * 2 + c), (r, mod4(y - 1) * 2 + c)]


def tp_sum(get, total, bufs):
    half_s, half_r, part, far_s, far_r, dir_s, dir_r, com_s, com_r, ss, rs = bufs
    t = lax.axis_index("tp")
    y, c = lax.div(t, 2), lax.rem(t, 2)
    core, up, down = tp_partners()
    order = [mod4(y + 2), mod4(y + 1), mod4(y - 1), y]
    sent = []

    def send(src, dst, n, dev):
        copy = rcopy(src, dst, ss.at[n], rs.at[n], dev)
        copy.start()
        sent.append(copy)

    def arrived(ref, n):
        rcopy(ref, ref, ss.at[n], rs.at[n], core).wait_recv()

    def pair(group, yy):
        return pl.ds(2 * (group * 4 + yy), 2)

    for k in range(4):
        half_s[k] = get((1 - c) * 4 + order[k]).astype(BF16)
        send(half_s.at[k], half_r.at[k], k, core)
    for k in range(4):
        mine = get(c * 4 + order[k])
        arrived(half_r.at[k], k)
        part[k] = mine + half_r[k].astype(F32)
        if k == 0:
            far_s[...] = part[0].astype(BF16)
            send(far_s.at[0], far_r.at[0], 4, up)
            send(far_s.at[1], far_r.at[1], 5, down)
        if k == 1:
            dir_s[1] = part[1, 1].astype(BF16)
            send(dir_s.at[1], dir_r.at[1], 7, up)
        if k == 2:
            dir_s[0] = part[2, 0].astype(BF16)
            send(dir_s.at[0], dir_r.at[0], 6, down)
    arrived(far_r.at[0], 4)
    com_s[0] = (part[1, 0] + far_r[0].astype(F32)).astype(BF16)
    send(com_s.at[0], com_r.at[0], 8, up)
    arrived(far_r.at[1], 5)
    com_s[1] = (part[2, 1] + far_r[1].astype(F32)).astype(BF16)
    send(com_s.at[1], com_r.at[1], 9, down)
    own = 2 * (c * 4 + y)
    for h in range(2):
        arrived(dir_r.at[h], 6 + h)
        arrived(com_r.at[h], 8 + h)
        total[own + h] = (part[3, h] + dir_r[h].astype(F32) + com_r[h].astype(F32)).astype(BF16)
    mine = total.at[pair(c, y)]
    send(mine, mine, 10, up)
    send(mine, mine, 11, down)
    send(mine, mine, 12, core)
    below = total.at[pair(c, mod4(y - 1))]
    above = total.at[pair(c, mod4(y + 1))]
    arrived(below, 10)
    first = total.at[2 * (c * 4 + mod4(y - 1))]
    send(first, first, 13, up)
    send(below, below, 15, core)
    arrived(above, 11)
    second = total.at[2 * (c * 4 + mod4(y + 1)) + 1]
    send(second, second, 14, down)
    send(above, above, 16, core)
    far = 2 * (c * 4 + mod4(y + 2))
    arrived(total.at[far], 13)
    send(total.at[far], total.at[far], 17, core)
    arrived(total.at[far + 1], 14)
    send(total.at[far + 1], total.at[far + 1], 18, core)
    arrived(total.at[pair(1 - c, y)], 12)
    arrived(total.at[pair(1 - c, mod4(y - 1))], 15)
    arrived(total.at[pair(1 - c, mod4(y + 1))], 16)
    other = 2 * ((1 - c) * 4 + mod4(y + 2))
    arrived(total.at[other], 17)
    arrived(total.at[other + 1], 18)
    for copy in sent:
        copy.wait_send()


def shift_req(axis, d):
    r, t = lax.axis_index("req"), lax.axis_index("tp")
    x, z = lax.div(r, 4), lax.rem(r, 4)
    if axis == 0:
        return (mod4(x + d) * 4 + z, t)
    return (x * 4 + mod4(z + d), t)


def req_place(axis):
    r = lax.axis_index("req")
    return lax.div(r, 4) if axis == 0 else lax.rem(r, 4)


def req_partners():
    return [shift_req(axis, d) for axis in (0, 1) for d in (1, -1)]


FRONT_SCRATCH = (
    [
        pltpu.VMEM((BLOCKS, BROWS, FEATS), BF16),
        pltpu.VMEM((4, 4 * BROWS, FEATS), BF16),
        pltpu.VMEM((4, 4 * BROWS, FEATS), BF16),
        pltpu.VMEM((4, 4 * BROWS, PAGE), F32),
    ]
    + [pltpu.VMEM((2, 4, 4 * BROWS, WIDE), BF16)] * 6
    + [pltpu.VMEM((2, 4, BROWS, WIDE), BF16)] * 6
    + [pltpu.VMEM((2, 4, 4, BROWS, WIDE), F32)]
    + [pltpu.SemaphoreType.DMA((6, 2, 4)), pltpu.SemaphoreType.DMA((6, 2, 4))]
    + [pltpu.VMEM((4 * BROWS, PAGE), BF16)] * 6
    + [pltpu.VMEM((BROWS, PAGE), BF16)] * 6
    + [pltpu.VMEM((4, BROWS, PAGE), F32)]
    + [pltpu.SemaphoreType.DMA((6,)), pltpu.SemaphoreType.DMA((6,))]
)


class ScatterSum:
    def __init__(self, axis, d, partial, bufs, total, ss, rs):
        self.axes = (axis, 1 - axis)
        self.d = d
        self.partial = partial
        self.far_s, self.far_r, self.dir_s, self.dir_r, self.com_s, self.com_r = bufs[:6]
        self.far2_s, self.far2_r, self.dir2_s, self.dir2_r, self.com2_s, self.com2_r = bufs[6:]
        self.total = total
        self.ss, self.rs = ss, rs

    def copy(self, n):
        src = (self.far_s, self.dir_s, self.com_s, self.far2_s, self.dir2_s, self.com2_s)[n]
        dst = (self.far_r, self.dir_r, self.com_r, self.far2_r, self.dir2_r, self.com2_r)[n]
        d = -self.d if n % 3 == 1 else self.d
        return rcopy(src, dst, self.ss(n), self.rs(n), shift_req(self.axes[n // 3], d))

    def far(self):
        p = req_place(self.axes[0])
        self.far_s[...] = self.partial(mod4(p + 2)).astype(BF16)
        self.copy(0).start()

    def direct(self):
        p = req_place(self.axes[0])
        self.dir_s[...] = self.partial(mod4(p - self.d)).astype(BF16)
        self.copy(1).start()

    def combined(self):
        p = req_place(self.axes[0])
        mine = self.partial(mod4(p + self.d))
        self.copy(0).wait_recv()
        self.com_s[...] = (mine + self.far_r[...].astype(F32)).astype(BF16)
        self.copy(2).start()

    def own(self):
        p, q = req_place(self.axes[0]), req_place(self.axes[1])
        mine = self.partial(p)
        self.copy(1).wait_recv()
        self.copy(2).wait_recv()
        mine = mine + self.dir_r[...].astype(F32) + self.com_r[...].astype(F32)
        self.total[...] = mine.reshape(4, BROWS, mine.shape[1])
        self.far2_s[...] = self.total[mod4(q + 2)].astype(BF16)
        self.copy(3).start()
        self.dir2_s[...] = self.total[mod4(q - self.d)].astype(BF16)
        self.copy(4).start()

    def combined2(self):
        q = req_place(self.axes[1])
        self.copy(3).wait_recv()
        self.com2_s[...] = (self.total[mod4(q + self.d)] + self.far2_r[...].astype(F32)).astype(
            BF16
        )
        self.copy(5).start()

    def result(self):
        q = req_place(self.axes[1])
        self.copy(4).wait_recv()
        self.copy(5).wait_recv()
        return self.total[q] + self.dir2_r[...].astype(F32) + self.com2_r[...].astype(F32)

    def drain(self):
        for n in range(6):
            self.copy(n).wait_send()


def front_kernel(ids, emb, gain, w_inner, w_gate, out, *scratch):
    tp_bufs, rest = scratch[: len(TP_SCRATCH)], scratch[len(TP_SCRATCH) :]
    embedded, lhs_x, lhs_z, squares = rest[:4]
    big = rest[4:17]
    big_ss, big_rs = rest[17:19]
    small = rest[19:32]
    small_ss, small_rs = rest[32:34]
    greet(tp_partners() + req_partners())

    def looked(ch):
        want = ids[pl.ds(2 * ch, 2)].reshape(2 * BROWS, 1)
        span = 1024
        acc = jnp.zeros((2 * BROWS, FEATS), F32)
        for k in range(emb.shape[0] // span):
            lane = lax.broadcasted_iota(jnp.int32, (2 * BROWS, span), 1) + k * span
            hot = jnp.where(lane == want, 1.0, 0.0).astype(BF16)
            acc = acc + dot(hot, emb[k * span : (k + 1) * span, :])
        return acc.reshape(2, BROWS, FEATS)

    tp_sum(looked, embedded, tp_bufs)

    def spread(b, carry):
        x, z = lax.div(b, 4), lax.rem(b, 4)
        rows = embedded[b].astype(F32)
        scaled = (rows * gain[...]).astype(BF16)
        lhs_x[x, pl.ds(pl.multiple_of(z * BROWS, BROWS), BROWS), :] = scaled
        lhs_z[z, pl.ds(pl.multiple_of(x * BROWS, BROWS), BROWS), :] = scaled
        squares[x, pl.ds(pl.multiple_of(z * BROWS, BROWS), BROWS), :] = jnp.broadcast_to(
            jnp.sum(rows * rows, axis=1, keepdims=True), (BROWS, PAGE)
        )
        return carry

    lax.fori_loop(0, BLOCKS, spread, 0)

    def unit(ab, u):
        lhs, weight = ((lhs_x, w_inner), (lhs_z, w_gate))[ab]

        def partial(chunk):
            cols = pl.ds(pl.multiple_of(u * WIDE, WIDE), WIDE)
            return dot(lhs[chunk], weight[:, cols])

        views = [ref.at[ab, u] for ref in big[:12]]
        return ScatterSum(
            ab,
            1 - 2 * lax.rem(u, 2),
            partial,
            views,
            big[12].at[ab, u],
            lambda n: big_ss.at[n, ab, u],
            lambda n: big_rs.at[n, ab, u],
        )

    norm = ScatterSum(
        0, 1, lambda chunk: squares[chunk], small[:12], small[12],
        lambda n: small_ss.at[n], lambda n: small_rs.at[n],
    )

    def each(step):
        def body(u, carry):
            for ab in range(2):
                step(ab, u, unit(ab, u))
            return carry

        lax.fori_loop(0, 4, body, 0)

    norm.far()
    each(lambda ab, u, s: s.far())
    norm.direct()
    each(lambda ab, u, s: s.direct())
    norm.combined()
    each(lambda ab, u, s: s.combined())
    norm.own()
    each(lambda ab, u, s: s.own())
    norm.combined2()
    each(lambda ab, u, s: s.combined2())
    inv_rms = lax.rsqrt(norm.result()[:, :1] / D + 1e-05)

    def finish(ab, u, s):
        cols = pl.ds(pl.multiple_of((ab * 4 + u) * WIDE, WIDE), WIDE)
        out[:, cols] = s.result() * inv_rms

    each(finish)
    norm.drain()
    each(lambda ab, u, s: s.drain())


def vmem_call(kernel, out_shape, n_in, scratch, **params):
    spec = pl.BlockSpec(memory_space=pltpu.VMEM)
    return pl.pallas_call(
        kernel,
        out_shape=out_shape,
        in_specs=[spec] * n_in,
        out_specs=jax.tree.map(lambda _: spec, out_shape),
        scratch_shapes=scratch,
        compiler_params=pltpu.CompilerParams(vmem_limit_bytes=VMEM_LIMIT, **params),
    )


def silu(v):
    return v / (1.0 + jnp.exp(-v))


RCOLS = RANK + 128


def rank_kernel(
    sums, conv, taps, bias, w_low, w_select, w_dt, dt_bias, step, activ, select,
    pair_s, pair_r, quad_s, quad_r, full, ss, rs,
):
    r, t = lax.axis_index("req"), lax.axis_index("tp")
    y, c = lax.div(t, 2), lax.rem(t, 2)
    core = (r, y * 2 + 1 - c)
    others = [(r, mod4(y + d) * 2 + c) for d in (1, 2, 3)]
    greet([core] + others)
    for n in range(STEPS):
        total = bias[...] + jnp.zeros((ROWS, INNER), F32)
        for k in range(4):
            at = n + k
            if at < 3:
                row = conv[at * ROWS : (at + 1) * ROWS, :]
            else:
                row = sums[(at - 3) * ROWS : (at - 2) * ROWS, :INNER].astype(BF16).astype(F32)
            total = total + row * taps[k : k + 1, :]
        activ[n * ROWS : (n + 1) * ROWS, :] = silu(total).astype(BF16).astype(F32)
    act = activ[...].astype(BF16)
    low = dot(act, w_low[...]).reshape(2, BROWS // 2, RANK)
    sel = lax.dot_general(
        act, w_select[...], (((1,), (1,)), ((), ())), preferred_element_type=F32
    ).reshape(2, BROWS // 2, 128)
    pair_s[:, :, :RANK] = low
    pair_s[:, :, RANK:] = sel
    swap = rcopy(pair_s, pair_r, ss.at[0], rs.at[0], core)
    swap.start()
    swap.wait_recv()
    chip = pair_s[c] + pair_r[c]
    quad_s[...] = chip.astype(BF16)
    copies = [rcopy(quad_s, quad_r.at[n], ss.at[1 + n], rs.at[1 + n], others[n]) for n in range(3)]
    for copy in copies:
        copy.start()
    acc = quad_s[...].astype(F32)
    for n in range(3):
        copies[n].wait_recv()
        acc = acc + quad_r[n].astype(F32)
    full[c] = acc
    back = rcopy(full.at[c], full.at[c], ss.at[4], rs.at[4], core)
    back.start()
    rcopy(full.at[1 - c], full.at[1 - c], ss.at[4], rs.at[4], core).wait_recv()
    low_rank = full[:, :, :RANK].reshape(BROWS, RANK).astype(BF16)
    select[...] = full[:, :, RANK:].reshape(BROWS, 128)
    v = dot(low_rank, w_dt[...]) + dt_bias[...]
    step[...] = jnp.maximum(v, 0.0) + jnp.log1p(jnp.exp(-jnp.abs(v)))
    swap.wait_send()
    for copy in copies:
        copy.wait_send()
    back.wait_send()


def state_kernel(
    codes, scales, step, activ, select, sums, conv, decay_log, skip,
    gated, final, new_codes, source, output, scale_rows, rates,
):
    lane = lax.broadcasted_iota(jnp.int32, (STATE, 128), 1)
    row_of = lax.broadcasted_iota(jnp.int32, (STATE, 128), 0)
    page_lane = lax.broadcasted_iota(jnp.int32, (1, 128), 1)
    width = 4 * PAGE

    def request(i, carry):
        b_in, c_out = [], []
        for n in range(STEPS):
            row = select[pl.ds(n * ROWS + i, 1), :]
            b_in.append(jnp.sum(jnp.where(lane == row_of, row, 0.0), axis=1, keepdims=True))
            c_out.append(
                jnp.sum(jnp.where(lane == row_of + STATE, row, 0.0), axis=1, keepdims=True)
            )
        kept = [jnp.zeros((1, 128), F32) for _ in range(STEPS)]
        for part in range(INNER // width):
            cols = slice(part * width, (part + 1) * width)
            rate = rates[:, cols]
            current = codes[i, :, cols].astype(F32) * scales[pl.ds(i, 1), cols]
            for n in range(STEPS):
                at = n * ROWS + i
                dt = step[pl.ds(at, 1), cols]
                act = activ[pl.ds(at, 1), cols]
                current = jnp.exp2(dt * rate) * current + (dt * act) * b_in[n]
                output[pl.ds(at, 1), cols] = jnp.sum(current * c_out[n], axis=0, keepdims=True)
                peak = jnp.max(jnp.abs(current), axis=0, keepdims=True)
                for page in range(4):
                    here = slice(page * PAGE, (page + 1) * PAGE)
                    top = jnp.max(peak[:, here], axis=1, keepdims=True)
                    scale = (top + 1e-06).astype(BF16).astype(F32)
                    kept[n] = jnp.where(page_lane == part * 4 + page, scale, kept[n])
                    new_codes[at, :, part * width + page * PAGE : part * width + (page + 1) * PAGE] = (
                        current[:, here] * (1.0 / scale)
                    ).astype(BF16)
        for n in range(STEPS):
            scale_rows[pl.ds(n * ROWS + i, 1), :] = kept[n]
        final[i] = new_codes[(STEPS - 1) * ROWS + i]
        return carry

    rates[...] = -jnp.exp(decay_log[...]) * 1.4426950408889634
    lax.fori_loop(0, ROWS, request, 0)
    gated[...] = (
        (output[...] + skip[...] * activ[...]) * silu(sums[:, INNER:])
    ).astype(BF16)
    for k in range(3):
        if k < 2:
            source[k * BROWS : (k + 1) * BROWS, :] = jnp.concatenate(
                [conv[(k + 1) * ROWS :, :], sums[: (k + 2) * ROWS, :INNER]], axis=0
            ).astype(BF16)
        else:
            source[k * BROWS : (k + 1) * BROWS, :] = sums[:, :INNER].astype(BF16)
    source[3 * BROWS :, :] = jnp.zeros((BROWS, INNER), BF16)
    source[3 * BROWS :, :128] = scale_rows[...].astype(BF16)


BACK_SCRATCH = [
    pltpu.VMEM((BLOCKS, BROWS, INNER // 2), BF16),
    pltpu.VMEM((BLOCKS, BROWS, INNER // 2), BF16),
    pltpu.VMEM((BLOCKS, BROWS, FEATS), F32),
    pltpu.SemaphoreType.DMA((2, 16)),
    pltpu.SemaphoreType.DMA((2, 16)),
]


class Gather:
    def __init__(self, axis, buf, ss, rs):
        self.axes = (axis, 1 - axis)
        self.buf, self.ss, self.rs = buf, ss, rs
        self.q, self.p = req_place(axis), req_place(1 - axis)
        self.order = [self.q, mod4(self.q - 1), mod4(self.q + 1), mod4(self.q + 2)]
        self.sent = []

    def send(self, ref, n, axis, d):
        copy = rcopy(ref, ref, self.ss.at[n], self.rs.at[n], shift_req(axis, d))
        copy.start()
        self.sent.append(copy)

    def arrived(self, ref, n):
        rcopy(ref, ref, self.ss.at[n], self.rs.at[n], shift_req(self.axes[0], 1)).wait_recv()

    def block(self, p, q):
        return self.buf.at[p * 4 + q]

    def rows(self, p, q, h):
        return self.buf.at[p * 4 + q, pl.ds(h * (BROWS // 2), BROWS // 2)]

    def start(self):
        mine = self.block(self.p, self.q)
        self.send(mine, 0, self.axes[0], 1)
        self.send(mine, 1, self.axes[0], -1)
        self.spread(0)

    def spread(self, k):
        block = self.block(self.p, self.order[k])
        self.send(block, 4 + k, self.axes[1], 1)
        self.send(block, 8 + k, self.axes[1], -1)

    def near(self):
        self.arrived(self.block(self.p, self.order[1]), 0)
        self.send(self.rows(self.p, self.order[1], 0), 2, self.axes[0], 1)
        self.spread(1)
        self.arrived(self.block(self.p, self.order[2]), 1)
        self.send(self.rows(self.p, self.order[2], 1), 3, self.axes[0], -1)
        self.spread(2)

    def last(self):
        self.arrived(self.rows(self.p, self.order[3], 0), 2)
        self.arrived(self.rows(self.p, self.order[3], 1), 3)
        self.spread(3)

    def relay(self, k):
        below, above = mod4(self.p - 1), mod4(self.p + 1)
        self.arrived(self.block(below, self.order[k]), 4 + k)
        if k < 2:
            self.send(self.block(below, self.order[k]), 12 + k, self.axes[1], 1)
        self.arrived(self.block(above, self.order[k]), 8 + k)
        if k >= 2:
            self.send(self.block(above, self.order[k]), 12 + k, self.axes[1], -1)

    def end(self, k):
        self.arrived(self.block(mod4(self.p + 2), self.order[k]), 12 + k)

    def drain(self):
        for copy in self.sent:
            copy.wait_send()


class Project:
    def __init__(self, gated, w_out, scratch):
        self.tp_bufs, rest = scratch[: len(TP_SCRATCH)], scratch[len(TP_SCRATCH) :]
        self.buf_a, self.buf_b, self.acc, gss, grs = rest
        self.gated, self.w_out = gated, w_out
        self.parts = [
            Gather(1, self.buf_a, gss.at[0], grs.at[0]),
            Gather(0, self.buf_b, gss.at[1], grs.at[1]),
        ]

    def start(self):
        r = lax.axis_index("req")
        self.acc[...] = jnp.zeros_like(self.acc)
        self.buf_a[r] = self.gated[:, :HALF]
        self.buf_b[lax.rem(r, 4) * 4 + lax.div(r, 4)] = self.gated[:, HALF:]
        for part in self.parts:
            part.start()

    def project(self, n, p, k):
        q = self.parts[n].order[k]
        if n == 0:
            self.acc[p * 4 + q] += dot(self.buf_a[p * 4 + q], self.w_out[:HALF, :])
        else:
            self.acc[q * 4 + p] += dot(self.buf_b[p * 4 + q], self.w_out[HALF:, :])

    def gather(self):
        parts = self.parts
        for part in parts:
            part.near()
        for part in parts:
            part.last()
        for k in range(4):
            for n in range(2):
                self.project(n, parts[n].p, k)
        for k in range(4):
            for part in parts:
                part.relay(k)
            for n in range(2):
                self.project(n, mod4(parts[n].p - 1), k)
                self.project(n, mod4(parts[n].p + 1), k)
        for k in range(4):
            for n in range(2):
                parts[n].end(k)
                self.project(n, mod4(parts[n].p + 2), k)

    def total(self, mixed):
        tp_sum(lambda ch: self.acc[pl.ds(2 * ch, 2)], mixed, self.tp_bufs)
        for part in self.parts:
            part.drain()


def project_kernel(gated, w_out, mixed, *scratch):
    greet(tp_partners() + req_partners())
    work = Project(gated, w_out, scratch)
    work.start()
    work.gather()
    work.total(mixed)


MOST = 32
HALF = INNER // 2
FAR = (2, 1, 3)


def save_scratch(room):
    return [
        pltpu.VMEM((2, 4 * room, STATE, HALF), BF16),
        pltpu.VMEM((2, 4 * room, STATE, HALF), BF16),
        pltpu.VMEM((2, 4 * room, STATE, HALF), BF16),
        pltpu.VMEM((2, 16 * room, HALF), BF16),
        pltpu.VMEM((2, 16 * room, HALF), BF16),
        pltpu.VMEM((2, 16 * room, HALF), BF16),
        pltpu.SemaphoreType.DMA((2, 2, 3, 2)),
        pltpu.SemaphoreType.DMA((2, 2, 3, 2)),
    ]


class Save:
    def __init__(self, counts, room, index, want, codes, source, scratch):
        self.counts, self.room = counts, room
        self.index, self.want = index, want
        self.codes, self.source = codes, source
        self.sent, self.got1, self.got2, self.side, self.side1, self.side2, self.ss, self.rs = (
            scratch
        )

    def clear(self):
        self.side1[...] = jnp.zeros_like(self.side1)
        self.side2[...] = jnp.zeros_like(self.side2)

    def hot(self, want, span):
        if self.room != MOST and span != self.source.shape[0]:
            row = lax.div(want, 4 * MOST) * (4 * self.room) + lax.rem(want, 4 * MOST)
            want = jnp.where(want >= 0, row, -1)
        lane = lax.broadcasted_iota(jnp.int32, (want.shape[0], span), 1)
        return jnp.where(lane == want, 1.0, 0.0).astype(BF16)

    def place_of(self, at):
        at = jnp.maximum(at, 0)
        return lax.div(at, MOST) * self.room + lax.rem(at, MOST)

    def buffers(self, n):
        return ((self.got1, self.side1), (self.got2, self.side2))[n]

    def axis(self, n, h):
        return h if n == 0 else 1 - h

    def rows(self, ref, h, block, each):
        count = each * self.room
        return lambda used: ref.at[h, pl.ds(pl.multiple_of(block * count, 16 if each > 1 else 4), used)]

    def used(self, n):
        return self.counts[n], -(-4 * self.counts[n] // 16) * 16

    def copies(self, n, h, k):
        d = FAR[k]
        here = req_place(self.axis(n, h))
        dest, dev = mod4(here + d), shift_req(self.axis(n, h), d)
        into, side_into = self.buffers(n)
        few, many = self.used(n)
        return [
            rcopy(
                self.rows(src, h, dest, each)(used), self.rows(dst, h, here, each)(used),
                self.ss.at[n, h, k, i], self.rs.at[n, h, k, i], dev,
            )
            for i, (src, dst, each, used) in enumerate(
                ((self.sent, into, 1, few), (self.side, side_into, 4, many))
            )
        ]

    def send(self, n):
        into, side_into = self.buffers(n)
        room, many = self.room, self.used(n)[1]
        for k, d in enumerate(FAR + (0,)):
            for h in range(2):
                dest = mod4(req_place(self.axis(n, h)) + d)
                keep, side_keep = (into, side_into) if d == 0 else (self.sent, self.side)

                def pack(m, carry):
                    at = self.index[(n * 2 + h) * 4 * MOST + dest * MOST + m]
                    if n == 0:
                        row = self.codes[jnp.maximum(at, 0), :, h * HALF : (h + 1) * HALF]
                    else:
                        row = self.got1[h, self.place_of(at)]
                    keep[h, dest * room + m] = row
                    return carry

                lax.fori_loop(0, self.counts[n], pack, 0)
                rows = self.source[:, h * HALF : (h + 1) * HALF] if n == 0 else self.side1[h]
                want = self.want[n][h, pl.ds(pl.multiple_of(dest * 4 * MOST, 128), many), :]
                block = pl.ds(pl.multiple_of(dest * 4 * room, 16), many)
                side_keep[h, block, :] = dot(self.hot(want, rows.shape[0]), rows).astype(BF16)
                if d != 0:
                    for copy in self.copies(n, h, k):
                        copy.start()

    def receive(self, n):
        into, side_into = self.buffers(n)
        few, many = self.used(n)
        for k, d in enumerate(FAR):
            for h in range(2):
                origin = mod4(req_place(self.axis(n, h)) - d)
                dev = shift_req(self.axis(n, h), d)
                for i, (ref, each, used) in enumerate(((into, 1, few), (side_into, 4, many))):
                    block = self.rows(ref, h, origin, each)(used)
                    rcopy(
                        block, block, self.ss.at[n, h, k, i], self.rs.at[n, h, k, i], dev
                    ).wait_recv()
        for k in range(3):
            for h in range(2):
                for copy in self.copies(n, h, k):
                    copy.wait_send()

    def place(self, out, windows, scale):
        base = 4 * 4 * MOST

        def one(s, carry):
            for h in range(2):
                at = self.index[base + h * SLOTS + s]
                row = self.got2[h, self.place_of(at)]
                out[s, :, h * HALF : (h + 1) * HALF] = jnp.where(at >= 0, row, jnp.zeros_like(row))
            return carry

        lax.fori_loop(0, SLOTS, one, 0)
        want = self.want[2]
        span = 16 * self.room
        for h in range(2):
            cols = slice(h * HALF, (h + 1) * HALF)
            for k, ref in enumerate(windows):
                ref[:, cols] = dot(self.hot(want[h, k], span), self.side2[h]).astype(BF16)
        scale[...] = dot(self.hot(want[0, 3], span), self.side2[0, :, :128]).astype(BF16)


def save_partners():
    return [shift_req(axis, d) for axis in (0, 1) for d in FAR]


def save_kernel(
    counts, index, want1, want2, want3, codes, source, out, win0, win1, win2, scale, *scratch
):
    work = Save(counts, MOST, index, (want1, want2, want3), codes, source, scratch)
    work.clear()
    greet(save_partners())
    work.send(0)
    work.receive(0)
    work.send(1)
    work.receive(1)
    work.place(out, (win0, win1, win2), scale)


def both_kernel(
    counts, index, want1, want2, want3, codes, source, gated, w_out,
    mixed, out, win0, win1, win2, scale, *scratch,
):
    cut = len(TP_SCRATCH) + len(BACK_SCRATCH)
    project = Project(gated, w_out, scratch[:cut])
    save = Save(counts, ROOM, index, (want1, want2, want3), codes, source, scratch[cut:])
    save.clear()
    greet(tp_partners() + save_partners())
    project.start()
    save.send(0)
    project.gather()
    save.receive(0)
    save.send(1)
    project.total(mixed)
    save.receive(1)
    save.place(out, (win0, win1, win2), scale)


ROOM = 28
SAVE_COUNTS = ((20, 24), (24, 26), (MOST, MOST))


def before(flags, keys):
    n = flags.shape[1]
    earlier = jnp.arange(n)[None, :] < jnp.arange(n)[:, None]
    same = earlier[None] & flags[:, None, :] & (keys[:, None, :] == keys[:, :, None])
    return jnp.sum(same.astype(jnp.int32), axis=2)


def chosen(mask, value):
    return jnp.sum(jnp.where(mask, value + 1, 0), axis=-1) - 1


def save_plan(finish, holder, slot_index, me):
    def events(a):
        return a.reshape(STEPS, 4, 4, ROWS).transpose(1, 2, 0, 3).reshape(4, 4, BROWS)

    fin, own, slot = events(finish) == 1, events(holder), events(slot_index)
    first, second, last, needs = [], [], [], []
    for h in range(2):
        if h == 1:
            fin, own, slot = (a.transpose(1, 0, 2) for a in (fin, own, slot))
        p_of = (lax.div(own, 4), lax.rem(own, 4))[h]
        q_of = (lax.rem(own, 4), lax.div(own, 4))[h]
        p_me = (lax.div(me, 4), lax.rem(me, 4))[h]
        q_me = (lax.rem(me, 4), lax.div(me, 4))[h]
        rank1 = before(fin.reshape(16, BROWS), p_of.reshape(16, BROWS)).reshape(4, 4, BROWS)
        by_q = [a.transpose(1, 0, 2).reshape(4, 4 * BROWS) for a in (fin, own)]
        rank2 = before(*by_q).reshape(4, 4, BROWS).transpose(1, 0, 2)
        needs.append((jnp.max(jnp.where(fin, rank1, 0)), jnp.max(jnp.where(fin, rank2, 0))))
        number = jnp.arange(4)[:, None, None]
        count = jnp.arange(MOST)[None, :, None]

        def mine(a):
            return lax.dynamic_slice(a, (p_me, q_me, 0), (1, 1, BROWS)).reshape(1, 1, BROWS)

        mask = mine(fin) & (mine(p_of) == number) & (mine(rank1) == count)
        first.append(chosen(mask, jnp.arange(BROWS)[None, None, :]))

        def column(a):
            return lax.dynamic_slice(a, (0, q_me, 0), (4, 1, BROWS)).reshape(1, 1, 4 * BROWS)

        at = jnp.arange(4)[:, None, None] * MOST + rank1
        mask = column(fin) & (column(p_of) == p_me) & (column(q_of) == number)
        second.append(chosen(mask & (column(rank2) == count), column(at)))
        at = jnp.arange(4)[None, :, None] * MOST + rank2
        mask = (fin & (own == me)).reshape(1, -1) & (
            slot.reshape(1, -1) == jnp.arange(SLOTS)[:, None]
        )
        last.append(chosen(mask, at.reshape(1, -1)))
    first, second, last = (jnp.stack(a) for a in (first, second, last))
    index = jnp.concatenate([first.reshape(-1), second.reshape(-1), last.reshape(-1)])
    kind = jnp.arange(4, dtype=jnp.int32)

    def column_of(base, value, axis):
        return jnp.where(jnp.expand_dims(base, axis) >= 0, value, -1)

    want1 = column_of(first, first[..., None] + kind * BROWS, -1).reshape(2, 16 * MOST, 1)
    want2 = column_of(second, second[..., None] * 4 + kind, -1).reshape(2, 16 * MOST, 1)
    want3 = column_of(last, last[:, None, :] * 4 + kind[:, None], 1).reshape(2, 4, SLOTS, 1)
    need1 = jnp.maximum(needs[0][0], needs[1][0]) + 1
    need2 = jnp.maximum(needs[0][1], needs[1][1]) + 1
    return index, want1, want2, want3, need1, need2


def per_device(
    tokens, finish, holder, slot_index, embedding, norm_gain, proj_inner, proj_gate, conv_weight,
    conv_bias, proj_low, proj_select, proj_dt, dt_bias, decay_log, skip_gain, proj_out, state_codes,
    state_scales, conv_state,
):
    me = lax.axis_index("req")
    ids = tokens.reshape(STEPS, BLOCKS, ROWS).transpose(1, 0, 2).reshape(BLOCKS, BROWS, 1)
    ids = ids - lax.axis_index("tp") * embedding.shape[0]
    index, want1, want2, want3, need1, need2 = save_plan(finish, holder, slot_index, me)
    conv = conv_state.transpose(1, 0, 2).reshape(3 * ROWS, INNER).astype(F32)
    scales = jnp.repeat(state_scales.astype(F32), PAGE, axis=1)
    shape = jax.ShapeDtypeStruct
    sums = vmem_call(
        front_kernel, shape((BROWS, 2 * INNER), F32), 5, TP_SCRATCH + list(FRONT_SCRATCH),
        collective_id=0, has_side_effects=True,
    )(ids, embedding, norm_gain.reshape(1, -1), proj_inner, proj_gate)
    half = BROWS // 2
    select_pad = jnp.pad(proj_select, ((0, 128 - 2 * STATE), (0, 0)))
    step, activ, select = vmem_call(
        rank_kernel,
        [shape((BROWS, INNER), F32), shape((BROWS, INNER), F32), shape((BROWS, 128), F32)],
        8,
        [
            pltpu.VMEM((2, half, RCOLS), F32),
            pltpu.VMEM((2, half, RCOLS), F32),
            pltpu.VMEM((half, RCOLS), BF16),
            pltpu.VMEM((3, half, RCOLS), BF16),
            pltpu.VMEM((2, half, RCOLS), F32),
            pltpu.SemaphoreType.DMA((5,)),
            pltpu.SemaphoreType.DMA((5,)),
        ],
        collective_id=1, has_side_effects=True,
    )(
        sums, conv, conv_weight, conv_bias.reshape(1, -1), proj_low, select_pad, proj_dt,
        dt_bias.reshape(1, -1),
    )
    vmem = pl.BlockSpec(memory_space=pltpu.VMEM)
    smem = pl.BlockSpec(memory_space=pltpu.SMEM)
    gated, final, new_codes, source = vmem_call(
        state_kernel,
        [
            shape((BROWS, INNER), BF16),
            shape((ROWS, STATE, INNER), BF16),
            shape((BROWS, STATE, INNER), BF16),
            shape((4 * BROWS, INNER), BF16),
        ],
        9,
        [
            pltpu.VMEM((BROWS, INNER), F32),
            pltpu.VMEM((BROWS, 128), F32),
            pltpu.VMEM((STATE, INNER), F32),
        ],
    )(
        state_codes, scales, step, activ, select, sums, conv, decay_log, skip_gain.reshape(1, -1),
    )
    saved = [shape((SLOTS, STATE, INNER), BF16)] + [shape((SLOTS, INNER), BF16)] * 3 + [
        shape((SLOTS, 128), BF16)
    ]
    mixed_shape = shape((BLOCKS, BROWS, FEATS), BF16)
    back_scratch = TP_SCRATCH + BACK_SCRATCH

    def call(kernel, results, operands, scratch, number):
        return pl.pallas_call(
            kernel,
            out_shape=results,
            in_specs=[smem] + [vmem] * (len(operands) - 1),
            out_specs=[vmem] * len(results),
            scratch_shapes=scratch,
            compiler_params=pltpu.CompilerParams(
                vmem_limit_bytes=VMEM_LIMIT, collective_id=number, has_side_effects=True
            ),
        )(*operands)

    def together(n):
        def run(*operands):
            return tuple(
                call(
                    functools.partial(both_kernel, SAVE_COUNTS[n]), [mixed_shape] + saved,
                    operands, back_scratch + save_scratch(ROOM), 3 + n,
                )
            )

        return run

    def apart(*operands):
        mixed = vmem_call(
            project_kernel, mixed_shape, 2, back_scratch, collective_id=2, has_side_effects=True
        )(*operands[6:])
        rest = call(
            functools.partial(save_kernel, SAVE_COUNTS[2]), saved, operands[:6],
            save_scratch(MOST), 5,
        )
        return tuple([mixed, *rest])

    tight = [(need1 <= a) & (need2 <= b) for a, b in SAVE_COUNTS[:2]]
    which = jnp.where(tight[0], 0, jnp.where(tight[1], 1, 2))
    mixed, cache_codes, win0, win1, win2, cache_scales = lax.switch(
        which, [together(0), together(1), apart], index, want1, want2, want3, new_codes, source,
        gated, proj_out,
    )
    mixed = mixed.reshape(BLOCKS, STEPS, ROWS, FEATS).transpose(1, 0, 2, 3)
    mixed = mixed.reshape(STEPS, BLOCKS * ROWS, FEATS)
    last = slice((STEPS - 1) * ROWS, BROWS)
    pages = INNER // PAGE
    next_scales = source[3 * BROWS :][last, :pages]
    next_window = jnp.stack([source[k * BROWS : (k + 1) * BROWS][last] for k in range(3)], axis=1)
    cache_window = jnp.stack([win0, win1, win2], axis=1)
    return (
        mixed, final, next_scales, next_window, cache_codes, cache_scales[:, :pages], cache_window,
    )


def solution(mesh):
    in_specs = (
        P(), P(), P(), P(), P("tp", "req"), P("req"), P("req", "tp"), P("req", "tp"),
        P(None, "tp"), P("tp"), P("tp", None), P(None, "tp"), P(None, "tp"), P("tp"),
        P(None, "tp"), P("tp"), P("tp", "req"), P("req", None, "tp"), P("req", "tp"),
        P("req", None, "tp"),
    )
    out_specs = (
        P(None, None, "req"), P("req", None, "tp"), P("req", "tp"), P("req", None, "tp"),
        P("req", None, "tp"), P("req", "tp"), P("req", None, "tp"),
    )
    return jax.shard_map(
        per_device, mesh=mesh, in_specs=in_specs, out_specs=out_specs, check_vma=False
    )
```

```python
import functools

import jax
import jax.numpy as jnp
from jax import lax
from jax.experimental import pallas as pl
from jax.experimental.pallas import tpu as pltpu
from jax.sharding import PartitionSpec as P

D = 8192
STATE = 16
PAGE = 128
STEPS = 4
CAP = 2
ROWS = 24
BLOCKS = 16
BROWS = STEPS * ROWS
SLOTS = 64
INNER = 2048
HALF = INNER // 2
FEATS = 512
WIDE = 512
RANK = 512
PAIRS = STEPS * CAP
F32 = jnp.float32
BF16 = jnp.bfloat16
MESH = pl.DeviceIdType.MESH
VMEM_LIMIT = 62 * 1024 * 1024


def rcopy(src, dst, send, recv, dev):
    return pltpu.make_async_remote_copy(
        src_ref=src, dst_ref=dst, send_sem=send, recv_sem=recv, device_id=dev, device_id_type=MESH
    )


def mod4(v):
    return lax.rem(v + 8, 4)


def dot(a, b):
    return jnp.dot(a, b, preferred_element_type=F32)


def greet(devices):
    barrier = pltpu.get_barrier_semaphore()
    for dev in devices:
        pl.semaphore_signal(barrier, inc=1, device_id=dev, device_id_type=MESH)
    pl.semaphore_wait(barrier, len(devices))


def tp_scratch(rows):
    return (
        [pltpu.VMEM((4, 2, rows, FEATS), BF16)] * 2
        + [pltpu.VMEM((4, 2, rows, FEATS), F32)]
        + [pltpu.VMEM((2, rows, FEATS), BF16)] * 6
        + [pltpu.SemaphoreType.DMA((20,)), pltpu.SemaphoreType.DMA((20,))]
    )


TP_SCRATCH = tp_scratch(BROWS)


def tp_partners():
    r, t = lax.axis_index("req"), lax.axis_index("tp")
    y, c = lax.div(t, 2), lax.rem(t, 2)
    return [(r, y * 2 + 1 - c), (r, mod4(y + 1) * 2 + c), (r, mod4(y - 1) * 2 + c)]


def tp_steps(get, total, bufs):
    half_s, half_r, part, far_s, far_r, dir_s, dir_r, com_s, com_r, ss, rs = bufs
    t = lax.axis_index("tp")
    y, c = lax.div(t, 2), lax.rem(t, 2)
    core, up, down = tp_partners()
    order = [mod4(y + 2), mod4(y + 1), mod4(y - 1), y]
    sent = []

    def send(src, dst, n, dev):
        copy = rcopy(src, dst, ss.at[n], rs.at[n], dev)
        copy.start()
        sent.append(copy)

    def arrived(ref, n):
        rcopy(ref, ref, ss.at[n], rs.at[n], core).wait_recv()

    def pair(group, yy):
        return pl.ds(2 * (group * 4 + yy), 2)

    for k in range(4):
        half_s[k] = get((1 - c) * 4 + order[k]).astype(BF16)
        send(half_s.at[k], half_r.at[k], k, core)
    for k in range(4):
        mine = get(c * 4 + order[k])
        arrived(half_r.at[k], k)
        part[k] = mine + half_r[k].astype(F32)
        if k == 0:
            far_s[...] = part[0].astype(BF16)
            send(far_s.at[0], far_r.at[0], 4, up)
            send(far_s.at[1], far_r.at[1], 5, down)
        if k == 1:
            dir_s[1] = part[1, 1].astype(BF16)
            send(dir_s.at[1], dir_r.at[1], 7, up)
        if k == 2:
            dir_s[0] = part[2, 0].astype(BF16)
            send(dir_s.at[0], dir_r.at[0], 6, down)
    yield
    arrived(far_r.at[0], 4)
    com_s[0] = (part[1, 0] + far_r[0].astype(F32)).astype(BF16)
    send(com_s.at[0], com_r.at[0], 8, up)
    arrived(far_r.at[1], 5)
    com_s[1] = (part[2, 1] + far_r[1].astype(F32)).astype(BF16)
    send(com_s.at[1], com_r.at[1], 9, down)
    own = 2 * (c * 4 + y)
    for h in range(2):
        arrived(dir_r.at[h], 6 + h)
        arrived(com_r.at[h], 8 + h)
        total[own + h] = (part[3, h] + dir_r[h].astype(F32) + com_r[h].astype(F32)).astype(BF16)
    mine = total.at[pair(c, y)]
    send(mine, mine, 10, up)
    send(mine, mine, 11, down)
    send(mine, mine, 12, core)
    below = total.at[pair(c, mod4(y - 1))]
    above = total.at[pair(c, mod4(y + 1))]
    arrived(below, 10)
    first = total.at[2 * (c * 4 + mod4(y - 1))]
    send(first, first, 13, up)
    send(below, below, 15, core)
    arrived(above, 11)
    second = total.at[2 * (c * 4 + mod4(y + 1)) + 1]
    send(second, second, 14, down)
    send(above, above, 16, core)
    far = 2 * (c * 4 + mod4(y + 2))
    arrived(total.at[far], 13)
    send(total.at[far], total.at[far], 17, core)
    arrived(total.at[far + 1], 14)
    send(total.at[far + 1], total.at[far + 1], 18, core)
    arrived(total.at[pair(1 - c, y)], 12)
    arrived(total.at[pair(1 - c, mod4(y - 1))], 15)
    arrived(total.at[pair(1 - c, mod4(y + 1))], 16)
    other = 2 * ((1 - c) * 4 + mod4(y + 2))
    arrived(total.at[other], 17)
    arrived(total.at[other + 1], 18)
    for copy in sent:
        copy.wait_send()
    yield


def tp_sum(get, total, bufs):
    for _ in tp_steps(get, total, bufs):
        pass


def shift_req(axis, d):
    r, t = lax.axis_index("req"), lax.axis_index("tp")
    x, z = lax.div(r, 4), lax.rem(r, 4)
    if axis == 0:
        return (mod4(x + d) * 4 + z, t)
    return (x * 4 + mod4(z + d), t)


def req_place(axis):
    r = lax.axis_index("req")
    return lax.div(r, 4) if axis == 0 else lax.rem(r, 4)


def req_partners():
    return [shift_req(axis, d) for axis in (0, 1) for d in (1, -1)]


PROWS = BROWS // 2
FRONT_SCRATCH = (
    [
        pltpu.VMEM((2, BLOCKS, PROWS, FEATS), BF16),
        pltpu.VMEM((2, 4, 4 * PROWS, FEATS), BF16),
        pltpu.VMEM((2, 4, 4 * PROWS, FEATS), BF16),
        pltpu.VMEM((2, 4, 4 * PROWS, PAGE), F32),
    ]
    + [pltpu.VMEM((2, 2, 4, 4 * PROWS, WIDE), BF16)] * 6
    + [pltpu.VMEM((2, 2, 4, PROWS, WIDE), BF16)] * 6
    + [pltpu.VMEM((2, 2, 4, 4, PROWS, WIDE), F32)]
    + [pltpu.SemaphoreType.DMA((2, 6, 2, 4)), pltpu.SemaphoreType.DMA((2, 6, 2, 4))]
    + [pltpu.VMEM((2, 4 * PROWS, PAGE), BF16)] * 6
    + [pltpu.VMEM((2, PROWS, PAGE), BF16)] * 6
    + [pltpu.VMEM((2, 4, PROWS, PAGE), F32)]
    + [pltpu.SemaphoreType.DMA((2, 6)), pltpu.SemaphoreType.DMA((2, 6))]
)


class ScatterSum:
    def __init__(self, axis, d, partial, bufs, total, ss, rs):
        self.axes = (axis, 1 - axis)
        self.d = d
        self.partial = partial
        self.far_s, self.far_r, self.dir_s, self.dir_r, self.com_s, self.com_r = bufs[:6]
        self.far2_s, self.far2_r, self.dir2_s, self.dir2_r, self.com2_s, self.com2_r = bufs[6:]
        self.total = total
        self.ss, self.rs = ss, rs

    def copy(self, n):
        src = (self.far_s, self.dir_s, self.com_s, self.far2_s, self.dir2_s, self.com2_s)[n]
        dst = (self.far_r, self.dir_r, self.com_r, self.far2_r, self.dir2_r, self.com2_r)[n]
        d = -self.d if n % 3 == 1 else self.d
        return rcopy(src, dst, self.ss(n), self.rs(n), shift_req(self.axes[n // 3], d))

    def far(self):
        p = req_place(self.axes[0])
        self.far_s[...] = self.partial(mod4(p + 2)).astype(BF16)
        self.copy(0).start()

    def direct(self):
        p = req_place(self.axes[0])
        self.dir_s[...] = self.partial(mod4(p - self.d)).astype(BF16)
        self.copy(1).start()

    def combined(self):
        p = req_place(self.axes[0])
        mine = self.partial(mod4(p + self.d))
        self.copy(0).wait_recv()
        self.com_s[...] = (mine + self.far_r[...].astype(F32)).astype(BF16)
        self.copy(2).start()

    def own(self):
        p, q = req_place(self.axes[0]), req_place(self.axes[1])
        mine = self.partial(p)
        self.copy(1).wait_recv()
        self.copy(2).wait_recv()
        mine = mine + self.dir_r[...].astype(F32) + self.com_r[...].astype(F32)
        self.total[...] = mine.reshape(4, PROWS, mine.shape[1])
        self.far2_s[...] = self.total[mod4(q + 2)].astype(BF16)
        self.copy(3).start()
        self.dir2_s[...] = self.total[mod4(q - self.d)].astype(BF16)
        self.copy(4).start()

    def combined2(self):
        q = req_place(self.axes[1])
        self.copy(3).wait_recv()
        self.com2_s[...] = (self.total[mod4(q + self.d)] + self.far2_r[...].astype(F32)).astype(
            BF16
        )
        self.copy(5).start()

    def result(self):
        q = req_place(self.axes[1])
        self.copy(4).wait_recv()
        self.copy(5).wait_recv()
        return self.total[q] + self.dir2_r[...].astype(F32) + self.com2_r[...].astype(F32)

    def drain(self):
        for n in range(6):
            self.copy(n).wait_send()


class Front:
    def __init__(self, g, refs, out, tp_bufs, rest):
        self.g, self.out, self.tp_bufs = g, out, tp_bufs
        self.ids, self.emb, self.gain, self.w_inner, self.w_gate = refs
        self.embedded, self.lhs_x, self.lhs_z, self.squares = (ref.at[g] for ref in rest[:4])
        self.big = [ref.at[g] for ref in rest[4:17]]
        self.big_ss, self.big_rs = rest[17:19]
        small = [ref.at[g] for ref in rest[19:32]]
        small_ss, small_rs = rest[32:34]
        self.norm = ScatterSum(
            0, 1, lambda chunk: self.squares[chunk], small[:12], small[12],
            lambda n: small_ss.at[g, n], lambda n: small_rs.at[g, n],
        )

    def looked(self, ch):
        emb = self.emb
        want = self.ids[self.g, pl.ds(2 * ch, 2)].reshape(2 * PROWS, 1)
        span = 1024
        acc = jnp.zeros((2 * PROWS, FEATS), F32)
        for k in range(emb.shape[0] // span):
            lane = lax.broadcasted_iota(jnp.int32, (2 * PROWS, span), 1) + k * span
            hot = jnp.where(lane == want, 1.0, 0.0).astype(BF16)
            acc = acc + dot(hot, emb[k * span : (k + 1) * span, :])
        return acc.reshape(2, PROWS, FEATS)

    def lookup(self):
        return tp_steps(self.looked, self.embedded, self.tp_bufs)

    def spread(self):
        def body(b, carry):
            x, z = lax.div(b, 4), lax.rem(b, 4)
            rows = self.embedded[b].astype(F32)
            scaled = (rows * self.gain[...]).astype(BF16)
            along_z = pl.ds(pl.multiple_of(z * PROWS, PROWS), PROWS)
            along_x = pl.ds(pl.multiple_of(x * PROWS, PROWS), PROWS)
            self.lhs_x[x, along_z, :] = scaled
            self.lhs_z[z, along_x, :] = scaled
            self.squares[x, along_z, :] = jnp.broadcast_to(
                jnp.sum(rows * rows, axis=1, keepdims=True), (PROWS, PAGE)
            )
            return carry

        lax.fori_loop(0, BLOCKS, body, 0)

    def unit(self, ab, u):
        lhs, weight = ((self.lhs_x, self.w_inner), (self.lhs_z, self.w_gate))[ab]
        g = self.g

        def partial(chunk):
            cols = pl.ds(pl.multiple_of(u * WIDE, WIDE), WIDE)
            return dot(lhs[chunk], weight[:, cols])

        views = [ref.at[ab, u] for ref in self.big[:12]]
        return ScatterSum(
            ab, 1 - 2 * lax.rem(u, 2), partial, views, self.big[12].at[ab, u],
            lambda n: self.big_ss.at[g, n, ab, u], lambda n: self.big_rs.at[g, n, ab, u],
        )

    def each(self, step):
        step(self.norm)

        def body(u, carry):
            for ab in range(2):
                step(self.unit(ab, u))
            return carry

        lax.fori_loop(0, 4, body, 0)

    def finish(self):
        inv_rms = lax.rsqrt(self.norm.result()[:, :1] / D + 1e-05)

        def body(u, carry):
            for ab in range(2):
                cols = pl.ds(pl.multiple_of((ab * 4 + u) * WIDE, WIDE), WIDE)
                rows = slice(self.g * PROWS, (self.g + 1) * PROWS)
                self.out[rows, cols] = self.unit(ab, u).result() * inv_rms
            return carry

        lax.fori_loop(0, 4, body, 0)


PLAN, FIRST, SECOND, LAST, SIDE1, SIDE2, WHICH = 24, 0, 4, 8, 9, 13, 17
GROUP = 4 * BROWS
MOST = 32


def make_plan(events, plan):
    r = lax.axis_index("req")
    shape = (GROUP, 128)
    lane = lax.broadcasted_iota(jnp.int32, shape, 1)
    number = lax.broadcasted_iota(jnp.int32, shape, 0)
    kind, quarter = lax.rem(lane, 4), lax.div(lane, 4)
    block = lax.div(number, BROWS)
    row = lax.broadcasted_iota(jnp.int32, (GROUP, GROUP), 0)
    col = lax.broadcasted_iota(jnp.int32, (GROUP, GROUP), 1)
    earlier = col < row
    near = earlier & (lax.div(col, BROWS) == lax.div(row, BROWS))
    earlier = jnp.where(earlier, 1.0, 0.0).astype(BF16)
    near = jnp.where(near, 1.0, 0.0).astype(BF16)

    def ahead(which, mask):
        return dot(which, jnp.where(mask, 1.0, 0.0).astype(BF16)).astype(jnp.int32)

    def parts(packed):
        packed = jnp.broadcast_to(packed, shape)
        owner = jnp.bitwise_and(jnp.right_shift(packed, 6), 15)
        return packed >= 4096, owner, jnp.bitwise_and(packed, 63)

    def fold(mask, value):
        return jnp.sum(jnp.where(mask, value + 1, 0), axis=0, keepdims=True) - 1

    plan[...] = jnp.zeros_like(plan)
    need1 = jnp.zeros((1, 128), jnp.int32)
    need2 = jnp.zeros((1, 128), jnp.int32)
    for h in range(2):
        p_me, q_me = req_place(h), req_place(1 - h)
        done, owner, _ = parts(events[h, q_me])
        p_of = lax.div(owner, 4) if h == 0 else lax.rem(owner, 4)
        q_of = lax.rem(owner, 4) if h == 0 else lax.div(owner, 4)
        mask1 = done & (p_of == lane)
        rank1 = ahead(near, mask1)
        mask2 = done & (p_of == p_me) & (q_of == lane)
        rank2 = ahead(earlier, mask2)
        here = jnp.sum(jnp.where(lane == p_me, rank1, 0), axis=1, keepdims=True)
        at = block * MOST + here
        mine = block == p_me
        event = number - p_me * BROWS
        base = PLAN * h
        for d in range(4):
            rank = jnp.broadcast_to(rank1[:, d : d + 1], shape)
            mask = mine & done & (p_of == d)
            plan[base + FIRST + d : base + FIRST + d + 1, :] = fold(mask & (rank == lane), event)
            plan[base + SIDE1 + d : base + SIDE1 + d + 1, :] = fold(
                mask & (rank == quarter), kind * BROWS + event
            )
            rank = jnp.broadcast_to(rank2[:, d : d + 1], shape)
            mask = done & (p_of == p_me) & (q_of == d)
            plan[base + SECOND + d : base + SECOND + d + 1, :] = fold(mask & (rank == lane), at)
            plan[base + SIDE2 + d : base + SIDE2 + d + 1, :] = fold(
                mask & (rank == quarter), at * 4 + kind
            )
        found = jnp.zeros((1, 128), jnp.int32)
        for q in range(4):
            done, owner, slot = parts(events[h, q])
            mask = done & (owner == r)
            value = q * MOST + ahead(earlier, mask)
            found = found + fold(mask & (slot == lane), value) + 1
            p_of = lax.div(owner, 4) if h == 0 else lax.rem(owner, 4)
            leaving = jnp.where(done & (p_of == lane), 1, 0).reshape(4, BROWS, 128)
            for n in range(4):
                need1 = jnp.maximum(need1, jnp.sum(leaving[n], axis=0, keepdims=True))
            staying = jnp.where(done & (owner == lane), 1, 0)
            need2 = jnp.maximum(need2, jnp.sum(staying, axis=0, keepdims=True))
        plan[base + LAST : base + LAST + 1, :] = found - 1
    need1 = jnp.max(need1, axis=1, keepdims=True)
    need2 = jnp.max(need2, axis=1, keepdims=True)
    which = jnp.full((1, 1), len(SAVE_COUNTS) - 1, jnp.int32)
    for n in range(len(SAVE_COUNTS) - 2, -1, -1):
        few, many = SAVE_COUNTS[n]
        which = jnp.where((need1 <= few) & (need2 <= many), n, which)
    plan[WHICH : WHICH + 1, :] = jnp.broadcast_to(which, (1, 128))


TP_PAIR = tp_scratch(PROWS)


def front_kernel(ids, emb, gain, w_inner, w_gate, events, out, plan, *scratch):
    cut = len(TP_PAIR)
    refs = (ids, emb, gain, w_inner, w_gate)
    one, two = (
        Front(g, refs, out, scratch[g * cut : (g + 1) * cut], scratch[2 * cut :]) for g in range(2)
    )
    greet(tp_partners() + req_partners())
    for _ in one.lookup():
        pass
    one.spread()
    one.each(lambda s: s.far())
    one.each(lambda s: s.direct())
    lookup = two.lookup()
    next(lookup)
    one.each(lambda s: s.combined())
    next(lookup)
    two.spread()
    two.each(lambda s: s.far())
    one.each(lambda s: s.own())
    two.each(lambda s: s.direct())
    one.each(lambda s: s.combined2())
    make_plan(events, plan)
    two.each(lambda s: s.combined())
    one.finish()
    two.each(lambda s: s.own())
    two.each(lambda s: s.combined2())
    two.finish()
    one.each(lambda s: s.drain())
    two.each(lambda s: s.drain())


def vmem_call(kernel, out_shape, n_in, scratch, **params):
    spec = pl.BlockSpec(memory_space=pltpu.VMEM)
    return pl.pallas_call(
        kernel,
        out_shape=out_shape,
        in_specs=[spec] * n_in,
        out_specs=jax.tree.map(lambda _: spec, out_shape),
        scratch_shapes=scratch,
        compiler_params=pltpu.CompilerParams(vmem_limit_bytes=VMEM_LIMIT, **params),
    )


def silu(v):
    return v / (1.0 + jnp.exp(-v))


RCOLS = RANK + 128


def rank_kernel(
    sums, conv, taps, bias, w_low, w_select, w_dt, dt_bias, step, activ, select,
    pair_s, pair_r, quad_s, quad_r, full, ss, rs,
):
    r, t = lax.axis_index("req"), lax.axis_index("tp")
    y, c = lax.div(t, 2), lax.rem(t, 2)
    core = (r, y * 2 + 1 - c)
    others = [(r, mod4(y + d) * 2 + c) for d in (1, 2, 3)]
    greet([core] + others)
    for n in range(STEPS):
        total = bias[...] + jnp.zeros((ROWS, INNER), F32)
        for k in range(4):
            at = n + k
            if at < 3:
                row = conv[at].astype(F32)
            else:
                row = sums[(at - 3) * ROWS : (at - 2) * ROWS, :INNER].astype(BF16).astype(F32)
            total = total + row * taps[k : k + 1, :]
        activ[n * ROWS : (n + 1) * ROWS, :] = silu(total).astype(BF16).astype(F32)
    act = activ[...].astype(BF16)
    low = dot(act, w_low[...]).reshape(2, BROWS // 2, RANK)
    sel = lax.dot_general(
        act, w_select[...], (((1,), (1,)), ((), ())), preferred_element_type=F32
    )
    sel = jnp.concatenate([sel, jnp.zeros((BROWS, 128 - 2 * STATE), F32)], axis=1)
    sel = sel.reshape(2, BROWS // 2, 128)
    pair_s[:, :, :RANK] = low
    pair_s[:, :, RANK:] = sel
    swap = rcopy(pair_s, pair_r, ss.at[0], rs.at[0], core)
    swap.start()
    swap.wait_recv()
    chip = pair_s[c] + pair_r[c]
    quad_s[...] = chip.astype(BF16)
    copies = [rcopy(quad_s, quad_r.at[n], ss.at[1 + n], rs.at[1 + n], others[n]) for n in range(3)]
    for copy in copies:
        copy.start()
    acc = quad_s[...].astype(F32)
    for n in range(3):
        copies[n].wait_recv()
        acc = acc + quad_r[n].astype(F32)
    full[c] = acc
    back = rcopy(full.at[c], full.at[c], ss.at[4], rs.at[4], core)
    back.start()
    rcopy(full.at[1 - c], full.at[1 - c], ss.at[4], rs.at[4], core).wait_recv()
    low_rank = full[:, :, :RANK].reshape(BROWS, RANK).astype(BF16)
    select[...] = full[:, :, RANK:].reshape(BROWS, 128)
    v = dot(low_rank, w_dt[...]) + dt_bias[...]
    step[...] = jnp.maximum(v, 0.0) + jnp.log1p(jnp.exp(-jnp.abs(v)))
    swap.wait_send()
    for copy in copies:
        copy.wait_send()
    back.wait_send()


def state_kernel(
    codes, scales, step, activ, select, sums, conv, decay_log, skip,
    gated, final, new_codes, source, last_window, output, scale_rows, rates,
):
    lane = lax.broadcasted_iota(jnp.int32, (STATE, 128), 1)
    row_of = lax.broadcasted_iota(jnp.int32, (STATE, 128), 0)
    page_lane = lax.broadcasted_iota(jnp.int32, (1, 128), 1)
    width = 4 * PAGE

    def request(i, carry):
        b_in, c_out = [], []
        for n in range(STEPS):
            row = select[pl.ds(n * ROWS + i, 1), :]
            b_in.append(jnp.sum(jnp.where(lane == row_of, row, 0.0), axis=1, keepdims=True))
            c_out.append(
                jnp.sum(jnp.where(lane == row_of + STATE, row, 0.0), axis=1, keepdims=True)
            )
        kept = [jnp.zeros((1, 128), F32) for _ in range(STEPS)]
        for part in range(INNER // width):
            cols = slice(part * width, (part + 1) * width)
            rate = rates[:, cols]
            current = codes[i, :, cols].astype(F32) * scales[pl.ds(i, 1), cols]
            for n in range(STEPS):
                at = n * ROWS + i
                dt = step[pl.ds(at, 1), cols]
                act = activ[pl.ds(at, 1), cols]
                current = jnp.exp2(dt * rate) * current + (dt * act) * b_in[n]
                output[pl.ds(at, 1), cols] = jnp.sum(current * c_out[n], axis=0, keepdims=True)
                peak = jnp.max(jnp.abs(current), axis=0, keepdims=True)
                for page in range(4):
                    here = slice(page * PAGE, (page + 1) * PAGE)
                    top = jnp.max(peak[:, here], axis=1, keepdims=True)
                    scale = (top + 1e-06).astype(BF16).astype(F32)
                    kept[n] = jnp.where(page_lane == part * 4 + page, scale, kept[n])
                    new_codes[at, :, part * width + page * PAGE : part * width + (page + 1) * PAGE] = (
                        current[:, here] * (1.0 / scale)
                    ).astype(BF16)
        for n in range(STEPS):
            scale_rows[pl.ds(n * ROWS + i, 1), :] = kept[n]
        final[i] = new_codes[(STEPS - 1) * ROWS + i]
        return carry

    rates[...] = -jnp.exp(decay_log[...]) * 1.4426950408889634
    lax.fori_loop(0, ROWS, request, 0)
    gated[...] = (
        (output[...] + skip[...] * activ[...]) * silu(sums[:, INNER:])
    ).astype(BF16)
    rows = [conv[k].astype(F32) for k in range(3)]
    rows += [sums[n * ROWS : (n + 1) * ROWS, :INNER] for n in range(STEPS)]
    for k in range(3):
        source[k * BROWS : (k + 1) * BROWS, :] = jnp.concatenate(
            rows[k + 1 : k + 1 + STEPS], axis=0
        ).astype(BF16)
        last_window[k] = rows[STEPS + k].astype(BF16)
    source[3 * BROWS :, :] = jnp.zeros((BROWS, INNER), BF16)
    source[3 * BROWS :, :128] = scale_rows[...].astype(BF16)


def middle_kernel(
    sums, conv, taps, bias, w_low, w_select, w_dt, dt_bias, codes, scales, decay_log, skip,
    gated, final, new_codes, source, last_window, step, activ, select, output, scale_rows, rates,
    *rest,
):
    rank_kernel(
        sums, conv, taps, bias, w_low, w_select, w_dt, dt_bias, step, activ, select, *rest
    )
    state_kernel(
        codes, scales, step, activ, select, sums, conv, decay_log, skip,
        gated, final, new_codes, source, last_window, output, scale_rows, rates,
    )


BACK_SCRATCH = [
    pltpu.VMEM((BLOCKS, BROWS, INNER // 2), BF16),
    pltpu.VMEM((BLOCKS, BROWS, INNER // 2), BF16),
    pltpu.VMEM((BLOCKS, BROWS, FEATS), F32),
    pltpu.SemaphoreType.DMA((2, 16)),
    pltpu.SemaphoreType.DMA((2, 16)),
]


class Gather:
    def __init__(self, axis, buf, ss, rs):
        self.axes = (axis, 1 - axis)
        self.buf, self.ss, self.rs = buf, ss, rs
        self.q, self.p = req_place(axis), req_place(1 - axis)
        self.order = [self.q, mod4(self.q - 1), mod4(self.q + 1), mod4(self.q + 2)]
        self.sent = []

    def send(self, ref, n, axis, d):
        copy = rcopy(ref, ref, self.ss.at[n], self.rs.at[n], shift_req(axis, d))
        copy.start()
        self.sent.append(copy)

    def arrived(self, ref, n):
        rcopy(ref, ref, self.ss.at[n], self.rs.at[n], shift_req(self.axes[0], 1)).wait_recv()

    def block(self, p, q):
        return self.buf.at[p * 4 + q]

    def rows(self, p, q, h):
        return self.buf.at[p * 4 + q, pl.ds(h * (BROWS // 2), BROWS // 2)]

    def start(self):
        mine = self.block(self.p, self.q)
        self.send(mine, 0, self.axes[0], 1)
        self.send(mine, 1, self.axes[0], -1)
        self.spread(0)

    def spread(self, k):
        block = self.block(self.p, self.order[k])
        self.send(block, 4 + k, self.axes[1], 1)
        self.send(block, 8 + k, self.axes[1], -1)

    def near(self):
        self.arrived(self.block(self.p, self.order[1]), 0)
        self.send(self.rows(self.p, self.order[1], 0), 2, self.axes[0], 1)
        self.spread(1)
        self.arrived(self.block(self.p, self.order[2]), 1)
        self.send(self.rows(self.p, self.order[2], 1), 3, self.axes[0], -1)
        self.spread(2)

    def last(self):
        self.arrived(self.rows(self.p, self.order[3], 0), 2)
        self.arrived(self.rows(self.p, self.order[3], 1), 3)
        self.spread(3)

    def relay(self, k):
        below, above = mod4(self.p - 1), mod4(self.p + 1)
        self.arrived(self.block(below, self.order[k]), 4 + k)
        if k < 2:
            self.send(self.block(below, self.order[k]), 12 + k, self.axes[1], 1)
        self.arrived(self.block(above, self.order[k]), 8 + k)
        if k >= 2:
            self.send(self.block(above, self.order[k]), 12 + k, self.axes[1], -1)

    def end(self, k):
        self.arrived(self.block(mod4(self.p + 2), self.order[k]), 12 + k)

    def drain(self):
        for copy in self.sent:
            copy.wait_send()


class Project:
    def __init__(self, gated, w_out, scratch):
        self.tp_bufs, rest = scratch[: len(TP_SCRATCH)], scratch[len(TP_SCRATCH) :]
        self.buf_a, self.buf_b, self.acc, gss, grs = rest
        self.gated, self.w_out = gated, w_out
        self.parts = [
            Gather(1, self.buf_a, gss.at[0], grs.at[0]),
            Gather(0, self.buf_b, gss.at[1], grs.at[1]),
        ]

    def start(self):
        r = lax.axis_index("req")
        self.acc[...] = jnp.zeros_like(self.acc)
        self.buf_a[r] = self.gated[:, :HALF]
        self.buf_b[lax.rem(r, 4) * 4 + lax.div(r, 4)] = self.gated[:, HALF:]
        for part in self.parts:
            part.start()

    def project(self, n, p, k):
        q = self.parts[n].order[k]
        if n == 0:
            self.acc[p * 4 + q] += dot(self.buf_a[p * 4 + q], self.w_out[:HALF, :])
        else:
            self.acc[q * 4 + p] += dot(self.buf_b[p * 4 + q], self.w_out[HALF:, :])

    def gather(self):
        parts = self.parts
        for part in parts:
            part.near()
        for part in parts:
            part.last()
        for k in range(4):
            for n in range(2):
                self.project(n, parts[n].p, k)
        for k in range(4):
            for part in parts:
                part.relay(k)
            for n in range(2):
                self.project(n, mod4(parts[n].p - 1), k)
                self.project(n, mod4(parts[n].p + 1), k)
        for k in range(4):
            for n in range(2):
                parts[n].end(k)
                self.project(n, mod4(parts[n].p + 2), k)

    def total(self, mixed):
        tp_sum(lambda ch: self.acc[pl.ds(2 * ch, 2)], mixed, self.tp_bufs)
        for part in self.parts:
            part.drain()


def project_kernel(gated, w_out, mixed, *scratch):
    greet(tp_partners() + req_partners())
    work = Project(gated, w_out, scratch)
    work.start()
    work.gather()
    work.total(mixed)


FAR = (2, 1, 3)


def save_scratch(room):
    return [
        pltpu.VMEM((2, 4 * room, STATE, HALF), BF16),
        pltpu.VMEM((2, 4 * room, STATE, HALF), BF16),
        pltpu.VMEM((2, 4 * room, STATE, HALF), BF16),
        pltpu.VMEM((2, 16 * room, HALF), BF16),
        pltpu.VMEM((2, 16 * room, HALF), BF16),
        pltpu.VMEM((2, 16 * room, HALF), BF16),
        pltpu.SemaphoreType.DMA((2, 2, 3, 2)),
        pltpu.SemaphoreType.DMA((2, 2, 3, 2)),
    ]


class Save:
    def __init__(self, counts, room, index, plan, codes, source, scratch):
        self.counts, self.room = counts, room
        self.index, self.plan = index, plan
        self.codes, self.source = codes, source
        self.sent, self.got1, self.got2, self.side, self.side1, self.side2, self.ss, self.rs = (
            scratch
        )

    def clear(self):
        self.side1[...] = jnp.zeros_like(self.side1)
        self.side2[...] = jnp.zeros_like(self.side2)

    def pick(self, want, rows):
        span = rows.shape[0]
        if self.room != MOST and span != self.source.shape[0]:
            row = lax.div(want, 4 * MOST) * (4 * self.room) + lax.rem(want, 4 * MOST)
            want = jnp.where(want >= 0, row, -1)
        number = lax.broadcasted_iota(jnp.int32, (span, 128), 0)
        hot = jnp.where(number == want, 1.0, 0.0).astype(BF16)
        picked = lax.dot_general(hot, rows, (((0,), (0,)), ((), ())), preferred_element_type=F32)
        return picked.astype(BF16)

    def place_of(self, at):
        at = jnp.maximum(at, 0)
        return lax.div(at, MOST) * self.room + lax.rem(at, MOST)

    def buffers(self, n):
        return ((self.got1, self.side1), (self.got2, self.side2))[n]

    def axis(self, n, h):
        return h if n == 0 else 1 - h

    def rows(self, ref, h, block, each):
        count = each * self.room
        return lambda used: ref.at[h, pl.ds(pl.multiple_of(block * count, 16 if each > 1 else 4), used)]

    def used(self, n):
        return self.counts[n], -(-4 * self.counts[n] // 16) * 16

    def copy(self, n, h, k, i):
        d = FAR[k]
        here = req_place(self.axis(n, h))
        dest, dev = mod4(here + d), shift_req(self.axis(n, h), d)
        src, dst = ((self.sent, self.side)[i], self.buffers(n)[i])
        each, used = (1, 4)[i], self.used(n)[i]
        return rcopy(
            self.rows(src, h, dest, each)(used), self.rows(dst, h, here, each)(used),
            self.ss.at[n, h, k, i], self.rs.at[n, h, k, i], dev,
        )

    def send(self, n):
        into, side_into = self.buffers(n)
        room, many = self.room, self.used(n)[1]
        order = [(k, d, h) for k, d in enumerate(FAR + (0,)) for h in range(2)]
        for k, d, h in order:
            dest = mod4(req_place(self.axis(n, h)) + d)
            keep = into if d == 0 else self.sent

            def pack(m, carry):
                at = self.index[PLAN * h + (FIRST, SECOND)[n] + dest, m]
                if n == 0:
                    row = self.codes[jnp.maximum(at, 0), :, h * HALF : (h + 1) * HALF]
                else:
                    row = self.got1[h, self.place_of(at)]
                keep[h, dest * room + m] = row
                return carry

            lax.fori_loop(0, self.counts[n], pack, 0)
            if d != 0:
                self.copy(n, h, k, 0).start()
        for k, d, h in order:
            dest = mod4(req_place(self.axis(n, h)) + d)
            keep = side_into if d == 0 else self.side
            rows = self.source[:, h * HALF : (h + 1) * HALF] if n == 0 else self.side1[h]
            want = self.plan[pl.ds(PLAN * h + (SIDE1, SIDE2)[n] + dest, 1), :]
            block = pl.ds(pl.multiple_of(dest * 4 * room, 16), many)
            keep[h, block, :] = self.pick(want, rows)[:many]
            if d != 0:
                self.copy(n, h, k, 1).start()

    def receive(self, n):
        into, side_into = self.buffers(n)
        few, many = self.used(n)
        for k, d in enumerate(FAR):
            for h in range(2):
                origin = mod4(req_place(self.axis(n, h)) - d)
                dev = shift_req(self.axis(n, h), d)
                for i, (ref, each, used) in enumerate(((into, 1, few), (side_into, 4, many))):
                    block = self.rows(ref, h, origin, each)(used)
                    rcopy(
                        block, block, self.ss.at[n, h, k, i], self.rs.at[n, h, k, i], dev
                    ).wait_recv()
        for k in range(3):
            for h in range(2):
                for i in range(2):
                    self.copy(n, h, k, i).wait_send()

    def place(self, out, windows, scale):
        def one(s, carry):
            for h in range(2):
                at = self.index[PLAN * h + LAST, s]
                row = self.got2[h, self.place_of(at)]
                out[s, :, h * HALF : (h + 1) * HALF] = jnp.where(at >= 0, row, jnp.zeros_like(row))
            return carry

        lax.fori_loop(0, SLOTS, one, 0)
        for h in range(2):
            at = self.plan[PLAN * h + LAST : PLAN * h + LAST + 1, :]
            for k in range(3):
                want = jnp.where(at >= 0, at * 4 + k, -1)
                windows[k, :, h * HALF : (h + 1) * HALF] = self.pick(want, self.side2[h])[:SLOTS]
            if h == 0:
                want = jnp.where(at >= 0, at * 4 + 3, -1)
                scale[...] = self.pick(want, self.side2[0, :, :128])[:SLOTS]


def save_partners():
    return [shift_req(axis, d) for axis in (0, 1) for d in FAR]


def save_kernel(
    counts, index, plan, codes, source, out, windows, scale, *scratch
):
    work = Save(counts, MOST, index, plan, codes, source, scratch)
    work.clear()
    greet(save_partners())
    work.send(0)
    work.receive(0)
    work.send(1)
    work.receive(1)
    work.place(out, windows, scale)


def both_kernel(
    counts, index, plan, codes, source, gated, w_out, mixed, out, windows, scale, *scratch,
):
    cut = len(TP_SCRATCH) + len(BACK_SCRATCH)
    project = Project(gated, w_out, scratch[:cut])
    save = Save(counts, ROOM, index, plan, codes, source, scratch[cut:])
    save.clear()
    greet(tp_partners() + save_partners())
    project.start()
    save.send(0)
    project.gather()
    save.receive(0)
    save.send(1)
    project.total(mixed)
    save.receive(1)
    save.place(out, windows, scale)


ROOM = 28
SAVE_COUNTS = ((20, 24), (24, 26), (MOST, MOST))


def pack_events(finish, holder, slot_index):
    packed = finish * 4096 + jnp.bitwise_and(holder, 15) * 64 + jnp.bitwise_and(slot_index, 63)
    packed = packed.reshape(STEPS, 4, 4, ROWS).transpose(2, 1, 0, 3)
    both = jnp.stack([packed, packed.transpose(1, 0, 2, 3)])
    return both.reshape(2, 4, GROUP, 1)


def per_device(
    tokens, finish, holder, slot_index, embedding, norm_gain, proj_inner, proj_gate, conv_weight,
    conv_bias, proj_low, proj_select, proj_dt, dt_bias, decay_log, skip_gain, proj_out, state_codes,
    state_scales, conv_state,
):
    ids = tokens.reshape(2, 2, BLOCKS, ROWS).transpose(0, 2, 1, 3).reshape(2, BLOCKS, PROWS, 1)
    ids = ids - lax.axis_index("tp") * embedding.shape[0]
    conv = conv_state.transpose(1, 0, 2)
    scales = jnp.repeat(state_scales.astype(F32), PAGE, axis=1)
    shape = jax.ShapeDtypeStruct
    sums, plan = vmem_call(
        front_kernel,
        [shape((BROWS, 2 * INNER), F32), shape((2 * PLAN, 128), jnp.int32)], 6, TP_PAIR * 2 + list(FRONT_SCRATCH),
        collective_id=0, has_side_effects=True,
    )(
        ids, embedding, norm_gain.reshape(1, -1), proj_inner, proj_gate,
        pack_events(finish, holder, slot_index),
    )
    half = BROWS // 2
    vmem = pl.BlockSpec(memory_space=pltpu.VMEM)
    smem = pl.BlockSpec(memory_space=pltpu.SMEM)
    gated, final, new_codes, source, last_window = vmem_call(
        middle_kernel,
        [
            shape((BROWS, INNER), BF16),
            shape((ROWS, STATE, INNER), BF16),
            shape((BROWS, STATE, INNER), BF16),
            shape((4 * BROWS, INNER), BF16),
            shape((3, ROWS, INNER), BF16),
        ],
        12,
        [
            pltpu.VMEM((BROWS, INNER), F32),
            pltpu.VMEM((BROWS, INNER), F32),
            pltpu.VMEM((BROWS, 128), F32),
            pltpu.VMEM((BROWS, INNER), F32),
            pltpu.VMEM((BROWS, 128), F32),
            pltpu.VMEM((STATE, INNER), F32),
            pltpu.VMEM((2, half, RCOLS), F32),
            pltpu.VMEM((2, half, RCOLS), F32),
            pltpu.VMEM((half, RCOLS), BF16),
            pltpu.VMEM((3, half, RCOLS), BF16),
            pltpu.VMEM((2, half, RCOLS), F32),
            pltpu.SemaphoreType.DMA((5,)),
            pltpu.SemaphoreType.DMA((5,)),
        ],
        collective_id=1, has_side_effects=True,
    )(
        sums, conv, conv_weight, conv_bias.reshape(1, -1), proj_low, proj_select, proj_dt,
        dt_bias.reshape(1, -1), state_codes, scales, decay_log, skip_gain.reshape(1, -1),
    )
    saved = [shape((SLOTS, STATE, INNER), BF16)] + [shape((3, SLOTS, INNER), BF16)] + [
        shape((SLOTS, 128), BF16)
    ]
    mixed_shape = shape((BLOCKS, BROWS, FEATS), BF16)
    back_scratch = TP_SCRATCH + BACK_SCRATCH

    def call(kernel, results, operands, scratch, number):
        return pl.pallas_call(
            kernel,
            out_shape=results,
            in_specs=[smem] + [vmem] * (len(operands) - 1),
            out_specs=[vmem] * len(results),
            scratch_shapes=scratch,
            compiler_params=pltpu.CompilerParams(
                vmem_limit_bytes=VMEM_LIMIT, collective_id=number, has_side_effects=True
            ),
        )(*operands)

    def together(n):
        def run(*operands):
            return tuple(
                call(
                    functools.partial(both_kernel, SAVE_COUNTS[n]), [mixed_shape] + saved,
                    operands, back_scratch + save_scratch(ROOM), 3 + n,
                )
            )

        return run

    def apart(*operands):
        mixed = vmem_call(
            project_kernel, mixed_shape, 2, back_scratch, collective_id=2, has_side_effects=True
        )(*operands[4:])
        rest = call(
            functools.partial(save_kernel, SAVE_COUNTS[2]), saved, operands[:4],
            save_scratch(MOST), 5,
        )
        return tuple([mixed, *rest])

    mixed, cache_codes, windows, cache_scales = lax.switch(
        plan[WHICH, 0], [together(0), together(1), apart], plan, plan, new_codes, source, gated, proj_out,
    )
    mixed = mixed.reshape(BLOCKS, STEPS, ROWS, FEATS).transpose(1, 0, 2, 3)
    mixed = mixed.reshape(STEPS, BLOCKS * ROWS, FEATS)
    last = slice((STEPS - 1) * ROWS, BROWS)
    pages = INNER // PAGE
    next_scales = source[3 * BROWS :][last, :pages]
    next_window = last_window.transpose(1, 0, 2)
    cache_window = windows.transpose(1, 0, 2)
    return (
        mixed, final, next_scales, next_window, cache_codes, cache_scales[:, :pages], cache_window,
    )


def solution(mesh):
    in_specs = (
        P(), P(), P(), P(), P("tp", "req"), P("req"), P("req", "tp"), P("req", "tp"),
        P(None, "tp"), P("tp"), P("tp", None), P(None, "tp"), P(None, "tp"), P("tp"),
        P(None, "tp"), P("tp"), P("tp", "req"), P("req", None, "tp"), P("req", "tp"),
        P("req", None, "tp"),
    )
    out_specs = (
        P(None, None, "req"), P("req", None, "tp"), P("req", "tp"), P("req", None, "tp"),
        P("req", None, "tp"), P("req", "tp"), P("req", None, "tp"),
    )
    return jax.shard_map(
        per_device, mesh=mesh, in_specs=in_specs, out_specs=out_specs, check_vma=False
    )
```

```python
import functools

import jax
import jax.numpy as jnp
from jax import lax
from jax.experimental import pallas as pl
from jax.experimental.pallas import tpu as pltpu
from jax.sharding import PartitionSpec as P

D = 8192
STATE = 16
PAGE = 128
STEPS = 4
CAP = 2
ROWS = 24
BLOCKS = 16
BROWS = STEPS * ROWS
SLOTS = 64
INNER = 2048
HALF = INNER // 2
FEATS = 512
WIDE = 512
RANK = 512
PAIRS = STEPS * CAP
F32 = jnp.float32
BF16 = jnp.bfloat16
MESH = pl.DeviceIdType.MESH
VMEM_LIMIT = 62 * 1024 * 1024


def rcopy(src, dst, send, recv, dev):
    return pltpu.make_async_remote_copy(
        src_ref=src, dst_ref=dst, send_sem=send, recv_sem=recv, device_id=dev, device_id_type=MESH
    )


def mod4(v):
    return lax.rem(v + 8, 4)


def dot(a, b):
    return jnp.dot(a, b, preferred_element_type=F32)


def greet(devices):
    barrier = pltpu.get_barrier_semaphore()
    for dev in devices:
        pl.semaphore_signal(barrier, inc=1, device_id=dev, device_id_type=MESH)
    pl.semaphore_wait(barrier, len(devices))


def tp_scratch(rows):
    return (
        [pltpu.VMEM((4, 2, rows, FEATS), BF16)] * 2
        + [pltpu.VMEM((4, 2, rows, FEATS), F32)]
        + [pltpu.VMEM((2, rows, FEATS), BF16)] * 6
        + [pltpu.SemaphoreType.DMA((20,)), pltpu.SemaphoreType.DMA((20,))]
    )


TP_SCRATCH = tp_scratch(BROWS)


def tp_partners():
    r, t = lax.axis_index("req"), lax.axis_index("tp")
    y, c = lax.div(t, 2), lax.rem(t, 2)
    return [(r, y * 2 + 1 - c), (r, mod4(y + 1) * 2 + c), (r, mod4(y - 1) * 2 + c)]


def tp_steps(get_all, total, bufs):
    half_s, half_r, part, far_s, far_r, dir_s, dir_r, com_s, com_r, ss, rs = bufs
    t = lax.axis_index("tp")
    y, c = lax.div(t, 2), lax.rem(t, 2)
    core, up, down = tp_partners()
    order = [mod4(y + 2), mod4(y + 1), mod4(y - 1), y]
    sent = []

    def send(src, dst, n, dev):
        copy = rcopy(src, dst, ss.at[n], rs.at[n], dev)
        copy.start()
        sent.append(copy)

    def arrived(ref, n):
        rcopy(ref, ref, ss.at[n], rs.at[n], core).wait_recv()

    def pair(group, yy):
        return pl.ds(2 * (group * 4 + yy), 2)

    get_all([(1 - c) * 4 + yy for yy in order], half_s)
    for k in range(4):
        send(half_s.at[k], half_r.at[k], k, core)
    get_all([c * 4 + yy for yy in order], part)
    for k in range(4):
        arrived(half_r.at[k], k)
        part[k] = part[k] + half_r[k].astype(F32)
        if k == 0:
            far_s[...] = part[0].astype(BF16)
            send(far_s.at[0], far_r.at[0], 4, up)
            send(far_s.at[1], far_r.at[1], 5, down)
        if k == 1:
            dir_s[1] = part[1, 1].astype(BF16)
            send(dir_s.at[1], dir_r.at[1], 7, up)
        if k == 2:
            dir_s[0] = part[2, 0].astype(BF16)
            send(dir_s.at[0], dir_r.at[0], 6, down)
    yield
    arrived(far_r.at[0], 4)
    com_s[0] = (part[1, 0] + far_r[0].astype(F32)).astype(BF16)
    send(com_s.at[0], com_r.at[0], 8, up)
    arrived(far_r.at[1], 5)
    com_s[1] = (part[2, 1] + far_r[1].astype(F32)).astype(BF16)
    send(com_s.at[1], com_r.at[1], 9, down)
    own = 2 * (c * 4 + y)
    for h in range(2):
        arrived(dir_r.at[h], 6 + h)
        arrived(com_r.at[h], 8 + h)
        total[own + h] = (part[3, h] + dir_r[h].astype(F32) + com_r[h].astype(F32)).astype(BF16)
    mine = total.at[pair(c, y)]
    send(mine, mine, 10, up)
    send(mine, mine, 11, down)
    send(mine, mine, 12, core)
    below = total.at[pair(c, mod4(y - 1))]
    above = total.at[pair(c, mod4(y + 1))]
    arrived(below, 10)
    first = total.at[2 * (c * 4 + mod4(y - 1))]
    send(first, first, 13, up)
    send(below, below, 15, core)
    arrived(above, 11)
    second = total.at[2 * (c * 4 + mod4(y + 1)) + 1]
    send(second, second, 14, down)
    send(above, above, 16, core)
    far = 2 * (c * 4 + mod4(y + 2))
    arrived(total.at[far], 13)
    send(total.at[far], total.at[far], 17, core)
    arrived(total.at[far + 1], 14)
    send(total.at[far + 1], total.at[far + 1], 18, core)
    arrived(total.at[pair(1 - c, y)], 12)
    arrived(total.at[pair(1 - c, mod4(y - 1))], 15)
    arrived(total.at[pair(1 - c, mod4(y + 1))], 16)
    other = 2 * ((1 - c) * 4 + mod4(y + 2))
    arrived(total.at[other], 17)
    arrived(total.at[other + 1], 18)
    for copy in sent:
        copy.wait_send()
    yield


def tp_sum(get, total, bufs):
    def get_all(chunks, into):
        for k in range(4):
            into[k] = get(chunks[k]).astype(into.dtype)

    for _ in tp_steps(get_all, total, bufs):
        pass


def shift_req(axis, d):
    r, t = lax.axis_index("req"), lax.axis_index("tp")
    x, z = lax.div(r, 4), lax.rem(r, 4)
    if axis == 0:
        return (mod4(x + d) * 4 + z, t)
    return (x * 4 + mod4(z + d), t)


def req_place(axis):
    r = lax.axis_index("req")
    return lax.div(r, 4) if axis == 0 else lax.rem(r, 4)


def req_partners():
    return [shift_req(axis, d) for axis in (0, 1) for d in (1, -1)]


PROWS = BROWS // 2
FRONT_SCRATCH = (
    [
        pltpu.VMEM((2, BLOCKS, PROWS, FEATS), BF16),
        pltpu.VMEM((2, 4, 4 * PROWS, FEATS), BF16),
        pltpu.VMEM((2, 4, 4 * PROWS, FEATS), BF16),
        pltpu.VMEM((2, 4, 4 * PROWS, PAGE), F32),
    ]
    + [pltpu.VMEM((2, 2, 4, 4 * PROWS, WIDE), BF16)] * 6
    + [pltpu.VMEM((2, 2, 4, PROWS, WIDE), BF16)] * 6
    + [pltpu.VMEM((2, 2, 4, 4, PROWS, WIDE), F32)]
    + [pltpu.SemaphoreType.DMA((2, 6, 2, 4)), pltpu.SemaphoreType.DMA((2, 6, 2, 4))]
    + [pltpu.VMEM((2, 4 * PROWS, PAGE), BF16)] * 6
    + [pltpu.VMEM((2, PROWS, PAGE), BF16)] * 6
    + [pltpu.VMEM((2, 4, PROWS, PAGE), F32)]
    + [pltpu.SemaphoreType.DMA((2, 6)), pltpu.SemaphoreType.DMA((2, 6))]
)


class ScatterSum:
    def __init__(self, axis, d, partial, bufs, total, ss, rs):
        self.axes = (axis, 1 - axis)
        self.d = d
        self.partial = partial
        self.far_s, self.far_r, self.dir_s, self.dir_r, self.com_s, self.com_r = bufs[:6]
        self.far2_s, self.far2_r, self.dir2_s, self.dir2_r, self.com2_s, self.com2_r = bufs[6:]
        self.total = total
        self.ss, self.rs = ss, rs

    def copy(self, n):
        src = (self.far_s, self.dir_s, self.com_s, self.far2_s, self.dir2_s, self.com2_s)[n]
        dst = (self.far_r, self.dir_r, self.com_r, self.far2_r, self.dir2_r, self.com2_r)[n]
        d = -self.d if n % 3 == 1 else self.d
        return rcopy(src, dst, self.ss(n), self.rs(n), shift_req(self.axes[n // 3], d))

    def far(self):
        p = req_place(self.axes[0])
        self.far_s[...] = self.partial(mod4(p + 2)).astype(BF16)
        self.copy(0).start()

    def direct(self):
        p = req_place(self.axes[0])
        self.dir_s[...] = self.partial(mod4(p - self.d)).astype(BF16)
        self.copy(1).start()

    def combined(self):
        p = req_place(self.axes[0])
        mine = self.partial(mod4(p + self.d))
        self.copy(0).wait_recv()
        self.com_s[...] = (mine + self.far_r[...].astype(F32)).astype(BF16)
        self.copy(2).start()

    def own(self):
        p, q = req_place(self.axes[0]), req_place(self.axes[1])
        mine = self.partial(p)
        self.copy(1).wait_recv()
        self.copy(2).wait_recv()
        mine = mine + self.dir_r[...].astype(F32) + self.com_r[...].astype(F32)
        self.total[...] = mine.reshape(4, PROWS, mine.shape[1])
        self.far2_s[...] = self.total[mod4(q + 2)].astype(BF16)
        self.copy(3).start()
        self.dir2_s[...] = self.total[mod4(q - self.d)].astype(BF16)
        self.copy(4).start()

    def combined2(self):
        q = req_place(self.axes[1])
        self.copy(3).wait_recv()
        self.com2_s[...] = (self.total[mod4(q + self.d)] + self.far2_r[...].astype(F32)).astype(
            BF16
        )
        self.copy(5).start()

    def result(self):
        q = req_place(self.axes[1])
        self.copy(4).wait_recv()
        self.copy(5).wait_recv()
        return self.total[q] + self.dir2_r[...].astype(F32) + self.com2_r[...].astype(F32)

    def drain(self):
        for n in range(6):
            self.copy(n).wait_send()


class Front:
    def __init__(self, g, refs, out, tp_bufs, rest):
        self.g, self.out, self.tp_bufs = g, out, tp_bufs
        self.ids, self.emb, self.gain, self.w_inner, self.w_gate = refs
        self.embedded, self.lhs_x, self.lhs_z, self.squares = (ref.at[g] for ref in rest[:4])
        self.big = [ref.at[g] for ref in rest[4:17]]
        self.big_ss, self.big_rs = rest[17:19]
        small = [ref.at[g] for ref in rest[19:32]]
        small_ss, small_rs = rest[32:34]
        self.norm = ScatterSum(
            0, 1, lambda chunk: self.squares[chunk], small[:12], small[12],
            lambda n: small_ss.at[g, n], lambda n: small_rs.at[g, n],
        )

    def looked(self, chunks, into):
        emb = self.emb
        want = jnp.concatenate(
            [self.ids[self.g, pl.ds(2 * ch, 2)].reshape(2 * PROWS, 1) for ch in chunks], axis=0
        )
        span = 1024
        acc = jnp.zeros((8 * PROWS, FEATS), F32)
        for k in range(emb.shape[0] // span):
            lane = lax.broadcasted_iota(jnp.int32, (8 * PROWS, span), 1) + k * span
            hot = jnp.where(lane == want, 1.0, 0.0).astype(BF16)
            acc = acc + dot(hot, emb[k * span : (k + 1) * span, :])
        into[...] = acc.reshape(4, 2, PROWS, FEATS).astype(into.dtype)

    def lookup(self):
        return tp_steps(self.looked, self.embedded, self.tp_bufs)

    def spread(self):
        def body(b, carry):
            x, z = lax.div(b, 4), lax.rem(b, 4)
            rows = self.embedded[b].astype(F32)
            scaled = (rows * self.gain[...]).astype(BF16)
            along_z = pl.ds(pl.multiple_of(z * PROWS, PROWS), PROWS)
            along_x = pl.ds(pl.multiple_of(x * PROWS, PROWS), PROWS)
            self.lhs_x[x, along_z, :] = scaled
            self.lhs_z[z, along_x, :] = scaled
            self.squares[x, along_z, :] = jnp.broadcast_to(
                jnp.sum(rows * rows, axis=1, keepdims=True), (PROWS, PAGE)
            )
            return carry

        lax.fori_loop(0, BLOCKS, body, 0)

    def unit(self, ab, u):
        lhs, weight = ((self.lhs_x, self.w_inner), (self.lhs_z, self.w_gate))[ab]
        g = self.g

        def partial(chunk):
            cols = pl.ds(pl.multiple_of(u * WIDE, WIDE), WIDE)
            return dot(lhs[chunk], weight[:, cols])

        views = [ref.at[ab, u] for ref in self.big[:12]]
        return ScatterSum(
            ab, 1 - 2 * lax.rem(u, 2), partial, views, self.big[12].at[ab, u],
            lambda n: self.big_ss.at[g, n, ab, u], lambda n: self.big_rs.at[g, n, ab, u],
        )

    def each(self, step):
        step(self.norm)

        def body(u, carry):
            for ab in range(2):
                step(self.unit(ab, u))
            return carry

        lax.fori_loop(0, 4, body, 0)

    def finish(self):
        inv_rms = lax.rsqrt(self.norm.result()[:, :1] / D + 1e-05)

        def body(u, carry):
            for ab in range(2):
                cols = pl.ds(pl.multiple_of((ab * 4 + u) * WIDE, WIDE), WIDE)
                rows = slice(self.g * PROWS, (self.g + 1) * PROWS)
                self.out[rows, cols] = self.unit(ab, u).result() * inv_rms
            return carry

        lax.fori_loop(0, 4, body, 0)


PLAN, FIRST, SECOND, LAST, SIDE1, SIDE2, WHICH = 24, 0, 4, 8, 9, 13, 17
GROUP = 4 * BROWS
MOST = 32


def make_plan(events, plan):
    r = lax.axis_index("req")
    shape = (GROUP, 128)
    lane = lax.broadcasted_iota(jnp.int32, shape, 1)
    number = lax.broadcasted_iota(jnp.int32, shape, 0)
    kind, quarter = lax.rem(lane, 4), lax.div(lane, 4)
    block = lax.div(number, BROWS)
    row = lax.broadcasted_iota(jnp.int32, (GROUP, GROUP), 0)
    col = lax.broadcasted_iota(jnp.int32, (GROUP, GROUP), 1)
    earlier = col < row
    near = earlier & (lax.div(col, BROWS) == lax.div(row, BROWS))
    earlier = jnp.where(earlier, 1.0, 0.0).astype(BF16)
    near = jnp.where(near, 1.0, 0.0).astype(BF16)

    def ahead(which, mask):
        return dot(which, jnp.where(mask, 1.0, 0.0).astype(BF16)).astype(jnp.int32)

    def parts(packed):
        packed = jnp.broadcast_to(packed, shape)
        owner = jnp.bitwise_and(jnp.right_shift(packed, 6), 15)
        return packed >= 4096, owner, jnp.bitwise_and(packed, 63)

    def fold(mask, value):
        return jnp.sum(jnp.where(mask, value + 1, 0), axis=0, keepdims=True) - 1

    plan[...] = jnp.zeros_like(plan)
    need1 = jnp.zeros((1, 128), jnp.int32)
    need2 = jnp.zeros((1, 128), jnp.int32)
    for h in range(2):
        p_me, q_me = req_place(h), req_place(1 - h)
        done, owner, _ = parts(events[h, q_me])
        p_of = lax.div(owner, 4) if h == 0 else lax.rem(owner, 4)
        q_of = lax.rem(owner, 4) if h == 0 else lax.div(owner, 4)
        mask1 = done & (p_of == lane)
        rank1 = ahead(near, mask1)
        mask2 = done & (p_of == p_me) & (q_of == lane)
        rank2 = ahead(earlier, mask2)
        here = jnp.sum(jnp.where(lane == p_me, rank1, 0), axis=1, keepdims=True)
        at = block * MOST + here
        mine = block == p_me
        event = number - p_me * BROWS
        base = PLAN * h
        for d in range(4):
            rank = jnp.broadcast_to(rank1[:, d : d + 1], shape)
            mask = mine & done & (p_of == d)
            plan[base + FIRST + d : base + FIRST + d + 1, :] = fold(mask & (rank == lane), event)
            plan[base + SIDE1 + d : base + SIDE1 + d + 1, :] = fold(
                mask & (rank == quarter), kind * BROWS + event
            )
            rank = jnp.broadcast_to(rank2[:, d : d + 1], shape)
            mask = done & (p_of == p_me) & (q_of == d)
            plan[base + SECOND + d : base + SECOND + d + 1, :] = fold(mask & (rank == lane), at)
            plan[base + SIDE2 + d : base + SIDE2 + d + 1, :] = fold(
                mask & (rank == quarter), at * 4 + kind
            )
        found = jnp.zeros((1, 128), jnp.int32)
        for q in range(4):
            done, owner, slot = parts(events[h, q])
            mask = done & (owner == r)
            value = q * MOST + ahead(earlier, mask)
            found = found + fold(mask & (slot == lane), value) + 1
            p_of = lax.div(owner, 4) if h == 0 else lax.rem(owner, 4)
            leaving = jnp.where(done & (p_of == lane), 1, 0).reshape(4, BROWS, 128)
            for n in range(4):
                need1 = jnp.maximum(need1, jnp.sum(leaving[n], axis=0, keepdims=True))
            staying = jnp.where(done & (owner == lane), 1, 0)
            need2 = jnp.maximum(need2, jnp.sum(staying, axis=0, keepdims=True))
        plan[base + LAST : base + LAST + 1, :] = found - 1
    need1 = jnp.max(need1, axis=1, keepdims=True)
    need2 = jnp.max(need2, axis=1, keepdims=True)
    which = jnp.full((1, 1), len(SAVE_COUNTS) - 1, jnp.int32)
    for n in range(len(SAVE_COUNTS) - 1):
        few, many = SAVE_COUNTS[n]
        which = jnp.where((need1 <= few) & (need2 <= many), n, which)
    plan[WHICH : WHICH + 1, :] = jnp.broadcast_to(which, (1, 128))


TP_PAIR = tp_scratch(PROWS)


def front_kernel(ids, emb, gain, inner_hbm, gate_hbm, events, out, plan, *scratch):
    cut = len(TP_PAIR)
    w_inner, w_gate, load_sems = scratch[-3:]
    refs = (ids, emb, gain, w_inner, w_gate)
    loads = [
        pltpu.make_async_copy(inner_hbm, w_inner, load_sems.at[0]),
        pltpu.make_async_copy(gate_hbm, w_gate, load_sems.at[1]),
    ]
    for load in loads:
        load.start()
    one, two = (
        Front(g, refs, out, scratch[g * cut : (g + 1) * cut], scratch[2 * cut :]) for g in range(2)
    )
    greet(tp_partners() + req_partners())
    for _ in one.lookup():
        pass
    one.spread()
    for load in loads:
        load.wait()
    one.each(lambda s: s.far())
    one.each(lambda s: s.direct())
    lookup = two.lookup()
    next(lookup)
    one.each(lambda s: s.combined())
    next(lookup)
    two.spread()
    two.each(lambda s: s.far())
    one.each(lambda s: s.own())
    two.each(lambda s: s.direct())
    one.each(lambda s: s.combined2())
    make_plan(events, plan)
    two.each(lambda s: s.combined())
    one.finish()
    two.each(lambda s: s.own())
    two.each(lambda s: s.combined2())
    two.finish()
    one.each(lambda s: s.drain())
    two.each(lambda s: s.drain())


def vmem_call(kernel, out_shape, n_in, scratch, in_hbm=(), **params):
    spec = pl.BlockSpec(memory_space=pltpu.VMEM)
    hbm = pl.BlockSpec(memory_space=pl.ANY)
    return pl.pallas_call(
        kernel,
        out_shape=out_shape,
        in_specs=[hbm if n in in_hbm else spec for n in range(n_in)],
        out_specs=jax.tree.map(lambda _: spec, out_shape),
        scratch_shapes=scratch,
        compiler_params=pltpu.CompilerParams(vmem_limit_bytes=VMEM_LIMIT, **params),
    )


def silu(v):
    return v / (1.0 + jnp.exp(-v))


RCOLS = RANK + 128


def rank_kernel(
    sums, conv, taps, bias, w_low, w_select, w_dt, dt_bias, step, activ, select,
    pair_s, pair_r, quad_s, quad_r, full, ss, rs,
):
    r, t = lax.axis_index("req"), lax.axis_index("tp")
    y, c = lax.div(t, 2), lax.rem(t, 2)
    core = (r, y * 2 + 1 - c)
    others = [(r, mod4(y + d) * 2 + c) for d in (1, 2, 3)]
    greet([core] + others)
    for n in range(STEPS):
        total = bias[...] + jnp.zeros((ROWS, INNER), F32)
        for k in range(4):
            at = n + k
            if at < 3:
                row = conv[at].astype(F32)
            else:
                row = sums[(at - 3) * ROWS : (at - 2) * ROWS, :INNER].astype(BF16).astype(F32)
            total = total + row * taps[k : k + 1, :]
        activ[n * ROWS : (n + 1) * ROWS, :] = silu(total).astype(BF16).astype(F32)
    act = activ[...].astype(BF16)
    low = dot(act, w_low[...]).reshape(2, BROWS // 2, RANK)
    sel = lax.dot_general(
        act, w_select[...], (((1,), (1,)), ((), ())), preferred_element_type=F32
    )
    sel = jnp.concatenate([sel, jnp.zeros((BROWS, 128 - 2 * STATE), F32)], axis=1)
    sel = sel.reshape(2, BROWS // 2, 128)
    pair_s[:, :, :RANK] = low
    pair_s[:, :, RANK:] = sel
    swap = rcopy(pair_s, pair_r, ss.at[0], rs.at[0], core)
    swap.start()
    swap.wait_recv()
    chip = pair_s[c] + pair_r[c]
    quad_s[...] = chip.astype(BF16)
    copies = [rcopy(quad_s, quad_r.at[n], ss.at[1 + n], rs.at[1 + n], others[n]) for n in range(3)]
    for copy in copies:
        copy.start()
    acc = quad_s[...].astype(F32)
    for n in range(3):
        copies[n].wait_recv()
        acc = acc + quad_r[n].astype(F32)
    full[c] = acc
    back = rcopy(full.at[c], full.at[c], ss.at[4], rs.at[4], core)
    back.start()
    rcopy(full.at[1 - c], full.at[1 - c], ss.at[4], rs.at[4], core).wait_recv()
    low_rank = full[:, :, :RANK].reshape(BROWS, RANK).astype(BF16)
    select[...] = full[:, :, RANK:].reshape(BROWS, 128)
    v = dot(low_rank, w_dt[...]) + dt_bias[...]
    step[...] = jnp.maximum(v, 0.0) + jnp.log1p(jnp.exp(-jnp.abs(v)))
    swap.wait_send()
    for copy in copies:
        copy.wait_send()
    back.wait_send()


def state_kernel(
    codes, scales, step, activ, select, sums, conv, decay_log, skip,
    gated, final, new_codes, source, last_window, output, scale_rows, rates,
):
    lane = lax.broadcasted_iota(jnp.int32, (STATE, 128), 1)
    row_of = lax.broadcasted_iota(jnp.int32, (STATE, 128), 0)
    page_lane = lax.broadcasted_iota(jnp.int32, (1, 128), 1)
    width = 4 * PAGE

    def request(i, carry):
        b_in, c_out = [], []
        for n in range(STEPS):
            row = select[pl.ds(n * ROWS + i, 1), :]
            b_in.append(jnp.sum(jnp.where(lane == row_of, row, 0.0), axis=1, keepdims=True))
            c_out.append(
                jnp.sum(jnp.where(lane == row_of + STATE, row, 0.0), axis=1, keepdims=True)
            )
        kept = [jnp.zeros((1, 128), F32) for _ in range(STEPS)]
        for part in range(INNER // width):
            cols = slice(part * width, (part + 1) * width)
            rate = rates[:, cols]
            current = codes[i, :, cols].astype(F32) * scales[pl.ds(i, 1), cols]
            for n in range(STEPS):
                at = n * ROWS + i
                dt = step[pl.ds(at, 1), cols]
                act = activ[pl.ds(at, 1), cols]
                current = jnp.exp2(dt * rate) * current + (dt * act) * b_in[n]
                output[pl.ds(at, 1), cols] = jnp.sum(current * c_out[n], axis=0, keepdims=True)
                peak = jnp.max(jnp.abs(current), axis=0, keepdims=True)
                for page in range(4):
                    here = slice(page * PAGE, (page + 1) * PAGE)
                    top = jnp.max(peak[:, here], axis=1, keepdims=True)
                    scale = (top + 1e-06).astype(BF16).astype(F32)
                    kept[n] = jnp.where(page_lane == part * 4 + page, scale, kept[n])
                    new_codes[at, :, part * width + page * PAGE : part * width + (page + 1) * PAGE] = (
                        current[:, here] * (1.0 / scale)
                    ).astype(BF16)
        for n in range(STEPS):
            scale_rows[pl.ds(n * ROWS + i, 1), :] = kept[n]
        final[i] = new_codes[(STEPS - 1) * ROWS + i]
        return carry

    rates[...] = -jnp.exp(decay_log[...]) * 1.4426950408889634
    lax.fori_loop(0, ROWS, request, 0)
    gated[...] = (
        (output[...] + skip[...] * activ[...]) * silu(sums[:, INNER:])
    ).astype(BF16)
    rows = [conv[k].astype(F32) for k in range(3)]
    rows += [sums[n * ROWS : (n + 1) * ROWS, :INNER] for n in range(STEPS)]
    for k in range(3):
        source[k * BROWS : (k + 1) * BROWS, :] = jnp.concatenate(
            rows[k + 1 : k + 1 + STEPS], axis=0
        ).astype(BF16)
        last_window[k] = rows[STEPS + k].astype(BF16)
    source[3 * BROWS :, :] = jnp.zeros((BROWS, INNER), BF16)
    source[3 * BROWS :, :128] = scale_rows[...].astype(BF16)


def middle_kernel(
    sums, conv, taps, bias, w_low, w_select, w_dt, dt_bias, codes, scales, decay_log, skip,
    gated, final, new_codes, source, last_window, step, activ, select, output, scale_rows, rates,
    *rest,
):
    rank_kernel(
        sums, conv, taps, bias, w_low, w_select, w_dt, dt_bias, step, activ, select, *rest
    )
    state_kernel(
        codes, scales, step, activ, select, sums, conv, decay_log, skip,
        gated, final, new_codes, source, last_window, output, scale_rows, rates,
    )


BACK_SCRATCH = [
    pltpu.VMEM((BLOCKS, BROWS, INNER // 2), BF16),
    pltpu.VMEM((BLOCKS, BROWS, INNER // 2), BF16),
    pltpu.VMEM((BLOCKS, BROWS, FEATS), F32),
    pltpu.SemaphoreType.DMA((2, 16)),
    pltpu.SemaphoreType.DMA((2, 16)),
]


class Gather:
    def __init__(self, axis, buf, ss, rs):
        self.axes = (axis, 1 - axis)
        self.buf, self.ss, self.rs = buf, ss, rs
        self.q, self.p = req_place(axis), req_place(1 - axis)
        self.order = [self.q, mod4(self.q - 1), mod4(self.q + 1), mod4(self.q + 2)]
        self.sent = []

    def send(self, ref, n, axis, d):
        copy = rcopy(ref, ref, self.ss.at[n], self.rs.at[n], shift_req(axis, d))
        copy.start()
        self.sent.append(copy)

    def arrived(self, ref, n):
        rcopy(ref, ref, self.ss.at[n], self.rs.at[n], shift_req(self.axes[0], 1)).wait_recv()

    def block(self, p, q):
        return self.buf.at[p * 4 + q]

    def rows(self, p, q, h):
        return self.buf.at[p * 4 + q, pl.ds(h * (BROWS // 2), BROWS // 2)]

    def start(self):
        mine = self.block(self.p, self.q)
        self.send(mine, 0, self.axes[0], 1)
        self.send(mine, 1, self.axes[0], -1)
        self.spread(0)

    def spread(self, k):
        block = self.block(self.p, self.order[k])
        self.send(block, 4 + k, self.axes[1], 1)
        self.send(block, 8 + k, self.axes[1], -1)

    def near(self):
        self.arrived(self.block(self.p, self.order[1]), 0)
        self.send(self.rows(self.p, self.order[1], 0), 2, self.axes[0], 1)
        self.spread(1)
        self.arrived(self.block(self.p, self.order[2]), 1)
        self.send(self.rows(self.p, self.order[2], 1), 3, self.axes[0], -1)
        self.spread(2)

    def last(self):
        self.arrived(self.rows(self.p, self.order[3], 0), 2)
        self.arrived(self.rows(self.p, self.order[3], 1), 3)
        self.spread(3)

    def relay(self, k):
        below, above = mod4(self.p - 1), mod4(self.p + 1)
        self.arrived(self.block(below, self.order[k]), 4 + k)
        if k < 2:
            self.send(self.block(below, self.order[k]), 12 + k, self.axes[1], 1)
        self.arrived(self.block(above, self.order[k]), 8 + k)
        if k >= 2:
            self.send(self.block(above, self.order[k]), 12 + k, self.axes[1], -1)

    def end(self, k):
        self.arrived(self.block(mod4(self.p + 2), self.order[k]), 12 + k)

    def drain(self):
        for copy in self.sent:
            copy.wait_send()


class Project:
    def __init__(self, gated, w_out, scratch):
        self.tp_bufs, rest = scratch[: len(TP_SCRATCH)], scratch[len(TP_SCRATCH) :]
        self.buf_a, self.buf_b, self.acc, gss, grs = rest
        self.gated, self.w_out = gated, w_out
        self.parts = [
            Gather(1, self.buf_a, gss.at[0], grs.at[0]),
            Gather(0, self.buf_b, gss.at[1], grs.at[1]),
        ]

    def start(self):
        r = lax.axis_index("req")
        self.acc[...] = jnp.zeros_like(self.acc)
        self.buf_a[r] = self.gated[:, :HALF]
        self.buf_b[lax.rem(r, 4) * 4 + lax.div(r, 4)] = self.gated[:, HALF:]
        for part in self.parts:
            part.start()

    def project(self, n, p, k):
        q = self.parts[n].order[k]
        if n == 0:
            self.acc[p * 4 + q] += dot(self.buf_a[p * 4 + q], self.w_out[:HALF, :])
        else:
            self.acc[q * 4 + p] += dot(self.buf_b[p * 4 + q], self.w_out[HALF:, :])

    def gather(self):
        parts = self.parts
        for part in parts:
            part.near()
        for part in parts:
            part.last()
        for k in range(4):
            for n in range(2):
                self.project(n, parts[n].p, k)
        for k in range(4):
            for part in parts:
                part.relay(k)
            for n in range(2):
                self.project(n, mod4(parts[n].p - 1), k)
                self.project(n, mod4(parts[n].p + 1), k)
        for k in range(4):
            for n in range(2):
                parts[n].end(k)
                self.project(n, mod4(parts[n].p + 2), k)

    def total(self, mixed):
        tp_sum(lambda ch: self.acc[pl.ds(2 * ch, 2)], mixed, self.tp_bufs)
        for part in self.parts:
            part.drain()


def project_kernel(gated, w_out, mixed, *scratch):
    greet(tp_partners() + req_partners())
    work = Project(gated, w_out, scratch)
    work.start()
    work.gather()
    work.total(mixed)


FAR = (2, 1, 3)


def save_scratch(room):
    return [
        pltpu.VMEM((2, 4 * room, STATE, HALF), BF16),
        pltpu.VMEM((2, 4 * room, STATE, HALF), BF16),
        pltpu.VMEM((2, 4 * room, STATE, HALF), BF16),
        pltpu.VMEM((2, 16 * room, HALF), BF16),
        pltpu.VMEM((2, 16 * room, HALF), BF16),
        pltpu.VMEM((2, 16 * room, HALF), BF16),
        pltpu.SemaphoreType.DMA((2, 2, 3, 2)),
        pltpu.SemaphoreType.DMA((2, 2, 3, 2)),
    ]


class Save:
    def __init__(self, counts, room, index, plan, codes, source, scratch):
        self.counts, self.room = counts, room
        self.index, self.plan = index, plan
        self.codes, self.source = codes, source
        self.sent, self.got1, self.got2, self.side, self.side1, self.side2, self.ss, self.rs = (
            scratch
        )

    def clear(self):
        self.side1[...] = jnp.zeros_like(self.side1)
        self.side2[...] = jnp.zeros_like(self.side2)

    def pick(self, want, rows):
        span = rows.shape[0]
        if self.room != MOST and span != self.source.shape[0]:
            row = lax.div(want, 4 * MOST) * (4 * self.room) + lax.rem(want, 4 * MOST)
            want = jnp.where(want >= 0, row, -1)
        number = lax.broadcasted_iota(jnp.int32, (span, 128), 0)
        hot = jnp.where(number == want, 1.0, 0.0).astype(BF16)
        picked = lax.dot_general(hot, rows, (((0,), (0,)), ((), ())), preferred_element_type=F32)
        return picked.astype(BF16)

    def place_of(self, at):
        at = jnp.maximum(at, 0)
        return lax.div(at, MOST) * self.room + lax.rem(at, MOST)

    def buffers(self, n):
        return ((self.got1, self.side1), (self.got2, self.side2))[n]

    def axis(self, n, h):
        return h if n == 0 else 1 - h

    def rows(self, ref, h, block, each):
        count = each * self.room
        return lambda used: ref.at[h, pl.ds(pl.multiple_of(block * count, 16 if each > 1 else 4), used)]

    def used(self, n):
        return self.counts[n], -(-4 * self.counts[n] // 16) * 16

    def copy(self, n, h, k, i):
        d = FAR[k]
        here = req_place(self.axis(n, h))
        dest, dev = mod4(here + d), shift_req(self.axis(n, h), d)
        src, dst = ((self.sent, self.side)[i], self.buffers(n)[i])
        each, used = (1, 4)[i], self.used(n)[i]
        return rcopy(
            self.rows(src, h, dest, each)(used), self.rows(dst, h, here, each)(used),
            self.ss.at[n, h, k, i], self.rs.at[n, h, k, i], dev,
        )

    def send(self, n):
        into, side_into = self.buffers(n)
        room, many = self.room, self.used(n)[1]
        order = [(k, d, h) for k, d in enumerate(FAR + (0,)) for h in range(2)]
        for k, d, h in order:
            dest = mod4(req_place(self.axis(n, h)) + d)
            keep = into if d == 0 else self.sent

            def pack(m, carry):
                at = self.index[PLAN * h + (FIRST, SECOND)[n] + dest, m]
                if n == 0:
                    row = self.codes[jnp.maximum(at, 0), :, h * HALF : (h + 1) * HALF]
                else:
                    row = self.got1[h, self.place_of(at)]
                keep[h, dest * room + m] = row
                return carry

            lax.fori_loop(0, self.counts[n], pack, 0)
            if d != 0:
                self.copy(n, h, k, 0).start()
        for k, d, h in order:
            dest = mod4(req_place(self.axis(n, h)) + d)
            keep = side_into if d == 0 else self.side
            rows = self.source[:, h * HALF : (h + 1) * HALF] if n == 0 else self.side1[h]
            want = self.plan[pl.ds(PLAN * h + (SIDE1, SIDE2)[n] + dest, 1), :]
            block = pl.ds(pl.multiple_of(dest * 4 * room, 16), many)
            keep[h, block, :] = self.pick(want, rows)[:many]
            if d != 0:
                self.copy(n, h, k, 1).start()

    def receive(self, n):
        into, side_into = self.buffers(n)
        few, many = self.used(n)
        for k, d in enumerate(FAR):
            for h in range(2):
                origin = mod4(req_place(self.axis(n, h)) - d)
                dev = shift_req(self.axis(n, h), d)
                for i, (ref, each, used) in enumerate(((into, 1, few), (side_into, 4, many))):
                    block = self.rows(ref, h, origin, each)(used)
                    rcopy(
                        block, block, self.ss.at[n, h, k, i], self.rs.at[n, h, k, i], dev
                    ).wait_recv()
        for k in range(3):
            for h in range(2):
                for i in range(2):
                    self.copy(n, h, k, i).wait_send()

    def place(self, out, windows, scale):
        def one(s, carry):
            for h in range(2):
                at = self.index[PLAN * h + LAST, s]
                row = self.got2[h, self.place_of(at)]
                out[s, :, h * HALF : (h + 1) * HALF] = jnp.where(at >= 0, row, jnp.zeros_like(row))
            return carry

        lax.fori_loop(0, SLOTS, one, 0)
        for h in range(2):
            at = self.plan[PLAN * h + LAST : PLAN * h + LAST + 1, :]
            for k in range(3):
                want = jnp.where(at >= 0, at * 4 + k, -1)
                windows[k, :, h * HALF : (h + 1) * HALF] = self.pick(want, self.side2[h])[:SLOTS]
            if h == 0:
                want = jnp.where(at >= 0, at * 4 + 3, -1)
                scale[...] = self.pick(want, self.side2[0, :, :128])[:SLOTS]


def save_partners():
    return [shift_req(axis, d) for axis in (0, 1) for d in FAR]


def save_kernel(
    counts, index, plan, codes, source, out, windows, scale, *scratch
):
    work = Save(counts, MOST, index, plan, codes, source, scratch)
    work.clear()
    greet(save_partners())
    work.send(0)
    work.receive(0)
    work.send(1)
    work.receive(1)
    work.place(out, windows, scale)


def both_kernel(
    counts, index, plan, codes_hbm, source, gated, out_hbm, mixed, out, windows, scale, *scratch,
):
    cut = len(TP_SCRATCH) + len(BACK_SCRATCH)
    *scratch, codes, w_out, load_sems = scratch
    loads = [
        pltpu.make_async_copy(codes_hbm, codes, load_sems.at[0]),
        pltpu.make_async_copy(out_hbm, w_out, load_sems.at[1]),
    ]
    for load in loads:
        load.start()
    project = Project(gated, w_out, scratch[:cut])
    save = Save(counts, ROOM, index, plan, codes, source, scratch[cut:])
    save.clear()
    greet(tp_partners() + save_partners())
    project.start()
    for load in loads:
        load.wait()
    save.send(0)
    project.gather()
    save.receive(0)
    save.send(1)
    project.total(mixed)
    save.receive(1)
    save.place(out, windows, scale)


ROOM = 28
SAVE_COUNTS = ((24, 26), (20, 24), (MOST, MOST))


def pack_events(finish, holder, slot_index):
    packed = finish * 4096 + jnp.bitwise_and(holder, 15) * 64 + jnp.bitwise_and(slot_index, 63)
    packed = packed.reshape(STEPS, 4, 4, ROWS).transpose(2, 1, 0, 3)
    both = jnp.stack([packed, packed.transpose(1, 0, 2, 3)])
    return both.reshape(2, 4, GROUP, 1)


def per_device(
    tokens, finish, holder, slot_index, embedding, norm_gain, proj_inner, proj_gate, conv_weight,
    conv_bias, proj_low, proj_select, proj_dt, dt_bias, decay_log, skip_gain, proj_out, state_codes,
    state_scales, conv_state,
):
    ids = tokens.reshape(2, 2, BLOCKS, ROWS).transpose(0, 2, 1, 3).reshape(2, BLOCKS, PROWS, 1)
    ids = ids - lax.axis_index("tp") * embedding.shape[0]
    conv = conv_state.transpose(1, 0, 2)
    scales = jnp.repeat(state_scales.astype(F32), PAGE, axis=1)
    shape = jax.ShapeDtypeStruct
    sums, plan = vmem_call(
        front_kernel,
        [shape((BROWS, 2 * INNER), F32), shape((2 * PLAN, 128), jnp.int32)], 6,
        TP_PAIR * 2
        + list(FRONT_SCRATCH)
        + [pltpu.VMEM((FEATS, INNER), BF16)] * 2
        + [pltpu.SemaphoreType.DMA((2,))],
        in_hbm=(3, 4), collective_id=0, has_side_effects=True,
    )(
        ids, embedding, norm_gain.reshape(1, -1), proj_inner, proj_gate,
        pack_events(finish, holder, slot_index),
    )
    half = BROWS // 2
    vmem = pl.BlockSpec(memory_space=pltpu.VMEM)
    smem = pl.BlockSpec(memory_space=pltpu.SMEM)
    gated, final, new_codes, source, last_window = vmem_call(
        middle_kernel,
        [
            shape((BROWS, INNER), BF16),
            shape((ROWS, STATE, INNER), BF16),
            shape((BROWS, STATE, INNER), BF16),
            shape((4 * BROWS, INNER), BF16),
            shape((3, ROWS, INNER), BF16),
        ],
        12,
        [
            pltpu.VMEM((BROWS, INNER), F32),
            pltpu.VMEM((BROWS, INNER), F32),
            pltpu.VMEM((BROWS, 128), F32),
            pltpu.VMEM((BROWS, INNER), F32),
            pltpu.VMEM((BROWS, 128), F32),
            pltpu.VMEM((STATE, INNER), F32),
            pltpu.VMEM((2, half, RCOLS), F32),
            pltpu.VMEM((2, half, RCOLS), F32),
            pltpu.VMEM((half, RCOLS), BF16),
            pltpu.VMEM((3, half, RCOLS), BF16),
            pltpu.VMEM((2, half, RCOLS), F32),
            pltpu.SemaphoreType.DMA((5,)),
            pltpu.SemaphoreType.DMA((5,)),
        ],
        collective_id=1, has_side_effects=True,
    )(
        sums, conv, conv_weight, conv_bias.reshape(1, -1), proj_low, proj_select, proj_dt,
        dt_bias.reshape(1, -1), state_codes, scales, decay_log, skip_gain.reshape(1, -1),
    )
    saved = [shape((SLOTS, STATE, INNER), BF16)] + [shape((3, SLOTS, INNER), BF16)] + [
        shape((SLOTS, 128), BF16)
    ]
    mixed_shape = shape((BLOCKS, BROWS, FEATS), BF16)
    back_scratch = TP_SCRATCH + BACK_SCRATCH

    def call(kernel, results, operands, scratch, number, in_hbm=()):
        return pl.pallas_call(
            kernel,
            out_shape=results,
            in_specs=[smem]
            + [
                pl.BlockSpec(memory_space=pl.ANY) if n in in_hbm else vmem
                for n in range(1, len(operands))
            ],
            out_specs=[vmem] * len(results),
            scratch_shapes=scratch,
            compiler_params=pltpu.CompilerParams(
                vmem_limit_bytes=VMEM_LIMIT, collective_id=number, has_side_effects=True
            ),
        )(*operands)

    def together(n):
        def run(*operands):
            return tuple(
                call(
                    functools.partial(both_kernel, SAVE_COUNTS[n]), [mixed_shape] + saved,
                    operands,
                    back_scratch
                    + save_scratch(ROOM)
                    + [
                        pltpu.VMEM((BROWS, STATE, INNER), BF16),
                        pltpu.VMEM((INNER, FEATS), BF16),
                        pltpu.SemaphoreType.DMA((2,)),
                    ],
                    3 + n, (2, 5),
                )
            )

        return run

    def apart(*operands):
        mixed = vmem_call(
            project_kernel, mixed_shape, 2, back_scratch, collective_id=2, has_side_effects=True
        )(*operands[4:])
        rest = call(
            functools.partial(save_kernel, SAVE_COUNTS[2]), saved, operands[:4],
            save_scratch(MOST), 5,
        )
        return tuple([mixed, *rest])

    mixed, cache_codes, windows, cache_scales = lax.switch(
        plan[WHICH, 0], [together(0), together(1), apart], plan, plan, new_codes, source, gated, proj_out,
    )
    mixed = mixed.reshape(BLOCKS, STEPS, ROWS, FEATS).transpose(1, 0, 2, 3)
    mixed = mixed.reshape(STEPS, BLOCKS * ROWS, FEATS)
    last = slice((STEPS - 1) * ROWS, BROWS)
    pages = INNER // PAGE
    next_scales = source[3 * BROWS :][last, :pages]
    next_window = last_window.transpose(1, 0, 2)
    cache_window = windows.transpose(1, 0, 2)
    return (
        mixed, final, next_scales, next_window, cache_codes, cache_scales[:, :pages], cache_window,
    )


def solution(mesh):
    in_specs = (
        P(), P(), P(), P(), P("tp", "req"), P("req"), P("req", "tp"), P("req", "tp"),
        P(None, "tp"), P("tp"), P("tp", None), P(None, "tp"), P(None, "tp"), P("tp"),
        P(None, "tp"), P("tp"), P("tp", "req"), P("req", None, "tp"), P("req", "tp"),
        P("req", None, "tp"),
    )
    out_specs = (
        P(None, None, "req"), P("req", None, "tp"), P("req", "tp"), P("req", None, "tp"),
        P("req", None, "tp"), P("req", "tp"), P("req", None, "tp"),
    )
    return jax.shard_map(
        per_device, mesh=mesh, in_specs=in_specs, out_specs=out_specs, check_vma=False
    )
```

```python
import functools

import jax
import jax.numpy as jnp
from jax import lax
from jax.experimental import pallas as pl
from jax.experimental.pallas import tpu as pltpu
from jax.sharding import PartitionSpec as P

D = 8192
STATE = 16
PAGE = 128
STEPS = 4
CAP = 2
ROWS = 24
BLOCKS = 16
BROWS = STEPS * ROWS
SLOTS = 64
INNER = 2048
HALF = INNER // 2
FEATS = 512
WIDE = 512
RANK = 512
PAIRS = STEPS * CAP
F32 = jnp.float32
BF16 = jnp.bfloat16
MESH = pl.DeviceIdType.MESH
VMEM_LIMIT = 62 * 1024 * 1024


def rcopy(src, dst, send, recv, dev):
    return pltpu.make_async_remote_copy(
        src_ref=src, dst_ref=dst, send_sem=send, recv_sem=recv, device_id=dev, device_id_type=MESH
    )


def mod4(v):
    return lax.rem(v + 8, 4)


def dot(a, b):
    return jnp.dot(a, b, preferred_element_type=F32)


def greet(devices):
    barrier = pltpu.get_barrier_semaphore()
    for dev in devices:
        pl.semaphore_signal(barrier, inc=1, device_id=dev, device_id_type=MESH)
    pl.semaphore_wait(barrier, len(devices))


def tp_scratch(rows):
    return (
        [pltpu.VMEM((4, 2, rows, FEATS), BF16)] * 2
        + [pltpu.VMEM((4, 2, rows, FEATS), F32)]
        + [pltpu.VMEM((2, rows, FEATS), BF16)] * 6
        + [pltpu.SemaphoreType.DMA((20,)), pltpu.SemaphoreType.DMA((20,))]
    )


TP_SCRATCH = tp_scratch(BROWS)


def tp_partners():
    r, t = lax.axis_index("req"), lax.axis_index("tp")
    y, c = lax.div(t, 2), lax.rem(t, 2)
    return [(r, y * 2 + 1 - c), (r, mod4(y + 1) * 2 + c), (r, mod4(y - 1) * 2 + c)]


def tp_steps(get_all, total, bufs):
    half_s, half_r, part, far_s, far_r, dir_s, dir_r, com_s, com_r, ss, rs = bufs
    t = lax.axis_index("tp")
    y, c = lax.div(t, 2), lax.rem(t, 2)
    core, up, down = tp_partners()
    order = [mod4(y + 2), mod4(y + 1), mod4(y - 1), y]
    sent = []

    def send(src, dst, n, dev):
        copy = rcopy(src, dst, ss.at[n], rs.at[n], dev)
        copy.start()
        sent.append(copy)

    def arrived(ref, n):
        rcopy(ref, ref, ss.at[n], rs.at[n], core).wait_recv()

    def pair(group, yy):
        return pl.ds(2 * (group * 4 + yy), 2)

    get_all([(1 - c) * 4 + yy for yy in order], half_s)
    for k in range(4):
        send(half_s.at[k], half_r.at[k], k, core)
    get_all([c * 4 + yy for yy in order], part)
    for k in range(4):
        arrived(half_r.at[k], k)
        part[k] = part[k] + half_r[k].astype(F32)
        if k == 0:
            far_s[...] = part[0].astype(BF16)
            send(far_s.at[0], far_r.at[0], 4, up)
            send(far_s.at[1], far_r.at[1], 5, down)
        if k == 1:
            dir_s[1] = part[1, 1].astype(BF16)
            send(dir_s.at[1], dir_r.at[1], 7, up)
        if k == 2:
            dir_s[0] = part[2, 0].astype(BF16)
            send(dir_s.at[0], dir_r.at[0], 6, down)
    yield
    arrived(far_r.at[0], 4)
    com_s[0] = (part[1, 0] + far_r[0].astype(F32)).astype(BF16)
    send(com_s.at[0], com_r.at[0], 8, up)
    arrived(far_r.at[1], 5)
    com_s[1] = (part[2, 1] + far_r[1].astype(F32)).astype(BF16)
    send(com_s.at[1], com_r.at[1], 9, down)
    own = 2 * (c * 4 + y)
    for h in range(2):
        arrived(dir_r.at[h], 6 + h)
        arrived(com_r.at[h], 8 + h)
        total[own + h] = (part[3, h] + dir_r[h].astype(F32) + com_r[h].astype(F32)).astype(BF16)
    mine = total.at[pair(c, y)]
    send(mine, mine, 10, up)
    send(mine, mine, 11, down)
    send(mine, mine, 12, core)
    below = total.at[pair(c, mod4(y - 1))]
    above = total.at[pair(c, mod4(y + 1))]
    arrived(below, 10)
    first = total.at[2 * (c * 4 + mod4(y - 1))]
    send(first, first, 13, up)
    send(below, below, 15, core)
    arrived(above, 11)
    second = total.at[2 * (c * 4 + mod4(y + 1)) + 1]
    send(second, second, 14, down)
    send(above, above, 16, core)
    far = 2 * (c * 4 + mod4(y + 2))
    arrived(total.at[far], 13)
    send(total.at[far], total.at[far], 17, core)
    arrived(total.at[far + 1], 14)
    send(total.at[far + 1], total.at[far + 1], 18, core)
    arrived(total.at[pair(1 - c, y)], 12)
    arrived(total.at[pair(1 - c, mod4(y - 1))], 15)
    arrived(total.at[pair(1 - c, mod4(y + 1))], 16)
    other = 2 * ((1 - c) * 4 + mod4(y + 2))
    arrived(total.at[other], 17)
    arrived(total.at[other + 1], 18)
    for copy in sent:
        copy.wait_send()
    yield


def tp_sum(get, total, bufs):
    def get_all(chunks, into):
        for k in range(4):
            into[k] = get(chunks[k]).astype(into.dtype)

    for _ in tp_steps(get_all, total, bufs):
        pass


def shift_req(axis, d):
    r, t = lax.axis_index("req"), lax.axis_index("tp")
    x, z = lax.div(r, 4), lax.rem(r, 4)
    if axis == 0:
        return (mod4(x + d) * 4 + z, t)
    return (x * 4 + mod4(z + d), t)


def req_place(axis):
    r = lax.axis_index("req")
    return lax.div(r, 4) if axis == 0 else lax.rem(r, 4)


def req_partners():
    return [shift_req(axis, d) for axis in (0, 1) for d in (1, -1)]


PROWS = BROWS // 2
FRONT_SCRATCH = (
    [
        pltpu.VMEM((2, BLOCKS, PROWS, FEATS), BF16),
        pltpu.VMEM((2, 4, 4 * PROWS, FEATS), BF16),
        pltpu.VMEM((2, 4, 4 * PROWS, FEATS), BF16),
        pltpu.VMEM((2, 4, 4 * PROWS, PAGE), F32),
    ]
    + [pltpu.VMEM((2, 2, 4, 4 * PROWS, WIDE), BF16)] * 6
    + [pltpu.VMEM((2, 2, 4, PROWS, WIDE), BF16)] * 6
    + [pltpu.VMEM((2, 2, 4, 4, PROWS, WIDE), F32)]
    + [pltpu.SemaphoreType.DMA((2, 6, 2, 4)), pltpu.SemaphoreType.DMA((2, 6, 2, 4))]
    + [pltpu.VMEM((2, 4 * PROWS, PAGE), BF16)] * 6
    + [pltpu.VMEM((2, PROWS, PAGE), BF16)] * 6
    + [pltpu.VMEM((2, 4, PROWS, PAGE), F32)]
    + [pltpu.SemaphoreType.DMA((2, 6)), pltpu.SemaphoreType.DMA((2, 6))]
)


class ScatterSum:
    def __init__(self, axis, d, partial, bufs, total, ss, rs):
        self.axes = (axis, 1 - axis)
        self.d = d
        self.partial = partial
        self.far_s, self.far_r, self.dir_s, self.dir_r, self.com_s, self.com_r = bufs[:6]
        self.far2_s, self.far2_r, self.dir2_s, self.dir2_r, self.com2_s, self.com2_r = bufs[6:]
        self.total = total
        self.ss, self.rs = ss, rs

    def copy(self, n):
        src = (self.far_s, self.dir_s, self.com_s, self.far2_s, self.dir2_s, self.com2_s)[n]
        dst = (self.far_r, self.dir_r, self.com_r, self.far2_r, self.dir2_r, self.com2_r)[n]
        d = -self.d if n % 3 == 1 else self.d
        return rcopy(src, dst, self.ss(n), self.rs(n), shift_req(self.axes[n // 3], d))

    def far(self):
        p = req_place(self.axes[0])
        self.far_s[...] = self.partial(mod4(p + 2)).astype(BF16)
        self.copy(0).start()

    def direct(self):
        p = req_place(self.axes[0])
        self.dir_s[...] = self.partial(mod4(p - self.d)).astype(BF16)
        self.copy(1).start()

    def combined(self):
        p = req_place(self.axes[0])
        mine = self.partial(mod4(p + self.d))
        self.copy(0).wait_recv()
        self.com_s[...] = (mine + self.far_r[...].astype(F32)).astype(BF16)
        self.copy(2).start()

    def own(self):
        p, q = req_place(self.axes[0]), req_place(self.axes[1])
        mine = self.partial(p)
        self.copy(1).wait_recv()
        self.copy(2).wait_recv()
        mine = mine + self.dir_r[...].astype(F32) + self.com_r[...].astype(F32)
        self.total[...] = mine.reshape(4, PROWS, mine.shape[1])
        self.far2_s[...] = self.total[mod4(q + 2)].astype(BF16)
        self.copy(3).start()
        self.dir2_s[...] = self.total[mod4(q - self.d)].astype(BF16)
        self.copy(4).start()

    def combined2(self):
        q = req_place(self.axes[1])
        self.copy(3).wait_recv()
        self.com2_s[...] = (self.total[mod4(q + self.d)] + self.far2_r[...].astype(F32)).astype(
            BF16
        )
        self.copy(5).start()

    def result(self):
        q = req_place(self.axes[1])
        self.copy(4).wait_recv()
        self.copy(5).wait_recv()
        return self.total[q] + self.dir2_r[...].astype(F32) + self.com2_r[...].astype(F32)

    def drain(self):
        for n in range(6):
            self.copy(n).wait_send()


class Front:
    def __init__(self, g, refs, out, tp_bufs, rest):
        self.g, self.out, self.tp_bufs = g, out, tp_bufs
        self.ids, self.emb, self.gain, self.w_inner, self.w_gate = refs
        self.embedded, self.lhs_x, self.lhs_z, self.squares = (ref.at[g] for ref in rest[:4])
        self.big = [ref.at[g] for ref in rest[4:17]]
        self.big_ss, self.big_rs = rest[17:19]
        small = [ref.at[g] for ref in rest[19:32]]
        small_ss, small_rs = rest[32:34]
        self.norm = ScatterSum(
            0, 1, lambda chunk: self.squares[chunk], small[:12], small[12],
            lambda n: small_ss.at[g, n], lambda n: small_rs.at[g, n],
        )

    def looked(self, chunks, into):
        emb = self.emb
        want = jnp.concatenate(
            [self.ids[self.g, pl.ds(2 * ch, 2)].reshape(2 * PROWS, 1) for ch in chunks], axis=0
        )
        span = 1024
        acc = jnp.zeros((8 * PROWS, FEATS), F32)
        for k in range(emb.shape[0] // span):
            lane = lax.broadcasted_iota(jnp.int32, (8 * PROWS, span), 1) + k * span
            hot = jnp.where(lane == want, 1.0, 0.0).astype(BF16)
            acc = acc + dot(hot, emb[k * span : (k + 1) * span, :])
        into[...] = acc.reshape(4, 2, PROWS, FEATS).astype(into.dtype)

    def lookup(self):
        return tp_steps(self.looked, self.embedded, self.tp_bufs)

    def spread(self):
        def body(b, carry):
            x, z = lax.div(b, 4), lax.rem(b, 4)
            rows = self.embedded[b].astype(F32)
            scaled = (rows * self.gain[...]).astype(BF16)
            along_z = pl.ds(pl.multiple_of(z * PROWS, PROWS), PROWS)
            along_x = pl.ds(pl.multiple_of(x * PROWS, PROWS), PROWS)
            self.lhs_x[x, along_z, :] = scaled
            self.lhs_z[z, along_x, :] = scaled
            self.squares[x, along_z, :] = jnp.broadcast_to(
                jnp.sum(rows * rows, axis=1, keepdims=True), (PROWS, PAGE)
            )
            return carry

        lax.fori_loop(0, BLOCKS, body, 0)

    def unit(self, ab, u):
        lhs, weight = ((self.lhs_x, self.w_inner), (self.lhs_z, self.w_gate))[ab]
        g = self.g

        def partial(chunk):
            cols = pl.ds(pl.multiple_of(u * WIDE, WIDE), WIDE)
            return dot(lhs[chunk], weight[:, cols])

        views = [ref.at[ab, u] for ref in self.big[:12]]
        return ScatterSum(
            ab, 1 - 2 * lax.rem(u, 2), partial, views, self.big[12].at[ab, u],
            lambda n: self.big_ss.at[g, n, ab, u], lambda n: self.big_rs.at[g, n, ab, u],
        )

    def each(self, step):
        step(self.norm)

        def body(u, carry):
            for ab in range(2):
                step(self.unit(ab, u))
            return carry

        lax.fori_loop(0, 4, body, 0)

    def finish(self):
        inv_rms = lax.rsqrt(self.norm.result()[:, :1] / D + 1e-05)

        def body(u, carry):
            for ab in range(2):
                cols = pl.ds(pl.multiple_of((ab * 4 + u) * WIDE, WIDE), WIDE)
                rows = slice(self.g * PROWS, (self.g + 1) * PROWS)
                self.out[rows, cols] = self.unit(ab, u).result() * inv_rms
            return carry

        lax.fori_loop(0, 4, body, 0)


PLAN, FIRST, SECOND, LAST, SIDE1, SIDE2, WHICH = 24, 0, 4, 8, 9, 13, 17
GROUP = 4 * BROWS
MOST = 32


def make_plan(events, plan):
    r = lax.axis_index("req")
    shape = (GROUP, 128)
    lane = lax.broadcasted_iota(jnp.int32, shape, 1)
    number = lax.broadcasted_iota(jnp.int32, shape, 0)
    kind, quarter = lax.rem(lane, 4), lax.div(lane, 4)
    block = lax.div(number, BROWS)
    row = lax.broadcasted_iota(jnp.int32, (GROUP, GROUP), 0)
    col = lax.broadcasted_iota(jnp.int32, (GROUP, GROUP), 1)
    earlier = col < row
    near = earlier & (lax.div(col, BROWS) == lax.div(row, BROWS))
    earlier = jnp.where(earlier, 1.0, 0.0).astype(BF16)
    near = jnp.where(near, 1.0, 0.0).astype(BF16)

    def ahead(which, mask):
        return dot(which, jnp.where(mask, 1.0, 0.0).astype(BF16)).astype(jnp.int32)

    def parts(packed):
        packed = jnp.broadcast_to(packed, shape)
        owner = jnp.bitwise_and(jnp.right_shift(packed, 6), 15)
        return packed >= 4096, owner, jnp.bitwise_and(packed, 63)

    def fold(mask, value):
        return jnp.sum(jnp.where(mask, value + 1, 0), axis=0, keepdims=True) - 1

    plan[...] = jnp.zeros_like(plan)
    need1 = jnp.zeros((1, 128), jnp.int32)
    need2 = jnp.zeros((1, 128), jnp.int32)
    for h in range(2):
        p_me, q_me = req_place(h), req_place(1 - h)
        done, owner, _ = parts(events[h, q_me])
        p_of = lax.div(owner, 4) if h == 0 else lax.rem(owner, 4)
        q_of = lax.rem(owner, 4) if h == 0 else lax.div(owner, 4)
        mask1 = done & (p_of == lane)
        rank1 = ahead(near, mask1)
        mask2 = done & (p_of == p_me) & (q_of == lane)
        rank2 = ahead(earlier, mask2)
        here = jnp.sum(jnp.where(lane == p_me, rank1, 0), axis=1, keepdims=True)
        at = block * MOST + here
        mine = block == p_me
        event = number - p_me * BROWS
        base = PLAN * h
        for d in range(4):
            rank = jnp.broadcast_to(rank1[:, d : d + 1], shape)
            mask = mine & done & (p_of == d)
            plan[base + FIRST + d : base + FIRST + d + 1, :] = fold(mask & (rank == lane), event)
            plan[base + SIDE1 + d : base + SIDE1 + d + 1, :] = fold(
                mask & (rank == quarter), kind * BROWS + event
            )
            rank = jnp.broadcast_to(rank2[:, d : d + 1], shape)
            mask = done & (p_of == p_me) & (q_of == d)
            plan[base + SECOND + d : base + SECOND + d + 1, :] = fold(mask & (rank == lane), at)
            plan[base + SIDE2 + d : base + SIDE2 + d + 1, :] = fold(
                mask & (rank == quarter), at * 4 + kind
            )
        found = jnp.zeros((1, 128), jnp.int32)
        for q in range(4):
            done, owner, slot = parts(events[h, q])
            mask = done & (owner == r)
            value = q * MOST + ahead(earlier, mask)
            found = found + fold(mask & (slot == lane), value) + 1
            p_of = lax.div(owner, 4) if h == 0 else lax.rem(owner, 4)
            leaving = jnp.where(done & (p_of == lane), 1, 0).reshape(4, BROWS, 128)
            for n in range(4):
                need1 = jnp.maximum(need1, jnp.sum(leaving[n], axis=0, keepdims=True))
            staying = jnp.where(done & (owner == lane), 1, 0)
            need2 = jnp.maximum(need2, jnp.sum(staying, axis=0, keepdims=True))
        plan[base + LAST : base + LAST + 1, :] = found - 1
    need1 = jnp.max(need1, axis=1, keepdims=True)
    need2 = jnp.max(need2, axis=1, keepdims=True)
    which = jnp.full((1, 1), len(SAVE_COUNTS) - 1, jnp.int32)
    for n in range(len(SAVE_COUNTS) - 1):
        few, many = SAVE_COUNTS[n]
        which = jnp.where((need1 <= few) & (need2 <= many), n, which)
    plan[WHICH : WHICH + 1, :] = jnp.broadcast_to(which, (1, 128))


TP_PAIR = tp_scratch(PROWS)


def front_kernel(ids, emb, gain, inner_hbm, gate_hbm, events, out, plan, *scratch):
    cut = len(TP_PAIR)
    w_inner, w_gate, load_sems = scratch[-3:]
    refs = (ids, emb, gain, w_inner, w_gate)
    loads = [
        pltpu.make_async_copy(inner_hbm, w_inner, load_sems.at[0]),
        pltpu.make_async_copy(gate_hbm, w_gate, load_sems.at[1]),
    ]
    for load in loads:
        load.start()
    one, two = (
        Front(g, refs, out, scratch[g * cut : (g + 1) * cut], scratch[2 * cut :]) for g in range(2)
    )
    greet(tp_partners() + req_partners())
    for _ in one.lookup():
        pass
    one.spread()
    for load in loads:
        load.wait()
    one.each(lambda s: s.far())
    one.each(lambda s: s.direct())
    lookup = two.lookup()
    next(lookup)
    one.each(lambda s: s.combined())
    next(lookup)
    two.spread()
    two.each(lambda s: s.far())
    one.each(lambda s: s.own())
    two.each(lambda s: s.direct())
    one.each(lambda s: s.combined2())
    make_plan(events, plan)
    two.each(lambda s: s.combined())
    one.finish()
    two.each(lambda s: s.own())
    two.each(lambda s: s.combined2())
    two.finish()
    one.each(lambda s: s.drain())
    two.each(lambda s: s.drain())


def vmem_call(kernel, out_shape, n_in, scratch, in_hbm=(), **params):
    spec = pl.BlockSpec(memory_space=pltpu.VMEM)
    hbm = pl.BlockSpec(memory_space=pl.ANY)
    return pl.pallas_call(
        kernel,
        out_shape=out_shape,
        in_specs=[hbm if n in in_hbm else spec for n in range(n_in)],
        out_specs=jax.tree.map(lambda _: spec, out_shape),
        scratch_shapes=scratch,
        compiler_params=pltpu.CompilerParams(vmem_limit_bytes=VMEM_LIMIT, **params),
    )


def silu(v):
    return v / (1.0 + jnp.exp(-v))


RCOLS = RANK + 128


def rank_kernel(
    sums, conv, taps, bias, w_low, w_select, w_dt, dt_bias, step, activ, select,
    pair_s, pair_r, quad_s, quad_r, full, ss, rs, loads,
):
    r, t = lax.axis_index("req"), lax.axis_index("tp")
    y, c = lax.div(t, 2), lax.rem(t, 2)
    core = (r, y * 2 + 1 - c)
    others = [(r, mod4(y + d) * 2 + c) for d in (1, 2, 3)]
    greet([core] + others)
    for n in range(STEPS):
        total = bias[...] + jnp.zeros((ROWS, INNER), F32)
        for k in range(4):
            at = n + k
            if at < 3:
                row = conv[at].astype(F32)
            else:
                row = sums[(at - 3) * ROWS : (at - 2) * ROWS, :INNER].astype(BF16).astype(F32)
            total = total + row * taps[k : k + 1, :]
        activ[n * ROWS : (n + 1) * ROWS, :] = silu(total).astype(BF16).astype(F32)
    act = activ[...].astype(BF16)
    loads[0].wait()
    low = dot(act, w_low[...]).reshape(2, BROWS // 2, RANK)
    sel = lax.dot_general(
        act, w_select[...], (((1,), (1,)), ((), ())), preferred_element_type=F32
    )
    sel = jnp.concatenate([sel, jnp.zeros((BROWS, 128 - 2 * STATE), F32)], axis=1)
    sel = sel.reshape(2, BROWS // 2, 128)
    pair_s[:, :, :RANK] = low
    pair_s[:, :, RANK:] = sel
    swap = rcopy(pair_s, pair_r, ss.at[0], rs.at[0], core)
    swap.start()
    swap.wait_recv()
    chip = pair_s[c] + pair_r[c]
    quad_s[...] = chip.astype(BF16)
    copies = [rcopy(quad_s, quad_r.at[n], ss.at[1 + n], rs.at[1 + n], others[n]) for n in range(3)]
    for copy in copies:
        copy.start()
    acc = quad_s[...].astype(F32)
    for n in range(3):
        copies[n].wait_recv()
        acc = acc + quad_r[n].astype(F32)
    full[c] = acc
    back = rcopy(full.at[c], full.at[c], ss.at[4], rs.at[4], core)
    back.start()
    rcopy(full.at[1 - c], full.at[1 - c], ss.at[4], rs.at[4], core).wait_recv()
    low_rank = full[:, :, :RANK].reshape(BROWS, RANK).astype(BF16)
    select[...] = full[:, :, RANK:].reshape(BROWS, 128)
    loads[1].wait()
    v = dot(low_rank, w_dt[...]) + dt_bias[...]
    step[...] = jnp.maximum(v, 0.0) + jnp.log1p(jnp.exp(-jnp.abs(v)))
    swap.wait_send()
    for copy in copies:
        copy.wait_send()
    back.wait_send()


def state_kernel(
    codes, scales, step, activ, select, sums, conv, decay_log, skip,
    gated, final, new_codes, source, last_window, output, scale_rows, rates,
):
    lane = lax.broadcasted_iota(jnp.int32, (STATE, 128), 1)
    row_of = lax.broadcasted_iota(jnp.int32, (STATE, 128), 0)
    page_lane = lax.broadcasted_iota(jnp.int32, (1, 128), 1)
    width = 4 * PAGE

    def request(i, carry):
        b_in, c_out = [], []
        for n in range(STEPS):
            row = select[pl.ds(n * ROWS + i, 1), :]
            b_in.append(jnp.sum(jnp.where(lane == row_of, row, 0.0), axis=1, keepdims=True))
            c_out.append(
                jnp.sum(jnp.where(lane == row_of + STATE, row, 0.0), axis=1, keepdims=True)
            )
        kept = [jnp.zeros((1, 128), F32) for _ in range(STEPS)]
        for part in range(INNER // width):
            cols = slice(part * width, (part + 1) * width)
            rate = rates[:, cols]
            current = codes[i, :, cols].astype(F32) * scales[pl.ds(i, 1), cols]
            for n in range(STEPS):
                at = n * ROWS + i
                dt = step[pl.ds(at, 1), cols]
                act = activ[pl.ds(at, 1), cols]
                current = jnp.exp2(dt * rate) * current + (dt * act) * b_in[n]
                output[pl.ds(at, 1), cols] = jnp.sum(current * c_out[n], axis=0, keepdims=True)
                peak = jnp.max(jnp.abs(current), axis=0, keepdims=True)
                for page in range(4):
                    here = slice(page * PAGE, (page + 1) * PAGE)
                    top = jnp.max(peak[:, here], axis=1, keepdims=True)
                    scale = (top + 1e-06).astype(BF16).astype(F32)
                    kept[n] = jnp.where(page_lane == part * 4 + page, scale, kept[n])
                    new_codes[at, :, part * width + page * PAGE : part * width + (page + 1) * PAGE] = (
                        current[:, here] * (1.0 / scale)
                    ).astype(BF16)
        for n in range(STEPS):
            scale_rows[pl.ds(n * ROWS + i, 1), :] = kept[n]
        final[i] = new_codes[(STEPS - 1) * ROWS + i]
        return carry

    rates[...] = -jnp.exp(decay_log[...]) * 1.4426950408889634
    lax.fori_loop(0, ROWS, request, 0)
    gated[...] = (
        (output[...] + skip[...] * activ[...]) * silu(sums[:, INNER:])
    ).astype(BF16)
    rows = [conv[k].astype(F32) for k in range(3)]
    rows += [sums[n * ROWS : (n + 1) * ROWS, :INNER] for n in range(STEPS)]
    for k in range(3):
        source[k * BROWS : (k + 1) * BROWS, :] = jnp.concatenate(
            rows[k + 1 : k + 1 + STEPS], axis=0
        ).astype(BF16)
        last_window[k] = rows[STEPS + k].astype(BF16)
    source[3 * BROWS :, :] = jnp.zeros((BROWS, INNER), BF16)
    source[3 * BROWS :, :128] = scale_rows[...].astype(BF16)


def middle_kernel(
    sums, conv, taps, bias, low_hbm, w_select, dt_hbm, dt_bias, codes_hbm, scales, decay_log, skip,
    gated, final, new_codes, source, last_window, step, activ, select, output, scale_rows, rates,
    *rest,
):
    *rest, w_low, w_dt, codes, load_sems = rest
    loads = [
        pltpu.make_async_copy(src, dst, load_sems.at[n])
        for n, (src, dst) in enumerate(((low_hbm, w_low), (dt_hbm, w_dt), (codes_hbm, codes)))
    ]
    for load in loads:
        load.start()
    rank_kernel(
        sums, conv, taps, bias, w_low, w_select, w_dt, dt_bias, step, activ, select, *rest,
        loads,
    )
    loads[2].wait()
    state_kernel(
        codes, scales, step, activ, select, sums, conv, decay_log, skip,
        gated, final, new_codes, source, last_window, output, scale_rows, rates,
    )


BACK_SCRATCH = [
    pltpu.VMEM((BLOCKS, BROWS, INNER // 2), BF16),
    pltpu.VMEM((BLOCKS, BROWS, INNER // 2), BF16),
    pltpu.VMEM((BLOCKS, BROWS, FEATS), F32),
    pltpu.SemaphoreType.DMA((2, 16)),
    pltpu.SemaphoreType.DMA((2, 16)),
]


class Gather:
    def __init__(self, axis, buf, ss, rs):
        self.axes = (axis, 1 - axis)
        self.buf, self.ss, self.rs = buf, ss, rs
        self.q, self.p = req_place(axis), req_place(1 - axis)
        self.order = [self.q, mod4(self.q - 1), mod4(self.q + 1), mod4(self.q + 2)]
        self.sent = []

    def send(self, ref, n, axis, d):
        copy = rcopy(ref, ref, self.ss.at[n], self.rs.at[n], shift_req(axis, d))
        copy.start()
        self.sent.append(copy)

    def arrived(self, ref, n):
        rcopy(ref, ref, self.ss.at[n], self.rs.at[n], shift_req(self.axes[0], 1)).wait_recv()

    def block(self, p, q):
        return self.buf.at[p * 4 + q]

    def rows(self, p, q, h):
        return self.buf.at[p * 4 + q, pl.ds(h * (BROWS // 2), BROWS // 2)]

    def start(self):
        mine = self.block(self.p, self.q)
        self.send(mine, 0, self.axes[0], 1)
        self.send(mine, 1, self.axes[0], -1)
        self.spread(0)

    def spread(self, k):
        block = self.block(self.p, self.order[k])
        self.send(block, 4 + k, self.axes[1], 1)
        self.send(block, 8 + k, self.axes[1], -1)

    def near(self):
        self.arrived(self.block(self.p, self.order[1]), 0)
        self.send(self.rows(self.p, self.order[1], 0), 2, self.axes[0], 1)
        self.spread(1)
        self.arrived(self.block(self.p, self.order[2]), 1)
        self.send(self.rows(self.p, self.order[2], 1), 3, self.axes[0], -1)
        self.spread(2)

    def last(self):
        self.arrived(self.rows(self.p, self.order[3], 0), 2)
        self.arrived(self.rows(self.p, self.order[3], 1), 3)
        self.spread(3)

    def relay(self, k):
        below, above = mod4(self.p - 1), mod4(self.p + 1)
        self.arrived(self.block(below, self.order[k]), 4 + k)
        if k < 2:
            self.send(self.block(below, self.order[k]), 12 + k, self.axes[1], 1)
        self.arrived(self.block(above, self.order[k]), 8 + k)
        if k >= 2:
            self.send(self.block(above, self.order[k]), 12 + k, self.axes[1], -1)

    def end(self, k):
        self.arrived(self.block(mod4(self.p + 2), self.order[k]), 12 + k)

    def drain(self):
        for copy in self.sent:
            copy.wait_send()


class Project:
    def __init__(self, gated, w_out, scratch):
        self.tp_bufs, rest = scratch[: len(TP_SCRATCH)], scratch[len(TP_SCRATCH) :]
        self.buf_a, self.buf_b, self.acc, gss, grs = rest
        self.gated, self.w_out = gated, w_out
        self.parts = [
            Gather(1, self.buf_a, gss.at[0], grs.at[0]),
            Gather(0, self.buf_b, gss.at[1], grs.at[1]),
        ]

    def start(self):
        r = lax.axis_index("req")
        self.acc[...] = jnp.zeros_like(self.acc)
        self.buf_a[r] = self.gated[:, :HALF]
        self.buf_b[lax.rem(r, 4) * 4 + lax.div(r, 4)] = self.gated[:, HALF:]
        for part in self.parts:
            part.start()

    def project(self, n, p, k):
        q = self.parts[n].order[k]
        if n == 0:
            self.acc[p * 4 + q] += dot(self.buf_a[p * 4 + q], self.w_out[:HALF, :])
        else:
            self.acc[q * 4 + p] += dot(self.buf_b[p * 4 + q], self.w_out[HALF:, :])

    def gather(self):
        parts = self.parts
        for part in parts:
            part.near()
        for part in parts:
            part.last()
        for k in range(4):
            for n in range(2):
                self.project(n, parts[n].p, k)
        for k in range(4):
            for part in parts:
                part.relay(k)
            for n in range(2):
                self.project(n, mod4(parts[n].p - 1), k)
                self.project(n, mod4(parts[n].p + 1), k)
        for k in range(4):
            for n in range(2):
                parts[n].end(k)
                self.project(n, mod4(parts[n].p + 2), k)

    def total(self, mixed):
        tp_sum(lambda ch: self.acc[pl.ds(2 * ch, 2)], mixed, self.tp_bufs)
        for part in self.parts:
            part.drain()


def project_kernel(gated, w_out, mixed, *scratch):
    greet(tp_partners() + req_partners())
    work = Project(gated, w_out, scratch)
    work.start()
    work.gather()
    work.total(mixed)


FAR = (2, 1, 3)


def save_scratch(room):
    return [
        pltpu.VMEM((2, 4 * room, STATE, HALF), BF16),
        pltpu.VMEM((2, 4 * room, STATE, HALF), BF16),
        pltpu.VMEM((2, 4 * room, STATE, HALF), BF16),
        pltpu.VMEM((2, 16 * room, HALF), BF16),
        pltpu.VMEM((2, 16 * room, HALF), BF16),
        pltpu.VMEM((2, 16 * room, HALF), BF16),
        pltpu.SemaphoreType.DMA((2, 2, 3, 2)),
        pltpu.SemaphoreType.DMA((2, 2, 3, 2)),
    ]


class Save:
    def __init__(self, counts, room, index, plan, codes, source, scratch):
        self.counts, self.room = counts, room
        self.index, self.plan = index, plan
        self.codes, self.source = codes, source
        self.sent, self.got1, self.got2, self.side, self.side1, self.side2, self.ss, self.rs = (
            scratch
        )

    def clear(self):
        self.side1[...] = jnp.zeros_like(self.side1)
        self.side2[...] = jnp.zeros_like(self.side2)

    def pick(self, want, rows):
        span = rows.shape[0]
        if self.room != MOST and span != self.source.shape[0]:
            row = lax.div(want, 4 * MOST) * (4 * self.room) + lax.rem(want, 4 * MOST)
            want = jnp.where(want >= 0, row, -1)
        number = lax.broadcasted_iota(jnp.int32, (span, 128), 0)
        hot = jnp.where(number == want, 1.0, 0.0).astype(BF16)
        picked = lax.dot_general(hot, rows, (((0,), (0,)), ((), ())), preferred_element_type=F32)
        return picked.astype(BF16)

    def place_of(self, at):
        at = jnp.maximum(at, 0)
        return lax.div(at, MOST) * self.room + lax.rem(at, MOST)

    def buffers(self, n):
        return ((self.got1, self.side1), (self.got2, self.side2))[n]

    def axis(self, n, h):
        return h if n == 0 else 1 - h

    def rows(self, ref, h, block, each):
        count = each * self.room
        return lambda used: ref.at[h, pl.ds(pl.multiple_of(block * count, 16 if each > 1 else 4), used)]

    def used(self, n):
        return self.counts[n], -(-4 * self.counts[n] // 16) * 16

    def copy(self, n, h, k, i):
        d = FAR[k]
        here = req_place(self.axis(n, h))
        dest, dev = mod4(here + d), shift_req(self.axis(n, h), d)
        src, dst = ((self.sent, self.side)[i], self.buffers(n)[i])
        each, used = (1, 4)[i], self.used(n)[i]
        return rcopy(
            self.rows(src, h, dest, each)(used), self.rows(dst, h, here, each)(used),
            self.ss.at[n, h, k, i], self.rs.at[n, h, k, i], dev,
        )

    def send(self, n):
        into, side_into = self.buffers(n)
        room, many = self.room, self.used(n)[1]
        order = [(k, d, h) for k, d in enumerate(FAR + (0,)) for h in range(2)]
        for k, d, h in order:
            dest = mod4(req_place(self.axis(n, h)) + d)
            keep = into if d == 0 else self.sent

            def pack(m, carry):
                at = self.index[PLAN * h + (FIRST, SECOND)[n] + dest, m]
                if n == 0:
                    row = self.codes[jnp.maximum(at, 0), :, h * HALF : (h + 1) * HALF]
                else:
                    row = self.got1[h, self.place_of(at)]
                keep[h, dest * room + m] = row
                return carry

            lax.fori_loop(0, self.counts[n], pack, 0)
            if d != 0:
                self.copy(n, h, k, 0).start()
        for k, d, h in order:
            dest = mod4(req_place(self.axis(n, h)) + d)
            keep = side_into if d == 0 else self.side
            rows = self.source[:, h * HALF : (h + 1) * HALF] if n == 0 else self.side1[h]
            want = self.plan[pl.ds(PLAN * h + (SIDE1, SIDE2)[n] + dest, 1), :]
            block = pl.ds(pl.multiple_of(dest * 4 * room, 16), many)
            keep[h, block, :] = self.pick(want, rows)[:many]
            if d != 0:
                self.copy(n, h, k, 1).start()

    def receive(self, n):
        into, side_into = self.buffers(n)
        few, many = self.used(n)
        for k, d in enumerate(FAR):
            for h in range(2):
                origin = mod4(req_place(self.axis(n, h)) - d)
                dev = shift_req(self.axis(n, h), d)
                for i, (ref, each, used) in enumerate(((into, 1, few), (side_into, 4, many))):
                    block = self.rows(ref, h, origin, each)(used)
                    rcopy(
                        block, block, self.ss.at[n, h, k, i], self.rs.at[n, h, k, i], dev
                    ).wait_recv()
        for k in range(3):
            for h in range(2):
                for i in range(2):
                    self.copy(n, h, k, i).wait_send()

    def place(self, out, windows, scale):
        def one(s, carry):
            for h in range(2):
                at = self.index[PLAN * h + LAST, s]
                row = self.got2[h, self.place_of(at)]
                out[s, :, h * HALF : (h + 1) * HALF] = jnp.where(at >= 0, row, jnp.zeros_like(row))
            return carry

        lax.fori_loop(0, SLOTS, one, 0)
        for h in range(2):
            at = self.plan[PLAN * h + LAST : PLAN * h + LAST + 1, :]
            for k in range(3):
                want = jnp.where(at >= 0, at * 4 + k, -1)
                windows[k, :, h * HALF : (h + 1) * HALF] = self.pick(want, self.side2[h])[:SLOTS]
            if h == 0:
                want = jnp.where(at >= 0, at * 4 + 3, -1)
                scale[...] = self.pick(want, self.side2[0, :, :128])[:SLOTS]


def save_partners():
    return [shift_req(axis, d) for axis in (0, 1) for d in FAR]


def save_kernel(
    counts, index, plan, codes, source, out, windows, scale, *scratch
):
    work = Save(counts, MOST, index, plan, codes, source, scratch)
    work.clear()
    greet(save_partners())
    work.send(0)
    work.receive(0)
    work.send(1)
    work.receive(1)
    work.place(out, windows, scale)


def both_kernel(
    counts, index, plan, codes_hbm, source, gated, out_hbm, mixed, out, windows, scale, *scratch,
):
    cut = len(TP_SCRATCH) + len(BACK_SCRATCH)
    *scratch, codes, w_out, load_sems = scratch
    loads = [
        pltpu.make_async_copy(codes_hbm, codes, load_sems.at[0]),
        pltpu.make_async_copy(out_hbm, w_out, load_sems.at[1]),
    ]
    for load in loads:
        load.start()
    project = Project(gated, w_out, scratch[:cut])
    save = Save(counts, ROOM, index, plan, codes, source, scratch[cut:])
    save.clear()
    greet(tp_partners() + save_partners())
    project.start()
    for load in loads:
        load.wait()
    save.send(0)
    project.gather()
    save.receive(0)
    save.send(1)
    project.total(mixed)
    save.receive(1)
    save.place(out, windows, scale)


ROOM = 28
SAVE_COUNTS = ((24, 26), (20, 24), (MOST, MOST))


def pack_events(finish, holder, slot_index):
    packed = finish * 4096 + jnp.bitwise_and(holder, 15) * 64 + jnp.bitwise_and(slot_index, 63)
    packed = packed.reshape(STEPS, 4, 4, ROWS).transpose(2, 1, 0, 3)
    both = jnp.stack([packed, packed.transpose(1, 0, 2, 3)])
    return both.reshape(2, 4, GROUP, 1)


def per_device(
    tokens, finish, holder, slot_index, embedding, norm_gain, proj_inner, proj_gate, conv_weight,
    conv_bias, proj_low, proj_select, proj_dt, dt_bias, decay_log, skip_gain, proj_out, state_codes,
    state_scales, conv_state,
):
    ids = tokens.reshape(2, 2, BLOCKS, ROWS).transpose(0, 2, 1, 3).reshape(2, BLOCKS, PROWS, 1)
    ids = ids - lax.axis_index("tp") * embedding.shape[0]
    conv = conv_state.transpose(1, 0, 2)
    scales = jnp.repeat(state_scales.astype(F32), PAGE, axis=1)
    shape = jax.ShapeDtypeStruct
    sums, plan = vmem_call(
        front_kernel,
        [shape((BROWS, 2 * INNER), F32), shape((2 * PLAN, 128), jnp.int32)], 6,
        TP_PAIR * 2
        + list(FRONT_SCRATCH)
        + [pltpu.VMEM((FEATS, INNER), BF16)] * 2
        + [pltpu.SemaphoreType.DMA((2,))],
        in_hbm=(3, 4), collective_id=0, has_side_effects=True,
    )(
        ids, embedding, norm_gain.reshape(1, -1), proj_inner, proj_gate,
        pack_events(finish, holder, slot_index),
    )
    half = BROWS // 2
    vmem = pl.BlockSpec(memory_space=pltpu.VMEM)
    smem = pl.BlockSpec(memory_space=pltpu.SMEM)
    gated, final, new_codes, source, last_window = vmem_call(
        middle_kernel,
        [
            shape((BROWS, INNER), BF16),
            shape((ROWS, STATE, INNER), BF16),
            shape((BROWS, STATE, INNER), BF16),
            shape((4 * BROWS, INNER), BF16),
            shape((3, ROWS, INNER), BF16),
        ],
        12,
        [
            pltpu.VMEM((BROWS, INNER), F32),
            pltpu.VMEM((BROWS, INNER), F32),
            pltpu.VMEM((BROWS, 128), F32),
            pltpu.VMEM((BROWS, INNER), F32),
            pltpu.VMEM((BROWS, 128), F32),
            pltpu.VMEM((STATE, INNER), F32),
            pltpu.VMEM((2, half, RCOLS), F32),
            pltpu.VMEM((2, half, RCOLS), F32),
            pltpu.VMEM((half, RCOLS), BF16),
            pltpu.VMEM((3, half, RCOLS), BF16),
            pltpu.VMEM((2, half, RCOLS), F32),
            pltpu.SemaphoreType.DMA((5,)),
            pltpu.SemaphoreType.DMA((5,)),
            pltpu.VMEM((INNER, RANK), BF16),
            pltpu.VMEM((RANK, INNER), BF16),
            pltpu.VMEM((ROWS, STATE, INNER), BF16),
            pltpu.SemaphoreType.DMA((3,)),
        ],
        in_hbm=(4, 6, 8),
        collective_id=1, has_side_effects=True,
    )(
        sums, conv, conv_weight, conv_bias.reshape(1, -1), proj_low, proj_select, proj_dt,
        dt_bias.reshape(1, -1), state_codes, scales, decay_log, skip_gain.reshape(1, -1),
    )
    saved = [shape((SLOTS, STATE, INNER), BF16)] + [shape((3, SLOTS, INNER), BF16)] + [
        shape((SLOTS, 128), BF16)
    ]
    mixed_shape = shape((BLOCKS, BROWS, FEATS), BF16)
    back_scratch = TP_SCRATCH + BACK_SCRATCH

    def call(kernel, results, operands, scratch, number, in_hbm=()):
        return pl.pallas_call(
            kernel,
            out_shape=results,
            in_specs=[smem]
            + [
                pl.BlockSpec(memory_space=pl.ANY) if n in in_hbm else vmem
                for n in range(1, len(operands))
            ],
            out_specs=[vmem] * len(results),
            scratch_shapes=scratch,
            compiler_params=pltpu.CompilerParams(
                vmem_limit_bytes=VMEM_LIMIT, collective_id=number, has_side_effects=True
            ),
        )(*operands)

    def together(n):
        def run(*operands):
            return tuple(
                call(
                    functools.partial(both_kernel, SAVE_COUNTS[n]), [mixed_shape] + saved,
                    operands,
                    back_scratch
                    + save_scratch(ROOM)
                    + [
                        pltpu.VMEM((BROWS, STATE, INNER), BF16),
                        pltpu.VMEM((INNER, FEATS), BF16),
                        pltpu.SemaphoreType.DMA((2,)),
                    ],
                    3 + n, (2, 5),
                )
            )

        return run

    def apart(*operands):
        mixed = vmem_call(
            project_kernel, mixed_shape, 2, back_scratch, collective_id=2, has_side_effects=True
        )(*operands[4:])
        rest = call(
            functools.partial(save_kernel, SAVE_COUNTS[2]), saved, operands[:4],
            save_scratch(MOST), 5,
        )
        return tuple([mixed, *rest])

    mixed, cache_codes, windows, cache_scales = lax.switch(
        plan[WHICH, 0], [together(0), together(1), apart], plan, plan, new_codes, source, gated, proj_out,
    )
    mixed = mixed.reshape(BLOCKS, STEPS, ROWS, FEATS).transpose(1, 0, 2, 3)
    mixed = mixed.reshape(STEPS, BLOCKS * ROWS, FEATS)
    last = slice((STEPS - 1) * ROWS, BROWS)
    pages = INNER // PAGE
    next_scales = source[3 * BROWS :][last, :pages]
    next_window = last_window.transpose(1, 0, 2)
    cache_window = windows.transpose(1, 0, 2)
    return (
        mixed, final, next_scales, next_window, cache_codes, cache_scales[:, :pages], cache_window,
    )


def solution(mesh):
    in_specs = (
        P(), P(), P(), P(), P("tp", "req"), P("req"), P("req", "tp"), P("req", "tp"),
        P(None, "tp"), P("tp"), P("tp", None), P(None, "tp"), P(None, "tp"), P("tp"),
        P(None, "tp"), P("tp"), P("tp", "req"), P("req", None, "tp"), P("req", "tp"),
        P("req", None, "tp"),
    )
    out_specs = (
        P(None, None, "req"), P("req", None, "tp"), P("req", "tp"), P("req", None, "tp"),
        P("req", None, "tp"), P("req", "tp"), P("req", None, "tp"),
    )
    return jax.shard_map(
        per_device, mesh=mesh, in_specs=in_specs, out_specs=out_specs, check_vma=False
    )
```
